32 devices in a mesh: wide: 16 (over z, x, core), narrow: 2 (over y).
Axes of the slice: x: 2, y: 2, z: 4, core: 2. Of those that a mesh axis runs over, the one named last changes fastest.
Arguments:
- block_input: bfloat16 [32, 1024, 960], P('wide', 'narrow'), may hold values from -6 to 6
- cotangent: bfloat16 [32, 1024, 960], P('wide', 'narrow'), may hold values from -6 to 6
- attn_gain: float32 [960], replicated, may hold values from 0.5 to 1.5
- ffn_gain: float32 [960], replicated, may hold values from 0.5 to 1.5
- query_weight: bfloat16 [960, 960], P('narrow', 'wide'), may hold values from -0.1875 to 0.1875
- key_weight: bfloat16 [960, 320], P('narrow', 'wide'), may hold values from -0.1875 to 0.1875
- value_weight: bfloat16 [960, 320], P('narrow', 'wide'), may hold values from -0.1875 to 0.1875
- out_weight: bfloat16 [960, 960], P('narrow', 'wide'), may hold values from -1.5 to 1.5
- gate_weight: bfloat16 [960, 2560], P('narrow', 'wide'), may hold values from -0.1875 to 0.1875
- up_weight: bfloat16 [960, 2560], P('narrow', 'wide'), may hold values from -0.1875 to 0.1875
- down_weight: bfloat16 [960, 2560], P('narrow', 'wide'), may hold values from -0.125 to 0.125
Outputs:
- block_output: bfloat16 [32, 1024, 960], P('wide', 'narrow')
- input_grad: float32 [32, 1024, 960], P('wide', 'narrow')
- attn_gain_grad: float32 [960], replicated
- ffn_gain_grad: float32 [960], replicated
- query_grad: float32 [960, 960], P('narrow', 'wide')
- key_grad: float32 [960, 320], P('narrow', 'wide')
- value_grad: float32 [960, 320], P('narrow', 'wide')
- out_grad: float32 [960, 960], P('narrow', 'wide')
- gate_grad: float32 [960, 2560], P('narrow', 'wide')
- up_grad: float32 [960, 2560], P('narrow', 'wide')
- down_grad: float32 [960, 2560], P('narrow', 'wide')
The draws below stay inside these ranges and needn't reach their ends.
All inputs are finite; a program needn't handle non-finite values.
Results may differ from the reference program's by a relative error of at most 0.029.
Values may be sent and summed in bfloat16 or wider, within the bound.
A program may use at most 512 MiB of HBM per device.

```python
import jax
import jax.numpy as jnp
from jax import lax

D = 960
H = 15
KV = 5
HD = 64
FF = 2560
SEQ_LEN = 1024
SEQS = 32


def levels(own_key, extent, shards, least, top_value):
    gain = 1.0
    for dim, parts in shards:
        heights = jax.random.uniform(jax.random.fold_in(jax.random.fold_in(own_key, 6), dim), (parts,), jnp.float32, least / len(shards), top_value / len(shards))
        gain = gain * jnp.repeat(jnp.exp(heights), extent[dim] // parts).reshape((-1,) + (1,) * (len(extent) - 1 - dim))
    return gain


def normal_values(own_key, extent, spread, most, cuts=(), kind=jnp.bfloat16):
    result = spread * jax.random.normal(own_key, extent, jnp.float32)
    if cuts:
        result = result * levels(own_key, extent, cuts, -0.22, 0.18)
    return jnp.clip(result, -most, most).astype(kind)


def setup_inputs(seed: int = 0) -> dict:
    key_list = jax.random.split(jax.random.key(seed), 12)
    return {
        "block_input": normal_values(key_list[0], (SEQS, SEQ_LEN, D), 1.0, 6.0, ((0, 16), (1, 2))),
        "cotangent": normal_values(key_list[1], (SEQS, SEQ_LEN, D), 1.0, 6.0, ((0, 16), (1, 2))),
        "attn_gain": jnp.clip(1.0 + 0.1 * jax.random.normal(key_list[2], (D,), jnp.float32), 0.5, 1.5),
        "ffn_gain": jnp.clip(1.0 + 0.1 * jax.random.normal(key_list[3], (D,), jnp.float32), 0.5, 1.5),
        "query_weight": normal_values(key_list[4], (D, H * HD), D ** -0.5, 0.1875, ((0, 2), (1, 16))),
        "key_weight": normal_values(key_list[5], (D, KV * HD), D ** -0.5, 0.1875, ((0, 2), (1, 16))),
        "value_weight": normal_values(key_list[6], (D, KV * HD), D ** -0.5, 0.1875, ((0, 2), (1, 16))),
        "out_weight": normal_values(key_list[7], (H * HD, D), (D // 64) ** -0.5, 1.5, ((0, 2), (1, 16))),
        "gate_weight": normal_values(key_list[8], (D, FF), D ** -0.5, 0.1875, ((0, 2), (1, 16))),
        "up_weight": normal_values(key_list[9], (D, FF), D ** -0.5, 0.1875, ((0, 2), (1, 16))),
        "down_weight": normal_values(key_list[10], (D, FF), FF ** -0.5, 0.125, ((0, 2), (1, 16))),
    }


@jax.custom_vjp
def low(v):
    return lax.optimization_barrier(v.astype(jnp.bfloat16)).astype(jnp.float32)

@jax.custom_vjp
def low_back(v):
    return v

def low_keep(v):
    return (low(v), None)

def low_pass(kept, grad):
    return (grad,)

def back_keep(v):
    return (v, None)

def back_low(kept, grad):
    return (low(grad),)
low.defvjp(low_keep, low_pass)
low_back.defvjp(back_keep, back_low)

def matmul(left, right):
    return jnp.dot(left, right, precision=lax.Precision.HIGHEST)

def rms_scale(values):
    return lax.rsqrt(lax.optimization_barrier(jnp.mean(values * values, axis=-1, keepdims=True)) + 1e-05)

def rotary_tables(count, first_row):
    positions = (first_row + jnp.arange(count, dtype=jnp.int32)).astype(jnp.float32)
    exponent = jnp.arange(HD // 2, dtype=jnp.int32).astype(jnp.float32) * (2.0 / HD)
    frequency = 10000.0 ** (-exponent)
    angles = positions[:, None] * frequency[None, :]
    return (jnp.cos(angles), jnp.sin(angles))

def rotate(values, cosine, sine_table):
    half_size = values.shape[-1] // 2
    first_half = values[..., :half_size]
    second_half = values[..., half_size:]
    return jnp.concatenate([first_half * cosine - second_half * sine_table, second_half * cosine + first_half * sine_table], axis=-1)

def run_block(run_input, attn_gain, ffn_gain, query_weight, key_weight, value_weight, out_weight, gate_weight, up_weight, down_weight):
    length = run_input.shape[0]
    groups = H // KV
    cosine, sine_table = rotary_tables(length, 0)
    normed_attn = low(run_input * rms_scale(run_input) * attn_gain)
    query_pre = low_back(matmul(normed_attn, query_weight)).reshape(length, KV, groups, HD)
    queries = low(rotate(query_pre, cosine[:, None, None, :], sine_table[:, None, None, :]))
    key_pre = low_back(matmul(normed_attn, key_weight)).reshape(length, KV, HD)
    keys_all = low(rotate(key_pre, cosine[:, None, :], sine_table[:, None, :]))
    values_all = low(low_back(matmul(normed_attn, value_weight))).reshape(length, KV, HD)
    block_rows = min(512, length)
    starts = jnp.arange(length // block_rows, dtype=jnp.int32) * block_rows

    def attend(pieces):
        query_block, offset = pieces
        attn_score = low_back(jnp.einsum('rgjd,pgd->gjrp', query_block, keys_all, precision=lax.Precision.HIGHEST) * HD ** (-0.5))
        visible = (offset + jnp.arange(block_rows, dtype=jnp.int32))[:, None] >= jnp.arange(length, dtype=jnp.int32)[None, :]
        attn_score = jnp.where(visible, attn_score, -jnp.inf)
        row_peak = lax.optimization_barrier(jnp.max(attn_score, axis=-1, keepdims=True))
        weight_exp = jnp.exp(attn_score - row_peak)
        probs_low = low(weight_exp / lax.optimization_barrier(jnp.sum(weight_exp, axis=-1, keepdims=True)))
        return jnp.einsum('gjrp,pgd->rgjd', probs_low, values_all, precision=lax.Precision.HIGHEST)
    mixed_heads = lax.map(jax.checkpoint(attend), (queries.reshape(length // block_rows, block_rows, KV, groups, HD), starts))
    mixed_low = low(low_back(mixed_heads.reshape(length, H * HD)))
    hidden_state = run_input + low_back(matmul(mixed_low, out_weight))
    normed_ffn = low(hidden_state * rms_scale(hidden_state) * ffn_gain)
    gate_proj = low_back(matmul(normed_ffn, gate_weight))
    up_proj = low_back(matmul(normed_ffn, up_weight))
    hidden = low(gate_proj / (1.0 + jnp.exp(-gate_proj)) * up_proj)
    return hidden_state + low_back(matmul(hidden, down_weight.T))

def forward_all(stack, attn_gain, ffn_gain, query_weight, key_weight, value_weight, out_weight, gate_weight, up_weight, down_weight):
    params = (attn_gain, ffn_gain, query_weight, key_weight, value_weight, out_weight, gate_weight, up_weight, down_weight)

    def apply_twice(sequence):
        middle_state = run_block(sequence, *params)
        return run_block(middle_state, *params)
    return lax.map(jax.checkpoint(apply_twice), stack)

def reference(block_input, cotangent, attn_gain, ffn_gain, query_weight, key_weight, value_weight, out_weight, gate_weight, up_weight, down_weight):
    floats = tuple((item.astype(jnp.float32) for item in (block_input, attn_gain, ffn_gain, query_weight, key_weight, value_weight, out_weight, gate_weight, up_weight, down_weight)))
    output, pullback = jax.vjp(forward_all, *floats)
    grads = pullback(cotangent.astype(jnp.float32))
    return (output.astype(jnp.bfloat16), grads[0], grads[1], grads[2], grads[3], grads[4], grads[5], grads[6], grads[7], grads[8], grads[9])
```

```python
import functools

import jax
import jax.numpy as jnp
import numpy as np
from jax import lax
from jax.experimental import pallas as pl
from jax.experimental.pallas import tpu as pltpu
from jax.sharding import PartitionSpec as P

H = 15
KV = 5
HD = 64
MESH = pl.DeviceIdType.MESH
F32 = jnp.float32
BF16 = jnp.bfloat16
GROUP = H // KV
PIECE = 160
CHUNKS = 5
ROWS = PIECE // CHUNKS
UNITS = 16 * ROWS
HALF = 512
WIDE = 2 * HALF
KEY_AT = 1024
VALUE_AT = 1408
QKV = 1792
VMEM_LIMIT = 62 << 20


def nt(left, right):
    return lax.dot_general(left, right, (((1,), (1,)), ((), ())), preferred_element_type=F32)


def nn(left, right):
    return jnp.dot(left, right, preferred_element_type=F32)


def tn(left, right):
    return lax.dot_general(left, right, (((0,), (0,)), ((), ())), preferred_element_type=F32)


def whole(*shape):
    return pl.BlockSpec(shape, lambda *_: (0,) * len(shape), pipeline_mode=pl.Buffered(1))


def compiler(**more):
    return pltpu.CompilerParams(vmem_limit_bytes=VMEM_LIMIT, **more)


def cost(flops, moved):
    return pl.CostEstimate(flops=int(flops), bytes_accessed=int(moved), transcendentals=0)


def span(ref, rows):
    return ref.at[..., pl.ds(rows[0], rows[1] - rows[0]), :]


class Place:
    def __init__(self):
        self.w = lax.axis_index("wide")
        self.y = lax.axis_index("narrow")
        self.z = self.w // 4
        self.x = (self.w // 2) % 2
        self.c = self.w % 2
        self.sibling = (self.w + 1 - 2 * self.c, self.y)

    def partners(self, dim):
        if dim == "x":
            return [(1 - self.x, (self.w + 2 - 4 * self.x, self.y))]
        if dim == "y":
            return [(1 - self.y, (self.w, 1 - self.y))]
        others = [(self.z + far) % 4 for far in (1, 2, 3)]
        return [(other, (self.w + 4 * (other - self.z), self.y)) for other in others]

    def origins(self, dim):
        if dim == "z":
            return [(self.z + far) % 4 for far in (3, 2, 1)]
        return [1 - getattr(self, dim)]

    def everyone(self):
        return [self.sibling] + [device for dim in "xyz" for _, device in self.partners(dim)]


def greet(devices):
    barrier = pltpu.get_barrier_semaphore()
    for device in devices:
        pl.semaphore_signal(barrier, inc=1, device_id=device, device_id_type=MESH)
    pl.semaphore_wait(barrier, len(devices))


def remote(source, target, send_sem, recv_sem, device):
    return pltpu.make_async_remote_copy(
        src_ref=source,
        dst_ref=target,
        send_sem=send_sem,
        recv_sem=recv_sem,
        device_id=device,
        device_id_type=MESH,
    )


STEPS = 3


class Gather:
    def __init__(self, me, flows, own, full, keep_sem, send, recv, cross_send, cross_recv):
        self.me, self.flows, self.own, self.full = me, flows, own, full
        self.keep_sem, self.send, self.recv = keep_sem, send, recv
        self.cross_send, self.cross_recv = cross_send, cross_recv

    def keep(self, t):
        me = self.me
        return pltpu.make_async_copy(
            self.own[t], self.full[t].at[me.y, me.z, me.x, me.c], self.keep_sem.at[t]
        )

    def blocks(self, t, flow, step, place):
        me = self.me
        rows, order = self.flows[t][flow]
        at = {"y": me.y, "z": me.z, "x": me.x}
        for name in order[:step]:
            at[name] = slice(None)
        at[order[step]] = place
        return span(self.full[t].at[at["y"], at["z"], at["x"], me.c], rows)

    def copies(self, t, flow, step):
        me = self.me
        rows, order = self.flows[t][flow]
        dim = order[step]
        target = self.blocks(t, flow, step, getattr(me, dim))
        source = span(self.own[t], rows) if step == 0 else target
        return [
            remote(
                source, target, self.send.at[t, flow, step, i], self.recv.at[t, flow, step, i], device
            )
            for i, (_, device) in enumerate(me.partners(dim))
        ]

    def landing(self, t, flow, step):
        me = self.me
        dim = self.flows[t][flow][1][step]
        devices = me.partners(dim)
        blocks = [self.blocks(t, flow, step, place) for place in me.origins(dim)]
        return [
            remote(
                block, block, self.send.at[t, flow, step, i], self.recv.at[t, flow, step, i],
                devices[i][1],
            )
            for i, block in enumerate(blocks)
        ]

    def cross(self, t, flow):
        blocks = span(self.full[t].at[:, :, :, self.me.c], self.flows[t][flow][0])
        return remote(
            blocks, blocks, self.cross_send.at[t, flow], self.cross_recv.at[t, flow],
            self.me.sibling,
        )

    def stage(self, t, step):
        count = len(self.flows[t])
        if step == 0:
            self.keep(t).start()
        if step == 1:
            self.keep(t).wait()
        for flow in range(count):
            if 0 < step <= STEPS:
                for copy in self.landing(t, flow, step - 1):
                    copy.wait_recv()
            if step < STEPS:
                for copy in self.copies(t, flow, step):
                    copy.start()
            if step == STEPS:
                self.cross(t, flow).start()
            if step == STEPS + 1:
                self.cross(t, flow).wait()
                for before in range(STEPS):
                    for copy in self.copies(t, flow, before):
                        copy.wait_send()

    @staticmethod
    def semaphores(types, flows):
        dma = pltpu.SemaphoreType.DMA
        return [
            dma((types,)), dma((types, flows, STEPS, 3)), dma((types, flows, STEPS, 3)),
            dma((types, flows)), dma((types, flows)),
        ]


class Scatter:
    def __init__(self, me, flows, terms, out, scratch):
        self.me, self.flows, self.terms, self.out = me, flows, terms, out
        (
            self.acc, self.arrived, self.load_sem, self.cross_send, self.cross_recv, self.send,
            self.recv, *self.buffers,
        ) = scratch
        self.piece = self.acc.shape[-2]

    @staticmethod
    def scratch(flows, piece):
        dma = pltpu.SemaphoreType.DMA
        types, count = len(flows), len(flows[0])
        refs = [
            pltpu.VMEM((types, 2, 4, 2, piece, HALF), BF16),
            pltpu.VMEM((types, 2, 4, 2, piece, HALF), BF16),
            dma((types,)), dma((types,)), dma((types,)),
            dma((types, count, STEPS, 3)), dma((types, count, STEPS, 3)),
        ]
        for own_flows in flows:
            for rows, order in own_flows:
                for step, dim in enumerate(order):
                    left = order[step + 1 :]
                    shape = tuple({"y": 2, "z": 4, "x": 2}[name] for name in "yzx" if name in left)
                    lines = (3 if dim == "z" else 1,)
                    refs.append(pltpu.VMEM(lines + shape + (rows[1] - rows[0], HALF), BF16))
        return refs

    def buffer(self, t, flow, step):
        return self.buffers[(t * len(self.flows[0]) + flow) * STEPS + step]

    def source(self, t, core):
        ref, first = self.terms[t]
        return span(ref.at[:, :, :, core], (first, first + self.piece))

    def cross(self, t):
        return remote(
            self.source(t, 1 - self.me.c), self.arrived.at[t], self.cross_send.at[t],
            self.cross_recv.at[t], self.me.sibling,
        )

    def load(self, t):
        return pltpu.make_async_copy(
            self.source(t, self.me.c), self.acc.at[t], self.load_sem.at[t]
        )

    def blocks(self, t, flow, step, place):
        rows, order = self.flows[t][flow]
        at = {"y": slice(None), "z": slice(None), "x": slice(None)}
        for name in order[:step]:
            at[name] = getattr(self.me, name)
        at[order[step]] = place
        return span(self.acc.at[t, at["y"], at["z"], at["x"]], rows)

    def copies(self, t, flow, step):
        buffer = self.buffer(t, flow, step)
        return [
            remote(
                self.blocks(t, flow, step, place), buffer.at[i], self.send.at[t, flow, step, i],
                self.recv.at[t, flow, step, i], device,
            )
            for i, (place, device) in enumerate(self.me.partners(self.flows[t][flow][1][step]))
        ]

    def take(self, t, flow, step):
        copies = self.copies(t, flow, step)
        for copy in copies:
            copy.wait_recv()
        target = self.blocks(t, flow, step, getattr(self.me, self.flows[t][flow][1][step]))
        buffer = self.buffer(t, flow, step)

        def add(*index):
            value = target.at[index][...] if index else target[...]
            for i in range(len(copies)):
                value = value + buffer.at[(i,) + index][...]
            if index:
                target.at[index][...] = value
            else:
                target[...] = value

        if len(target.shape) == 2:
            add()
        else:

            @pl.loop(0, target.shape[0])
            def _(index):
                add(index)

    def stage(self, t, step):
        flows = range(len(self.flows[t]))
        if step == 0:
            self.cross(t).start()
            self.load(t).start()
        if step == 1:
            self.load(t).wait()
            self.cross(t).wait()

            @pl.loop(0, 8)
            def _(index):
                half, block = index // 4, index % 4
                self.acc[t, half, block] = self.acc[t, half, block] + self.arrived[t, half, block]

        for flow in flows:
            if 1 < step <= STEPS + 1:
                self.take(t, flow, step - 2)
            if 1 <= step <= STEPS:
                for copy in self.copies(t, flow, step - 1):
                    copy.start()
        if step == STEPS + 1:
            me = self.me
            for flow in flows:
                for before in range(STEPS):
                    for copy in self.copies(t, flow, before):
                        copy.wait_send()
            self.out[t] = self.acc[t, me.y, me.z, me.x].astype(F32)


def staggered(types, stages, gap=1):
    ticks = stages + gap * (types - 1)
    return [
        [(t, tick - gap * t) for t in range(types) if 0 <= tick - gap * t < stages]
        for tick in range(ticks)
    ]


def widen(turned, half, model):
    size = model // 2
    part = turned[half * size : (half + 1) * size, :].astype(F32)
    fill = jnp.zeros((HALF - size, part.shape[1]), F32)
    return jnp.concatenate([part, fill], axis=0).T


def narrow(value, half, model):
    return value[:, half * HALF : (half + 1) * HALF].T[: model // 2]


def swap_halves(tile):
    lane = lax.broadcasted_iota(jnp.int32, tile.shape, 1)
    return jnp.where(
        lane % HD < HD // 2, pltpu.roll(tile, 128 - HD // 2, 1), pltpu.roll(tile, HD // 2, 1)
    )


def qkv_kernel(model, state, gain, weight, cosine, sine, normed, scale, queries, keys, values):
    inputs = state[...]
    inv = lax.rsqrt(jnp.sum(inputs * inputs, axis=-1, keepdims=True) * (1.0 / model) + 1e-05)
    scale[...] = inv
    low = (inputs * inv * gain[...]).astype(BF16)
    normed[...] = low
    left, right = low[:, :HALF], low[:, HALF:]
    cos, sin = cosine[...], sine[...]

    def project(first, last):
        rows = pl.ds(first, last - first)
        return nt(left, weight[0, rows, :]) + nt(right, weight[1, rows, :])

    def turned(pre):
        return pre * cos + swap_halves(pre) * sin

    for first, last in ((0, 512), (512, KEY_AT)):
        pre = project(first, last)
        for at in range(0, last - first, 128):
            both = (turned(pre[:, at : at + 128]) * HD ** (-0.5)).astype(BF16)
            head = (first + at) // HD
            queries[head] = both[:, :HD]
            if head + 1 < H:
                queries[head + 1] = both[:, HD:]
    pre = project(KEY_AT, QKV)
    for at in range(0, VALUE_AT - KEY_AT, 128):
        both = turned(pre[:, at : at + 128]).astype(BF16)
        head = at // HD
        keys[head] = both[:, :HD]
        if head + 1 < KV:
            keys[head + 1] = both[:, HD:]
    for at in range(0, QKV - VALUE_AT, 128):
        start = VALUE_AT - KEY_AT + at
        both = pre[:, start : start + 128].astype(BF16)
        head = at // HD
        values[head] = both[:, :HD]
        if head + 1 < KV:
            values[head + 1] = both[:, HD:]


def qkv_call(model, state, gain, weight, cosine, sine, rows=512):
    tokens = state.shape[0]
    by_row = lambda width: pl.BlockSpec((rows, width), lambda i: (i, 0))
    heads = lambda count: pl.BlockSpec((count, rows, HD), lambda i: (0, i, 0))
    return pl.pallas_call(
        functools.partial(qkv_kernel, model),
        grid=(tokens // rows,),
        in_specs=[
            by_row(WIDE), whole(1, WIDE), whole(2, QKV, HALF), by_row(128), by_row(128),
        ],
        out_specs=[by_row(WIDE), by_row(1), heads(H), heads(KV), heads(KV)],
        out_shape=[
            jax.ShapeDtypeStruct((tokens, WIDE), BF16),
            jax.ShapeDtypeStruct((tokens, 1), F32),
            jax.ShapeDtypeStruct((H, tokens, HD), BF16),
            jax.ShapeDtypeStruct((KV, tokens, HD), BF16),
            jax.ShapeDtypeStruct((KV, tokens, HD), BF16),
        ],
        compiler_params=compiler(),
        cost_estimate=cost(2 * tokens * WIDE * QKV, 20e6),
        name="project_qkv",
    )(state, gain, weight, cosine, sine)


def key_mask(block):
    row = lax.broadcasted_iota(jnp.int32, (block, GROUP * block), 0)
    column = lax.broadcasted_iota(jnp.int32, (block, GROUP * block), 1)
    return row <= jnp.bitwise_and(column, block - 1)


def ahead_of(items, count, make):
    pending = [make(item) for item in items[:count]]
    for turn, item in enumerate(items):
        if turn + count < len(items):
            pending.append(make(items[turn + count]))
        yield item, pending.pop(0)


def attend_kernel(block, ahead, queries, keys, values, mixed, log_sum):
    tokens = keys.shape[1]

    def scores(at):
        query = queries[:, at : at + block, :].reshape(GROUP * block, HD)
        tiles = [
            nt(keys[0, first : first + block, :], query) for first in range(0, at + block, block)
        ]
        tiles[-1] = jnp.where(key_mask(block), tiles[-1], -jnp.inf)
        return tiles

    for at, tiles in ahead_of(list(range(0, tokens, block)), ahead, scores):
        peak = functools.reduce(
            jnp.maximum, [jnp.max(tile, axis=0, keepdims=True) for tile in tiles]
        )
        total = out = 0.0
        for index, score in enumerate(tiles):
            weight = jnp.exp(score - peak)
            total = total + jnp.sum(weight, axis=0, keepdims=True)
            value = values[0, index * block : (index + 1) * block, :]
            out = out + nn(value.T, weight.astype(BF16))
        out = out * (1.0 / total)
        mixed[:, at : at + block, :] = out.T.astype(BF16).reshape(GROUP, block, HD)
        logs = peak + jnp.log(total)
        for head in range(GROUP):
            log_sum[head, :, at : at + block] = logs[:, head * block : (head + 1) * block]


def attend_call(queries, keys, values, block=256):
    tokens = queries.shape[1]
    heads = lambda count: pl.BlockSpec((count, tokens, HD), lambda i: (i, 0, 0))
    return pl.pallas_call(
        functools.partial(attend_kernel, block, 3),
        grid=(KV,),
        in_specs=[heads(GROUP), heads(1), heads(1)],
        out_specs=[heads(GROUP), pl.BlockSpec((GROUP, 1, tokens), lambda i: (i, 0, 0))],
        out_shape=[
            jax.ShapeDtypeStruct((H, tokens, HD), BF16),
            jax.ShapeDtypeStruct((H, 1, tokens), F32),
        ],
        compiler_params=compiler(),
        cost_estimate=cost(4 * tokens * tokens * H * 128, 20e6),
        name="attend",
    )(queries, keys, values)


def attend_back_kernel(
    block, queries, keys, values, log_sum, grad_mixed, grad_queries, grad_keys, grad_values
):
    tokens = keys.shape[1]

    def rows(ref, at):
        return ref[:, at : at + block, :].reshape(GROUP * block, HD)

    def products(at):
        query, grad = rows(queries, at), rows(grad_mixed, at)
        return [
            (
                nt(keys[0, first : first + block, :], query),
                nt(values[0, first : first + block, :], grad),
            )
            for first in range(0, at + block, block)
        ]

    for at, tiles in ahead_of(list(range(tokens - block, -1, -block)), 1, products):
        query, grad = rows(queries, at), rows(grad_mixed, at)
        logs = jnp.concatenate([log_sum[head, :, at : at + block] for head in range(GROUP)], axis=1)
        weights = []
        delta = 0.0
        for index, (score, grad_probs) in enumerate(tiles):
            probs = jnp.exp(score - logs)
            if index * block == at:
                probs = jnp.where(key_mask(block), probs, 0.0)
            delta = delta + jnp.sum(probs * grad_probs, axis=0, keepdims=True)
            weights.append(probs)
        by_query = 0.0
        for index, (_, grad_probs) in enumerate(tiles):
            part = pl.ds(index * block, block)
            probs = weights[index]
            low = (probs * (grad_probs - delta)).astype(BF16)
            by_query = by_query + nn(keys[0, part, :].T, low)
            key_part = nn(low, query)
            value_part = nn(probs.astype(BF16), grad)
            if at + block == tokens:
                grad_keys[0, part, :] = key_part
                grad_values[0, part, :] = value_part
            else:
                grad_keys[0, part, :] += key_part
                grad_values[0, part, :] += value_part
        grad_queries[:, at : at + block, :] = by_query.T.reshape(GROUP, block, HD)


def attend_back_call(queries, keys, values, log_sum, grad_mixed, block=256):
    tokens = queries.shape[1]
    heads = lambda count: pl.BlockSpec((count, tokens, HD), lambda i: (i, 0, 0))
    return pl.pallas_call(
        functools.partial(attend_back_kernel, block),
        grid=(KV,),
        in_specs=[
            heads(GROUP), heads(1), heads(1),
            pl.BlockSpec((GROUP, 1, tokens), lambda i: (i, 0, 0)), heads(GROUP),
        ],
        out_specs=[heads(GROUP), heads(1), heads(1)],
        out_shape=[
            jax.ShapeDtypeStruct((H, tokens, HD), F32),
            jax.ShapeDtypeStruct((KV, tokens, HD), F32),
            jax.ShapeDtypeStruct((KV, tokens, HD), F32),
        ],
        compiler_params=compiler(),
        cost_estimate=cost(10 * tokens * tokens * H * 128, 30e6),
        name="attend_back",
    )(queries, keys, values, log_sum, grad_mixed)


GATHER_FLOWS = ((((0, 80), "zyx"), ((80, 128), "zxy"), ((128, 160), "yxz")),) + (
    (((0, 48), "zyx"), ((48, 80), "zxy"), ((80, 96), "yxz")),
) * CHUNKS


def order_weights(model, sizes, sorter, raw, qkv_weight, out_weight):
    counts = [4 * size for size in sizes]
    starts = [sum(counts[:i]) for i in range(4)]
    rows = 4 * PIECE
    qkv_weight[...] = jnp.zeros(qkv_weight.shape, BF16)
    out_weight[...] = jnp.zeros(out_weight.shape, BF16)
    for half in range(2):
        for z in range(4):
            block = raw[half, z * rows : (z + 1) * rows, :]
            done = nn(sorter[...], block).astype(BF16)
            part = [done[starts[i] : starts[i] + counts[i]] for i in range(4)]
            for i, first in enumerate((0, KEY_AT, VALUE_AT)):
                at = first + z * counts[i]
                qkv_weight[half, at : at + counts[i], :] = part[i]
            at = z * counts[3] + (HALF - model // 2 if z >= 2 else 0)
            out_weight[half, at : at + counts[3], :] = part[3]


def sorter_matrix(sizes):
    rows = 4 * PIECE
    matrix = np.zeros((rows, rows), np.float32)
    to = 0
    first = 0
    for size in sizes:
        for device in range(4):
            for row in range(size):
                matrix[to, device * PIECE + first + row] = 1.0
                to += 1
        first += size
    return matrix


def feed_block(gate_weight, up_weight, normed, rows, gate, up):
    left, right = normed[rows, :HALF], normed[rows, HALF:]
    gate_proj = nt(left, gate_weight[0]) + nt(right, gate_weight[1])
    up_proj = nt(left, up_weight[0]) + nt(right, up_weight[1])
    gate[rows, :] = gate_proj.astype(BF16)
    up[rows, :] = up_proj.astype(BF16)
    return (gate_proj / (1.0 + jnp.exp(-gate_proj)) * up_proj).astype(BF16)


def out_block(model, state, heads, out_weight, gain, mixed, hidden_state, normed, scale):
    mixed[...] = jnp.zeros(mixed.shape, BF16)
    for head in range(H):
        for lane, first, size in places(head):
            mixed[:, lane : lane + size] = heads[head, :, first : first + size]
    after = state[...] + (nt(mixed[:, :HALF], out_weight[0]) + nt(mixed[:, HALF:], out_weight[1]))
    hidden_state[...] = after
    inv = lax.rsqrt(jnp.sum(after * after, axis=-1, keepdims=True) * (1.0 / model) + 1e-05)
    scale[...] = inv
    normed[...] = (after * inv * gain[...]).astype(BF16)


START_KINDS = lambda tokens, units: [
    ((2, QKV, HALF), BF16),
    ((2, WIDE, HALF), BF16),
    ((tokens, WIDE), F32),
    ((tokens, WIDE), BF16),
    ((tokens, 1), F32),
    ((H, tokens, HD), BF16),
    ((KV, tokens, HD), BF16),
    ((KV, tokens, HD), BF16),
    ((H, 1, tokens), F32),
    ((tokens, WIDE), F32),
    ((tokens, WIDE), BF16),
    ((tokens, WIDE), BF16),
    ((tokens, 1), F32),
]


def feed_spec(t, first=0):
    return pl.BlockSpec(
        (None, 2, 4, 2, 2, ROWS, HALF), lambda i: (first + i, 0, 0, 0, 0, t, 0)
    )


def start_kernel(
    model, sizes, own, feed_own, seqs, gain, feed_gain, cosine, sine, sorter,
    full, feed_full, output_out, gate_out, up_out, *rest,
):
    kinds = len(START_KINDS(0, 0))
    outs_refs, rest = rest[:kinds], rest[kinds:]
    (
        qkv_weight, out_weight, state, normed, scale, queries, keys, values, log_sum, hidden_state,
        mixed, feed_normed, feed_scale,
    ), rest = rest[:kinds], rest[kinds:]
    seq, heads, seq_sem, raw_sem, out_sem, *gather_sems = rest
    me = Place()
    y = me.y
    gather = Gather(
        me, GATHER_FLOWS, [own] + [feed_own.at[i] for i in range(CHUNKS)],
        [full] + [feed_full.at[i] for i in range(CHUNKS)], *gather_sems,
    )
    greet(me.everyone())
    swap = remote(
        seqs.at[1 - y], seq.at[y], seq_sem.at[0], seq_sem.at[1], me.partners("y")[0][1]
    )
    swap.start()
    stay = pltpu.make_async_copy(seqs.at[y], seq.at[y], seq_sem.at[2])
    stay.start()
    ticks = staggered(1 + CHUNKS, STEPS + 2)

    def tick(*counts):
        for count in counts:
            for t, stage in ticks[count]:
                gather.stage(t, stage)

    tick(0, 1, 2)
    rows = seq.shape[2]
    tokens = 2 * rows
    outs = []

    def give(index, source):
        copy = pltpu.make_async_copy(source, outs_refs[index], out_sem.at[index])
        copy.start()
        outs.append(copy)

    stay.wait()
    swap.wait()
    for part in range(2):
        for half in range(2):
            state[part * rows : (part + 1) * rows, half * HALF : (half + 1) * HALF] = widen(
                seq.at[part], half, model
            )
    give(2, state)
    tick(3, 4)

    def put_in_order(raw):
        fetch = pltpu.make_async_copy(full, raw, raw_sem.at[0])
        fetch.start()
        fetch.wait()
        order_weights(
            model, sizes, sorter, raw.reshape(2, 16 * PIECE, HALF), qkv_weight, out_weight
        )

    pl.run_scoped(put_in_order, pltpu.VMEM((2, 4, 2, 2, PIECE, HALF), BF16))
    give(0, qkv_weight)
    give(1, out_weight)
    for at in range(0, tokens, rows):
        part = pl.ds(at, rows)
        qkv_kernel(
            model, state.at[part], gain, qkv_weight, cosine.at[part], sine.at[part],
            normed.at[part], scale.at[part], queries.at[:, part], keys.at[:, part],
            values.at[:, part],
        )
    give(3, normed)
    give(4, scale)
    give(5, queries)
    give(6, keys)
    give(7, values)
    tick(5)

    @pl.loop(0, KV)
    def _(group):
        some = pl.ds(group * GROUP, GROUP)
        one = pl.ds(group, 1)
        attend_kernel(
            tokens // 4, 1, queries.at[some], keys.at[one], values.at[one], heads.at[some],
            log_sum.at[some],
        )
        pl.when(group == 1)(lambda: tick(6))
        pl.when(group == 3)(lambda: tick(7))

    give(8, log_sum)
    out_block(
        model, state, heads, out_weight, feed_gain, mixed, hidden_state, feed_normed, feed_scale
    )
    give(9, hidden_state)
    give(10, mixed)
    give(11, feed_normed)
    give(12, feed_scale)

    outs[0].wait()
    state[...] = hidden_state[...]

    def feed_body(gate_weight, up_weight, down_weight, gate, up):
        gates, ups, downs = (
            ref.reshape(2, UNITS, HALF) for ref in (gate_weight, up_weight, down_weight)
        )
        for at in range(0, tokens, rows):
            part = pl.ds(at, rows)
            low = feed_block(gates, ups, feed_normed, part, gate, up)
            state[part, :HALF] += nn(low, downs[0])
            state[part, HALF:] += nn(low, downs[1])

    def feed_chunks(first, count):
        by_unit = pl.BlockSpec((tokens, UNITS), lambda i: (0, first + i))
        pltpu.emit_pipeline(
            feed_body,
            grid=(count,),
            in_specs=[feed_spec(t, first) for t in range(3)],
            out_specs=[by_unit, by_unit],
        )(feed_full, feed_full, feed_full, gate_out, up_out)

    feed_chunks(0, 3)
    tick(8)
    feed_chunks(3, 1)
    tick(9)
    feed_chunks(4, 1)
    last = pltpu.make_async_copy(state, output_out, raw_sem.at[0])
    last.start()
    for copy in outs[1:]:
        copy.wait()
    last.wait()


def start_call(model, sizes, own, feed_own, seqs, gain, feed_gain, cosine, sine, sorter):
    types = 1 + CHUNKS
    tokens = 2 * seqs.shape[2]
    units = 16 * PIECE
    kinds = START_KINDS(tokens, units)
    dma = pltpu.SemaphoreType.DMA
    anywhere = pl.BlockSpec(memory_space=pl.ANY)
    inside = pl.BlockSpec(memory_space=pltpu.VMEM)
    outs = [
        ((2, 4, 2, 2, PIECE, HALF), BF16),
        ((CHUNKS, 2, 4, 2, 2, 3 * ROWS, HALF), BF16),
        ((tokens, WIDE), F32),
        ((tokens, units), BF16),
        ((tokens, units), BF16),
    ] + kinds
    return pl.pallas_call(
        functools.partial(start_kernel, model, sizes),
        out_shape=[jax.ShapeDtypeStruct(*kind) for kind in outs],
        in_specs=[anywhere] * 3 + [inside] * 5,
        out_specs=[anywhere] * len(outs),
        scratch_shapes=[pltpu.VMEM(*kind) for kind in kinds]
        + [
            pltpu.VMEM(seqs.shape, BF16),
            pltpu.VMEM((H, tokens, HD), BF16),
            dma((3,)), dma((1,)), dma((len(kinds),)),
        ]
        + Gather.semaphores(types, len(GATHER_FLOWS[0])),
        compiler_params=compiler(collective_id=0, has_side_effects=True),
        name="start",
    )(own, feed_own, seqs, gain, feed_gain, cosine, sine, sorter)


def places(head, model=H * HD):
    first, last, middle = head * HD, (head + 1) * HD, model // 2
    if last <= middle:
        return ((first, 0, HD),)
    if first >= middle:
        return ((HALF + first - middle, 0, HD),)
    return ((first, 0, middle - first), (HALF, middle - first, last - middle))


def feed_kernel(
    model, block, state, heads, out_weight, gain, gate_weight, up_weight, down_weight,
    final, hidden_state, mixed, normed, scale, gate, up, output,
):
    tokens = state.shape[0]

    @pl.when(pl.program_id(0) == 0)
    def _():
        out_block(model, state, heads, out_weight, gain, mixed, hidden_state, normed, scale)
        output[...] = hidden_state[...]

    gate_weight, up_weight, down_weight = (
        ref.reshape(2, UNITS, HALF) for ref in (gate_weight, up_weight, down_weight)
    )
    for at in range(0, tokens, block):
        rows = pl.ds(at, block)
        hidden = feed_block(gate_weight, up_weight, normed, rows, gate, up)
        output[rows, :HALF] += nn(hidden, down_weight[0])
        output[rows, HALF:] += nn(hidden, down_weight[1])

    @pl.when(pl.program_id(0) == pl.num_programs(0) - 1)
    def _():
        size = model // 2
        for part in range(2):
            value = output[part * tokens // 2 : (part + 1) * tokens // 2, :]
            for half in range(2):
                final[part, half * size : (half + 1) * size, :] = narrow(value, half, model).astype(
                    BF16
                )


def feed_call(model, state, heads, out_weight, gain, weights, block=512):
    tokens = state.shape[0]
    units = CHUNKS * UNITS
    by_unit = pl.BlockSpec((tokens, UNITS), lambda i: (0, i))
    return pl.pallas_call(
        functools.partial(feed_kernel, model, block),
        grid=(CHUNKS,),
        in_specs=[
            whole(tokens, WIDE), whole(H, tokens, HD), whole(2, WIDE, HALF), whole(1, WIDE),
            feed_spec(0), feed_spec(1), feed_spec(2),
        ],
        out_specs=[
            whole(2, model, tokens // 2), whole(tokens, WIDE), whole(tokens, WIDE),
            whole(tokens, WIDE), whole(tokens, 1), by_unit, by_unit,
        ],
        out_shape=[
            jax.ShapeDtypeStruct((2, model, tokens // 2), BF16),
            jax.ShapeDtypeStruct((tokens, WIDE), F32),
            jax.ShapeDtypeStruct((tokens, WIDE), BF16),
            jax.ShapeDtypeStruct((tokens, WIDE), BF16),
            jax.ShapeDtypeStruct((tokens, 1), F32),
            jax.ShapeDtypeStruct((tokens, units), BF16),
            jax.ShapeDtypeStruct((tokens, units), BF16),
        ],
        scratch_shapes=[pltpu.VMEM((tokens, WIDE), F32)],
        compiler_params=compiler(),
        cost_estimate=cost(2 * tokens * WIDE * (3 * units + H * HD), 50e6),
        name="feed",
    )(state, heads, out_weight, gain, weights, weights, weights)


def feed_back_kernel(
    model, block, pair, *refs,
):
    step = pl.program_id(0)
    if pair:
        mine, other, *refs = refs
        *refs, grad_out = refs
    else:
        grad_out, *refs = refs
    (
        hidden_state, gain, scale, gate, up, gate_weight, up_weight, down_weight,
        grad_state, gain_term, grad_low, grad_gate, grad_up, hidden,
    ) = refs
    tokens = grad_out.shape[0]

    @pl.when(step == 0)
    def _():
        if pair:
            count = tokens // 2
            y = lax.axis_index("narrow")
            for place, turned in ((y, mine), (1 - y, other)):
                rows = pl.ds(pl.multiple_of(place * count, count), count)
                for half in range(2):
                    columns = pl.ds(half * HALF, HALF)
                    grad_out[rows, columns] = widen(turned, half, model)
        grad_low[...] = grad_out[...].astype(BF16)
        grad_state[...] = jnp.zeros_like(grad_state)

    gate_weight, up_weight, down_weight = (
        ref.reshape(2, UNITS, HALF) for ref in (gate_weight, up_weight, down_weight)
    )

    for at in range(0, tokens, block):
        rows = pl.ds(at, block)
        grad_hidden = nt(grad_low[rows, :HALF], down_weight[0]) + nt(
            grad_low[rows, HALF:], down_weight[1]
        )
        gate_proj = gate[rows, :].astype(F32)
        up_proj = up[rows, :].astype(F32)
        sig = 1.0 / (1.0 + jnp.exp(-gate_proj))
        passed = gate_proj * sig
        hidden[rows, :] = (passed * up_proj).astype(BF16)
        by_gate = (grad_hidden * up_proj * (sig + passed * (1.0 - sig))).astype(BF16)
        by_up = (grad_hidden * passed).astype(BF16)
        grad_gate[rows, :] = by_gate
        grad_up[rows, :] = by_up
        grad_state[rows, :HALF] += nn(by_gate, gate_weight[0]) + nn(by_up, up_weight[0])
        grad_state[rows, HALF:] += nn(by_gate, gate_weight[1]) + nn(by_up, up_weight[1])

    @pl.when(step == pl.num_programs(0) - 1)
    def _():
        total = jnp.zeros(gain.shape, F32)
        for at in range(0, tokens, block):
            rows = pl.ds(at, block)
            grad, after, inv = grad_state[rows, :], hidden_state[rows, :], scale[rows, :]
            total = total + jnp.sum(grad * after * inv, axis=0, keepdims=True)
            upstream = grad * gain[...]
            inner = jnp.sum(upstream * after, axis=-1, keepdims=True) * (1.0 / model)
            grad_state[rows, :] = (
                grad_out[rows, :] + inv * upstream - after * (inv * inv * inv) * inner
            )
        gain_term[...] = total


def feed_back_call(
    model, grads, hidden_state, gain, scale, gate, up, weights, block=512
):
    tokens = hidden_state.shape[0]
    pair = len(grads) == 2
    units = CHUNKS * UNITS
    by_unit = pl.BlockSpec((tokens, UNITS), lambda i: (0, i))
    return pl.pallas_call(
        functools.partial(feed_back_kernel, model, block, pair),
        grid=(CHUNKS,),
        in_specs=[
            whole(*grad.shape) for grad in grads
        ]
        + [
            whole(tokens, WIDE), whole(1, WIDE), whole(tokens, 1),
            by_unit, by_unit, feed_spec(0), feed_spec(1), feed_spec(2),
        ],
        out_specs=[whole(tokens, WIDE), whole(1, WIDE), whole(tokens, WIDE)] + [by_unit] * 3,
        out_shape=[
            jax.ShapeDtypeStruct((tokens, WIDE), F32),
            jax.ShapeDtypeStruct((1, WIDE), F32),
            jax.ShapeDtypeStruct((tokens, WIDE), BF16),
        ]
        + [jax.ShapeDtypeStruct((tokens, units), BF16)] * 3,
        scratch_shapes=[pltpu.VMEM((tokens, WIDE), F32)] if pair else [],
        compiler_params=compiler(),
        cost_estimate=cost(6 * tokens * WIDE * units, 60e6),
        name="feed_back",
    )(*grads, hidden_state, gain, scale, gate, up, weights, weights, weights)


def out_back_rows(low, out_weight, grad_mixed):
    grads = [nn(low, out_weight[half]).astype(BF16) for half in range(2)]
    for head in range(H):
        for lane, first, size in places(head):
            part = grads[lane // HALF][:, lane % HALF : lane % HALF + size]
            grad_mixed[head, :, first : first + size] = part


def out_back_kernel(grad_state, out_weight, grad_mixed):
    out_back_rows(grad_state[...].astype(BF16), out_weight, grad_mixed)


def out_back_call(grad_state, out_weight, rows=512):
    tokens = grad_state.shape[0]
    return pl.pallas_call(
        out_back_kernel,
        grid=(tokens // rows,),
        in_specs=[pl.BlockSpec((rows, WIDE), lambda i: (i, 0)), whole(2, WIDE, HALF)],
        out_specs=pl.BlockSpec((H, rows, HD), lambda i: (0, i, 0)),
        out_shape=jax.ShapeDtypeStruct((H, tokens, HD), BF16),
        compiler_params=compiler(),
        cost_estimate=cost(2 * tokens * WIDE * H * HD, 10e6),
        name="out_back",
    )(grad_state, out_weight)


def qkv_back_rows(
    model, grad_queries, grad_keys, grad_values, state, scale, grad_state, gain, weight, cosine, sine,
    back,
):
    cos, sin = cosine[...], sine[...]
    blank = jnp.zeros((back.shape[0], HD), F32)

    def fill(first, heads, factor, turn):
        count = heads.shape[0]
        for head in range(0, count, 2):
            other = heads[head + 1] if head + 1 < count else blank
            both = jnp.concatenate([heads[head], other], axis=1)
            if turn:
                both = both * cos - swap_halves(both) * sin
            if factor != 1.0:
                both = both * factor
            back[:, first + head * HD : first + head * HD + 128] = both.astype(BF16)

    fill(0, grad_queries, HD ** (-0.5), True)
    fill(KEY_AT, grad_keys, 1.0, True)
    fill(VALUE_AT, grad_values, 1.0, False)
    low = back[...]
    grad = jnp.concatenate([nn(low, weight[0]), nn(low, weight[1])], axis=1)
    inputs, inv = state[...], scale[...]
    gain_part = jnp.sum(grad * inputs * inv, axis=0, keepdims=True)
    upstream = grad * gain[...]
    inner = jnp.sum(upstream * inputs, axis=-1, keepdims=True) * (1.0 / model)
    return gain_part, grad_state[...] + inv * upstream - inputs * (inv * inv * inv) * inner


def qkv_back_kernel(
    model, grad_queries, grad_keys, grad_values, state, scale, grad_state, gain, weight, cosine, sine,
    grad_input, gain_term, back,
):
    gain_part, grad = qkv_back_rows(
        model, grad_queries, grad_keys, grad_values, state, scale, grad_state, gain, weight, cosine,
        sine, back,
    )
    grad_input[...] = grad

    @pl.when(pl.program_id(0) == 0)
    def _():
        gain_term[...] = jnp.zeros(gain_term.shape, F32)

    gain_term[...] += gain_part


def qkv_back_call(
    model, grad_queries, grad_keys, grad_values, state, scale, grad_state, gain, weight, cosine,
    sine, rows=256,
):
    tokens = state.shape[0]
    by_row = lambda width: pl.BlockSpec((rows, width), lambda i: (i, 0))
    heads = lambda count: pl.BlockSpec((count, rows, HD), lambda i: (0, i, 0))
    return pl.pallas_call(
        functools.partial(qkv_back_kernel, model),
        grid=(tokens // rows,),
        in_specs=[
            heads(H), heads(KV), heads(KV), by_row(WIDE), by_row(1), by_row(WIDE), whole(1, WIDE),
            whole(2, QKV, HALF), by_row(128), by_row(128),
        ],
        out_specs=[by_row(WIDE), whole(1, WIDE), by_row(QKV)],
        out_shape=[
            jax.ShapeDtypeStruct((tokens, WIDE), F32),
            jax.ShapeDtypeStruct((1, WIDE), F32),
            jax.ShapeDtypeStruct((tokens, QKV), BF16),
        ],
        compiler_params=compiler(),
        cost_estimate=cost(2 * tokens * WIDE * QKV, 30e6),
        name="qkv_back",
    )(
        grad_queries, grad_keys, grad_values, state, scale, grad_state, gain, weight, cosine, sine
    )


def spread_rows(model, sizes, sorter, rows, z):
    counts = [4 * size for size in sizes]
    gap = HALF - model // 2
    firsts = [
        z * counts[0], KEY_AT + z * counts[1], VALUE_AT + z * counts[2],
        QKV + z * counts[3] + (gap if z >= 2 else 0),
    ]
    part = jnp.concatenate([rows[firsts[i] : firsts[i] + counts[i], :] for i in range(4)], axis=0)
    return tn(sorter[...], part)


def attn_terms_kernel(model, sizes, back, normed, grad_state, mixed, sorter, term, rows):
    low = grad_state[...].astype(BF16)
    for half in range(2):
        lanes = pl.ds(half * HALF, HALF)
        rows[:QKV, :] = tn(back[...], normed[:, lanes]).astype(BF16)
        rows[QKV:, :] = tn(low, mixed[:, lanes]).astype(BF16)
        for z in range(4):
            value = spread_rows(model, sizes, sorter, rows, z)
            term[half, z] = value.astype(BF16).reshape(2, 2, PIECE, HALF)


def attn_terms_call(model, sizes, back, normed, grad_state, mixed, sorter):
    tokens = normed.shape[0]
    return pl.pallas_call(
        functools.partial(attn_terms_kernel, model, sizes),
        out_shape=jax.ShapeDtypeStruct((2, 4, 2, 2, PIECE, HALF), BF16),
        scratch_shapes=[pltpu.VMEM((QKV + WIDE, HALF), BF16)],
        compiler_params=compiler(),
        cost_estimate=cost(2 * tokens * WIDE * (QKV + WIDE), 30e6),
        name="attn_terms",
    )(back, normed, grad_state, mixed, sorter)


MAIN_FLOWS = tuple(
    (((0, 48), first), ((48, 80), second), ((80, 96), third))
    for first, second, third in (("yxz", "xyz", "zxy"), ("xyz", "yxz", "zyx")) * 3
)[:CHUNKS]
LAST_ROWS = 80
LAST_FLOWS = ((((0, 32), "xyz"), ((32, 64), "yxz"), ((64, 80), "zxy")),) * 2

FEED_TICKS = {0: 0, 1: 1, 2: 2, 3: 3, 4: 4}
OUT_TICKS = {1: 5}
ATTEND_TICKS = {1: 6, 2: 7, 4: 8}


def finish_kernel(
    model, sizes, low_one, low_two, normed_one, normed_two, down_one, down_two, gate_one, gate_two,
    up_one, up_two, grad_state, out_weight, queries, keys, values, log_sum, state, scale, gain, qkv_weight,
    cosine, sine, sorter, normed, mixed, before,
    sums, mine, got, gain_term, term_out, back, low_out, grad_queries, grad_keys, grad_values,
    grad_mixed, packed, term_rows, made, swap_sem, *scratch,
):
    me = Place()
    swap = remote(packed, got, swap_sem.at[0], swap_sem.at[1], me.partners("y")[0][1])
    scatter = Scatter(
        me, MAIN_FLOWS, [(made.at[i % 2], 0) for i in range(CHUNKS)], sums, scratch
    )
    ticks = staggered(CHUNKS, STEPS + 2)
    tokens = grad_state.shape[0]
    rows = tokens // 4
    greet(me.everyone())

    def run_ticks(points):
        step = pl.program_id(0)
        for at, count in points.items():

            def act(count=count):
                for t, stage in ticks[count]:
                    scatter.stage(t, stage)

            pl.when(step == at)(act)

    def feed_terms(lows, normeds, load_sem):
        loads = [
            pltpu.make_async_copy(source, target, load_sem.at[i])
            for i, (source, target) in enumerate(
                (
                    (low_one, lows.at[0]), (low_two, lows.at[1]),
                    (normed_one, normeds.at[0]), (normed_two, normeds.at[1]),
                )
            )
        ]
        for load in loads:
            load.start()
        for load in loads:
            load.wait()

        def term_body(by_gate, by_gate_two, by_up, by_up_two, by_hidden, by_hidden_two):
            slot = made.at[lax.rem(pl.program_id(0), 2)]
            for t, (one, two, right) in enumerate(
                (
                    (by_gate, by_gate_two, normeds),
                    (by_up, by_up_two, normeds),
                    (by_hidden, by_hidden_two, lows),
                )
            ):
                for half in range(2):
                    lanes = pl.ds(half * HALF, HALF)
                    value = tn(one[...], right[0, :, lanes]) + tn(two[...], right[1, :, lanes])
                    slot.at[half, :, :, :, pl.ds(t * ROWS, ROWS), :][...] = value.astype(
                        BF16
                    ).reshape(4, 2, 2, ROWS, HALF)
            run_ticks(FEED_TICKS)

        by_unit = pl.BlockSpec((tokens, UNITS), lambda i: (0, i))
        pltpu.emit_pipeline(term_body, grid=(CHUNKS,), in_specs=[by_unit] * 6, out_specs=[])(
            gate_one, gate_two, up_one, up_two, down_one, down_two
        )

    pl.run_scoped(
        feed_terms,
        pltpu.VMEM((2, tokens, WIDE), BF16),
        pltpu.VMEM((2, tokens, WIDE), BF16),
        pltpu.SemaphoreType.DMA((4,)),
    )

    def out_body(grad, target, low):
        low[...] = grad[...].astype(BF16)
        out_back_rows(low[...], out_weight, target)
        run_ticks(OUT_TICKS)

    pltpu.emit_pipeline(
        out_body,
        grid=(2,),
        in_specs=[pl.BlockSpec((2 * rows, WIDE), lambda i: (i, 0))],
        out_specs=[
            pl.BlockSpec((H, 2 * rows, HD), lambda i: (0, i, 0)),
            pl.BlockSpec((2 * rows, WIDE), lambda i: (i, 0)),
        ],
    )(grad_state, grad_mixed, low_out)

    def attend_body(query, key, value, logs, grad, by_query, by_key, by_value):
        attend_back_kernel(rows, query, key, value, logs, grad, by_query, by_key, by_value)
        run_ticks(ATTEND_TICKS)

    heads = lambda count: pl.BlockSpec((count, tokens, HD), lambda i: (i, 0, 0))
    pltpu.emit_pipeline(
        attend_body,
        grid=(KV,),
        in_specs=[
            heads(GROUP), heads(1), heads(1),
            pl.BlockSpec((GROUP, 1, tokens), lambda i: (i, 0, 0)), heads(GROUP),
        ],
        out_specs=[heads(GROUP), heads(1), heads(1)],
    )(queries, keys, values, log_sum, grad_mixed, grad_queries, grad_keys, grad_values)

    gain_term[...] = jnp.zeros(gain_term.shape, F32)

    size = model // 2

    def qkv_body(by_query, by_key, by_value, inputs, inv, grad, cos, sin, by_input, low):
        gain_part, value = qkv_back_rows(
            model, by_query, by_key, by_value, inputs, inv, grad, gain, qkv_weight, cos, sin, low
        )
        gain_term[...] += gain_part
        step = pl.program_id(0)
        for count in range(2):

            @pl.when(step == count)
            def _(count=count):
                for half in range(2):
                    packed[
                        half * size : (half + 1) * size, count * rows : (count + 1) * rows
                    ] = narrow(value, half, model).astype(BF16)

        @pl.when(step == 1)
        def _():
            swap.start()

        @pl.when(step >= 2)
        def _():
            for half in range(2):
                by_input[half * size : (half + 1) * size, :] = narrow(value, half, model)

    order = lambda i: lax.rem(i + 2 * (1 - me.y), 4)
    by_row = lambda width: pl.BlockSpec((rows, width), lambda i: (order(i), 0))
    some = lambda count: pl.BlockSpec((count, rows, HD), lambda i: (0, order(i), 0))
    pltpu.emit_pipeline(
        qkv_body,
        grid=(4,),
        in_specs=[
            some(H), some(KV), some(KV), by_row(WIDE), by_row(1), by_row(WIDE), by_row(128),
            by_row(128),
        ],
        out_specs=[
            pl.BlockSpec((model, rows), lambda i: (0, jnp.maximum(i - 2, 0))), by_row(QKV),
        ],
    )(grad_queries, grad_keys, grad_values, state, scale, grad_state, cosine, sine, mine, back)

    def term_body(low, by_normed, grad, by_mixed, earlier, term):
        z = pl.program_id(1)

        @pl.when(z == 0)
        def _():
            term_rows[:QKV, :] = tn(low[...], by_normed[...]).astype(BF16)
            term_rows[QKV:, :] = tn(grad[...], by_mixed[...]).astype(BF16)

        for at in range(4):

            @pl.when(z == at)
            def _(at=at):
                value = spread_rows(model, sizes, sorter, term_rows, at)
                value = value + earlier[0, 0].reshape(4 * PIECE, HALF).astype(F32)
                term[0, 0] = value.astype(BF16).reshape(2, 2, PIECE, HALF)

    fixed = lambda width: pl.BlockSpec((tokens, width), lambda i, z: (0, 0))
    by_half = pl.BlockSpec((tokens, HALF), lambda i, z: (0, i))
    piece = pl.BlockSpec((1, 1, 2, 2, PIECE, HALF), lambda i, z: (i, z, 0, 0, 0, 0))
    pltpu.emit_pipeline(
        term_body,
        grid=(2, 4),
        in_specs=[fixed(QKV), by_half, fixed(WIDE), by_half, piece],
        out_specs=[piece],
    )(back, normed, low_out, mixed, before, term_out)
    swap.wait()


def finish_call(
    model, sizes, operands, grad_state, out_weight, queries, keys, values, log_sum, state, scale, gain,
    qkv_weight, cosine, sine, sorter, normed, mixed, before,
):
    tokens = grad_state.shape[0]
    anywhere = pl.BlockSpec(memory_space=pl.ANY)
    inside = pl.BlockSpec(memory_space=pltpu.VMEM)
    outs = [
        ((CHUNKS, 3 * ROWS, HALF), F32, inside),
        ((model, tokens // 2), F32, anywhere),
        ((model, tokens // 2), BF16, anywhere),
        ((1, WIDE), F32, inside),
        ((2, 4, 2, 2, PIECE, HALF), BF16, anywhere),
        ((tokens, QKV), BF16, anywhere),
        ((tokens, WIDE), BF16, anywhere),
        ((H, tokens, HD), F32, anywhere),
        ((KV, tokens, HD), F32, anywhere),
        ((KV, tokens, HD), F32, anywhere),
        ((H, tokens, HD), BF16, anywhere),
    ]
    return pl.pallas_call(
        functools.partial(finish_kernel, model, sizes),
        out_shape=[jax.ShapeDtypeStruct(shape, kind) for shape, kind, _ in outs],
        in_specs=[anywhere] * 11 + [inside] + [anywhere] * 6 + [inside] * 2 + [anywhere] * 2
        + [inside] + [anywhere] * 3,
        out_specs=[where for *_, where in outs],
        scratch_shapes=[
            pltpu.VMEM((model, tokens // 2), BF16),
            pltpu.VMEM((QKV + WIDE, HALF), BF16),
            pltpu.VMEM((2, 2, 4, 2, 2, 3 * ROWS, HALF), BF16),
            pltpu.SemaphoreType.DMA((2,)),
        ]
        + Scatter.scratch(MAIN_FLOWS, 3 * ROWS),
        compiler_params=compiler(collective_id=1, has_side_effects=True),
        name="finish",
    )(
        *operands, grad_state, out_weight, queries, keys, values, log_sum, state, scale, gain,
        qkv_weight, cosine, sine, sorter, normed, mixed, before,
    )[:5]


def last_kernel(term, gains, sums, gains_out, gain_own, gain_get, gain_send, gain_recv, *scratch):
    me = Place()
    y, z = me.y, me.z
    z_one = (me.w + 4 - 8 * (z % 2), y)
    z_two = (me.w + 8 - 16 * (z // 2), y)
    types = len(LAST_FLOWS)
    scatter = Scatter(me, LAST_FLOWS, [(term, t * LAST_ROWS) for t in range(types)], sums, scratch)
    ticks = staggered(types, STEPS + 2)
    gain_own[0] = gains[...]
    greet(me.everyone())

    def tick(count):
        for t, stage in ticks[count]:
            scatter.stage(t, stage)

    tick(0)
    partners = (me.sibling, me.partners("y")[0][1], me.partners("x")[0][1], z_one, z_two)

    def gain_copy(step):
        return remote(
            gain_own.at[step], gain_get.at[step], gain_send.at[step], gain_recv.at[step],
            partners[step],
        )

    gain_copy(0).start()
    for step in range(5):
        tick(1 + step)
        gain_copy(step).wait()
        if step < 4:
            gain_own[step + 1] = gain_own[step] + gain_get[step]
            gain_copy(step + 1).start()
        else:
            gains_out[...] = gain_own[step] + gain_get[step]
    for count in range(6, len(ticks)):
        tick(count)


def last_call(term, gains):
    dma = pltpu.SemaphoreType.DMA
    inside = pl.BlockSpec(memory_space=pltpu.VMEM)
    return pl.pallas_call(
        last_kernel,
        out_shape=[
            jax.ShapeDtypeStruct((len(LAST_FLOWS), LAST_ROWS, HALF), F32),
            jax.ShapeDtypeStruct(gains.shape, F32),
        ],
        in_specs=[pl.BlockSpec(memory_space=pl.ANY), inside],
        out_specs=[inside, inside],
        scratch_shapes=[
            pltpu.VMEM((5,) + gains.shape, F32),
            pltpu.VMEM((5,) + gains.shape, F32),
            dma((5,)),
            dma((5,)),
        ]
        + Scatter.scratch(LAST_FLOWS, LAST_ROWS),
        compiler_params=compiler(collective_id=2, has_side_effects=True),
        name="last",
    )(term, gains)


def halves(array, model):
    pad = [(0, 0)] * (array.ndim - 1)
    left, right = array[..., : model // 2], array[..., model // 2 :]
    pad = pad + [(0, HALF - model // 2)]
    return jnp.concatenate([jnp.pad(left, pad), jnp.pad(right, pad)], axis=-1)


def joined(array, model):
    return jnp.concatenate([array[..., : model // 2], array[..., HALF : HALF + model // 2]], axis=-1)


def rotary(count):
    positions = np.arange(count, dtype=np.float32)
    exponent = np.arange(HD // 2, dtype=np.float32) * np.float32(2.0 / HD)
    frequency = np.power(np.float32(10000.0), -exponent).astype(np.float32)
    angles = positions[:, None] * frequency[None, :]
    cosine, sine = np.cos(angles), np.sin(angles)
    return (
        jnp.asarray(np.tile(cosine, (1, 4)), F32),
        jnp.asarray(np.concatenate([-sine, sine, -sine, sine], axis=1), F32),
    )


def on_device_whole(
    block_input, cotangent, attn_gain, ffn_gain,
    query_weight, key_weight, value_weight, out_weight, gate_weight, up_weight, down_weight,
):
    _, half_rows, model = block_input.shape
    tokens = 2 * half_rows
    y = lax.axis_index("narrow")
    flip = [(0, 1), (1, 0)]
    pieces = (query_weight, key_weight, value_weight, out_weight)
    sizes = tuple(piece.shape[1] for piece in pieces)
    starts = [sum(sizes[:i]) for i in range(5)]
    fill = lambda array: jnp.pad(
        array, [(0, 0)] * (array.ndim - 1) + [(0, HALF - array.shape[-1])]
    )
    own = fill(jnp.concatenate([piece.T for piece in pieces], axis=0))
    feed_own = fill(
        jnp.stack(
            [piece.T.reshape(CHUNKS, ROWS, -1) for piece in (gate_weight, up_weight, down_weight)],
            axis=1,
        ).reshape(CHUNKS, 3 * ROWS, -1)
    )
    gain_a = halves(attn_gain[None, :], model)
    gain_f = halves(ffn_gain[None, :], model)
    cosine, sine = rotary(tokens)
    sorter = jnp.asarray(sorter_matrix(sizes), BF16)
    (
        _, weights, output, gate, up, qkv_weight, full_out, state, normed_a, scale_a, queries, keys,
        values, log_sum, hidden_state, mixed, normed_f, scale_f,
    ) = start_call(
        model, sizes, own, feed_own, block_input.swapaxes(1, 2), gain_a, gain_f, cosine, sine, sorter
    )
    first_kept = (
        state, normed_a, scale_a, queries, keys, values, log_sum, hidden_state, mixed,
        normed_f, scale_f, gate, up,
    )

    def pick(array, index):
        return lax.dynamic_index_in_dim(array, index, 0, keepdims=False)

    state, cotangent = lax.optimization_barrier((output, cotangent))
    cotangent = cotangent.swapaxes(1, 2)
    grad_other = lax.ppermute(pick(cotangent, 1 - y), "narrow", flip)
    normed_a, scale_a, queries, keys, values = qkv_call(
        model, state, gain_a, qkv_weight, cosine, sine
    )
    heads, log_sum = attend_call(queries, keys, values)
    final, hidden_state, mixed, normed_f, scale_f, gate, up = feed_call(
        model, state, heads, full_out, gain_f, weights
    )
    final_got = lax.ppermute(pick(final, 1 - y), "narrow", flip)

    grad_state, gain_f_two, *feed_two = feed_back_call(
        model, (pick(cotangent, y), grad_other), hidden_state, gain_f, scale_f, gate, up, weights
    )
    feed_two = (feed_two[0], normed_f, feed_two[3], feed_two[1], feed_two[2])
    grad_mixed = out_back_call(grad_state, full_out)
    grad_queries, grad_keys, grad_values = attend_back_call(
        queries, keys, values, log_sum, grad_mixed
    )
    grad, gain_a_two, back = qkv_back_call(
        model, grad_queries, grad_keys, grad_values, state, scale_a, grad_state, gain_a, qkv_weight,
        cosine, sine,
    )
    attn_term = attn_terms_call(model, sizes, back, normed_a, grad_state, mixed, sorter)

    (
        state, normed_a, scale_a, queries, keys, values, log_sum, hidden_state, mixed,
        normed_f, scale_f, gate, up,
    ) = first_kept
    grad_state, gain_f_one, *feed_one = feed_back_call(
        model, (grad,), hidden_state, gain_f, scale_f, gate, up, weights
    )
    feed_one = (feed_one[0], normed_f, feed_one[3], feed_one[1], feed_one[2])
    operands = [array for pair in zip(feed_one, feed_two) for array in pair]
    feed_sums, grad_mine, grad_got, gain_a_one, attn_term = finish_call(
        model, sizes, operands, grad_state, full_out, queries, keys, values, log_sum, state, scale_a,
        gain_a, qkv_weight, cosine, sine, sorter, normed_a, mixed, attn_term,
    )
    gains = jnp.concatenate([gain_a_one + gain_a_two, gain_f_one + gain_f_two], axis=0)
    attn_sums, gains = last_call(attn_term, gains)

    def placed(mine, theirs):
        theirs = theirs.astype(mine.dtype)
        return jnp.where(y == 0, jnp.stack([mine, theirs]), jnp.stack([theirs, mine])).swapaxes(1, 2)

    block_output = placed(pick(final, y), final_got)
    input_grad = placed(grad_mine, grad_got)
    gains = joined(gains, model)
    feed_sums = feed_sums[:, :, : model // 2].reshape(CHUNKS, 3, ROWS, -1)
    feed_sums = [feed_sums[:, t].reshape(PIECE, -1).T for t in range(3)]
    attn_sums = attn_sums.reshape(PIECE, HALF)
    attn_sums = [attn_sums[starts[i] : starts[i + 1], : model // 2].T for i in range(4)]
    return (
        block_output, input_grad, gains[0], gains[1], *attn_sums,
        *feed_sums,
    )


def rms_scale(values):
    return lax.rsqrt(jnp.mean(values * values, axis=-1, keepdims=True) + 1e-05)


def rotary_tables(count, first_row):
    positions = (first_row + jnp.arange(count, dtype=jnp.int32)).astype(jnp.float32)
    exponent = jnp.arange(HD // 2, dtype=jnp.int32).astype(jnp.float32) * (2.0 / HD)
    frequency = 10000.0 ** (-exponent)
    angles = positions[:, None] * frequency[None, :]
    return (jnp.cos(angles), jnp.sin(angles))


def rotate(values, cosine, sine_table):
    half_size = values.shape[-1] // 2
    first_half = values[..., :half_size]
    second_half = values[..., half_size:]
    return jnp.concatenate(
        [
            first_half * cosine - second_half * sine_table,
            second_half * cosine + first_half * sine_table,
        ],
        axis=-1,
    )


def rotate_back(values, cosine, sine_table):
    half_size = values.shape[-1] // 2
    first_half = values[..., :half_size]
    second_half = values[..., half_size:]
    return jnp.concatenate(
        [
            first_half * cosine + second_half * sine_table,
            second_half * cosine - first_half * sine_table,
        ],
        axis=-1,
    )


def contract_last(left, right):
    return lax.dot_general(
        left, right, (((1,), (1,)), ((), ())), preferred_element_type=jnp.float32
    )


def norm_back(upstream, values, inv_rms, norm_gain):
    gain_grad = jnp.sum(upstream * values * inv_rms, axis=0)
    scaled_up = upstream * norm_gain
    inner_mean = jnp.mean(scaled_up * values, axis=-1, keepdims=True)
    return (gain_grad, inv_rms * scaled_up - values * (inv_rms * inv_rms * inv_rms) * inner_mean)


def fetch_weights(
    query_weight, key_weight, value_weight, out_weight, gate_weight, up_weight, down_weight
):
    columns = (
        lax.all_gather(query_weight, "wide", axis=1, tiled=True),
        lax.all_gather(key_weight, "wide", axis=1, tiled=True),
        lax.all_gather(value_weight, "wide", axis=1, tiled=True),
        lax.all_gather(out_weight, "wide", axis=1, tiled=True),
        lax.all_gather(gate_weight, "wide", axis=1, tiled=True),
        lax.all_gather(up_weight, "wide", axis=1, tiled=True),
        lax.all_gather(down_weight, "wide", axis=1, tiled=True),
    )
    return (
        lax.all_gather(columns[0], "narrow", axis=0, tiled=True),
        lax.all_gather(columns[1], "narrow", axis=0, tiled=True),
        lax.all_gather(columns[2], "narrow", axis=0, tiled=True),
        lax.all_gather(columns[3], "narrow", axis=0, tiled=True),
        lax.all_gather(columns[4], "narrow", axis=0, tiled=True),
        lax.all_gather(columns[5], "narrow", axis=0, tiled=True),
        lax.all_gather(columns[6], "narrow", axis=0, tiled=True),
    )


def forward_run(run_input, attn_gain, ffn_gain, weights, cosine, sine_table, first_row):
    query_weight, key_weight, value_weight, out_weight, gate_weight, up_weight, down_weight = (
        weights
    )
    row_count = run_input.shape[0]
    groups = H // KV
    attn_scale = rms_scale(run_input)
    normed_attn = (run_input * attn_scale * attn_gain).astype(jnp.bfloat16)
    query_pre = jnp.dot(normed_attn, query_weight, preferred_element_type=jnp.float32).reshape(
        row_count, KV, groups, HD
    )
    queries = rotate(query_pre, cosine[:, None, None, :], sine_table[:, None, None, :]).astype(
        jnp.bfloat16
    )
    key_pre = jnp.dot(normed_attn, key_weight, preferred_element_type=jnp.float32).reshape(
        row_count, KV, HD
    )
    keys_local = (
        rotate(key_pre, cosine[:, None, :], sine_table[:, None, :])
        .astype(jnp.bfloat16)
        .reshape(row_count, KV * HD)
    )
    values_local = jnp.dot(normed_attn, value_weight, preferred_element_type=jnp.float32).astype(
        jnp.bfloat16
    )
    keys_all, values_all = (
        lax.all_gather(keys_local, "narrow", axis=0, tiled=True),
        lax.all_gather(values_local, "narrow", axis=0, tiled=True),
    )
    length = keys_all.shape[0]
    keys_all = keys_all.reshape(length, KV, HD)
    values_all = values_all.reshape(length, KV, HD)
    attn_score = jnp.einsum(
        "rgjd,pgd->gjrp", queries, keys_all, preferred_element_type=jnp.float32
    ) * HD ** (-0.5)
    visible = (first_row + jnp.arange(row_count, dtype=jnp.int32))[:, None] >= jnp.arange(
        length, dtype=jnp.int32
    )[None, :]
    attn_score = jnp.where(visible, attn_score, -jnp.inf)
    row_peak = jnp.max(attn_score, axis=-1, keepdims=True)
    weight_exp = jnp.exp(attn_score - row_peak)
    attn_probs = weight_exp / jnp.sum(weight_exp, axis=-1, keepdims=True)
    probs_low = attn_probs.astype(jnp.bfloat16)
    mixed_heads = jnp.einsum(
        "gjrp,pgd->rgjd", probs_low, values_all, preferred_element_type=jnp.float32
    ).reshape(row_count, H * HD)
    mixed_low = mixed_heads.astype(jnp.bfloat16)
    hidden_state = run_input + jnp.dot(mixed_low, out_weight, preferred_element_type=jnp.float32)
    ffn_scale = rms_scale(hidden_state)
    normed_ffn = (hidden_state * ffn_scale * ffn_gain).astype(jnp.bfloat16)
    gate_proj = jnp.dot(normed_ffn, gate_weight, preferred_element_type=jnp.float32)
    up_proj = jnp.dot(normed_ffn, up_weight, preferred_element_type=jnp.float32)
    hidden = (gate_proj / (1.0 + jnp.exp(-gate_proj)) * up_proj).astype(jnp.bfloat16)
    run_output = hidden_state + contract_last(hidden, down_weight)
    saved_parts = (
        attn_scale,
        normed_attn,
        queries,
        keys_all,
        values_all,
        attn_probs,
        probs_low,
        mixed_low,
        hidden_state,
        ffn_scale,
        normed_ffn,
        gate_proj,
        up_proj,
        hidden,
    )
    return (run_output, saved_parts)


def backward_run(
    grad_out, run_input, saved_parts, attn_gain, ffn_gain, weights, cosine, sine_table
):
    query_weight, key_weight, value_weight, out_weight, gate_weight, up_weight, down_weight = (
        weights
    )
    (
        attn_scale,
        normed_attn,
        queries,
        keys_all,
        values_all,
        attn_probs,
        probs_low,
        mixed_low,
        hidden_state,
        ffn_scale,
        normed_ffn,
        gate_proj,
        up_proj,
        hidden,
    ) = saved_parts
    row_count = run_input.shape[0]
    length = keys_all.shape[0]
    groups = H // KV
    grad_low = grad_out.astype(jnp.bfloat16)
    down_term = jnp.einsum("td,tf->df", grad_low, hidden, preferred_element_type=jnp.float32)
    grad_hidden = jnp.dot(grad_low, down_weight, preferred_element_type=jnp.float32)
    sigmoid_gate = 1.0 / (1.0 + jnp.exp(-gate_proj))
    grad_gate = (
        grad_hidden * up_proj * sigmoid_gate * (1.0 + gate_proj * (1.0 - sigmoid_gate))
    ).astype(jnp.bfloat16)
    grad_up = (grad_hidden * gate_proj * sigmoid_gate).astype(jnp.bfloat16)
    gate_term = jnp.einsum("td,tf->df", normed_ffn, grad_gate, preferred_element_type=jnp.float32)
    up_term = jnp.einsum("td,tf->df", normed_ffn, grad_up, preferred_element_type=jnp.float32)
    grad_normed_ffn = contract_last(grad_gate, gate_weight) + contract_last(grad_up, up_weight)
    ffn_gain_term, grad_through = norm_back(grad_normed_ffn, hidden_state, ffn_scale, ffn_gain)
    grad_state = grad_out + grad_through
    branch_low = grad_state.astype(jnp.bfloat16)
    out_term = jnp.einsum("tc,td->cd", mixed_low, branch_low, preferred_element_type=jnp.float32)
    grad_mixed = (
        contract_last(branch_low, out_weight)
        .astype(jnp.bfloat16)
        .reshape(row_count, KV, groups, HD)
    )
    grad_probs = jnp.einsum(
        "rgjd,pgd->gjrp", grad_mixed, values_all, preferred_element_type=jnp.float32
    )
    row_delta = jnp.sum(attn_probs * grad_probs, axis=-1, keepdims=True)
    grad_score = (attn_probs * (grad_probs - row_delta)).astype(jnp.bfloat16)
    grad_queries = jnp.einsum(
        "gjrp,pgd->rgjd", grad_score, keys_all, preferred_element_type=jnp.float32
    ) * HD ** (-0.5)
    grad_keys = jnp.einsum(
        "gjrp,rgjd->pgd", grad_score, queries, preferred_element_type=jnp.float32
    ) * HD ** (-0.5)
    grad_values = jnp.einsum(
        "gjrp,rgjd->pgd", probs_low, grad_mixed, preferred_element_type=jnp.float32
    )
    key_grads, value_grads = (
        lax.psum_scatter(
            grad_keys.reshape(length, KV * HD).astype(jnp.bfloat16),
            "narrow",
            scatter_dimension=0,
            tiled=True,
        ).astype(jnp.float32),
        lax.psum_scatter(
            grad_values.reshape(length, KV * HD).astype(jnp.bfloat16),
            "narrow",
            scatter_dimension=0,
            tiled=True,
        ).astype(jnp.float32),
    )
    query_back = (
        rotate_back(grad_queries, cosine[:, None, None, :], sine_table[:, None, None, :])
        .reshape(row_count, H * HD)
        .astype(jnp.bfloat16)
    )
    key_back = (
        rotate_back(
            key_grads.reshape(row_count, KV, HD), cosine[:, None, :], sine_table[:, None, :]
        )
        .reshape(row_count, KV * HD)
        .astype(jnp.bfloat16)
    )
    value_back = value_grads.astype(jnp.bfloat16)
    query_term = jnp.einsum(
        "td,tc->dc", normed_attn, query_back, preferred_element_type=jnp.float32
    )
    key_term = jnp.einsum("td,tc->dc", normed_attn, key_back, preferred_element_type=jnp.float32)
    value_term = jnp.einsum(
        "td,tc->dc", normed_attn, value_back, preferred_element_type=jnp.float32
    )
    grad_normed_attn = (
        contract_last(query_back, query_weight)
        + contract_last(key_back, key_weight)
        + contract_last(value_back, value_weight)
    )
    attn_gain_term, grad_norm_input = norm_back(grad_normed_attn, run_input, attn_scale, attn_gain)
    grad_input = grad_state + grad_norm_input
    return (
        grad_input,
        (attn_gain_term, ffn_gain_term),
        (query_term, key_term, value_term, out_term, gate_term, up_term, down_term),
    )


def on_device_parts(
    block_input,
    cotangent,
    attn_gain,
    ffn_gain,
    query_weight,
    key_weight,
    value_weight,
    out_weight,
    gate_weight,
    up_weight,
    down_weight,
):
    seq_count = block_input.shape[0]
    row_count = block_input.shape[1]
    first_row = lax.axis_index("narrow") * row_count
    cosine, sine_table = rotary_tables(row_count, first_row)

    def current():
        return fetch_weights(
            query_weight, key_weight, value_weight, out_weight, gate_weight, up_weight, down_weight
        )

    start_states = [block_input[item].astype(jnp.float32) for item in range(seq_count)]
    weights_now = current()
    middle_states = [
        forward_run(state, attn_gain, ffn_gain, weights_now, cosine, sine_table, first_row)[0]
        for state in start_states
    ]
    weights_now = current()
    final_states = [
        forward_run(state, attn_gain, ffn_gain, weights_now, cosine, sine_table, first_row)[0]
        for state in middle_states
    ]
    grad_states = [cotangent[item].astype(jnp.float32) for item in range(seq_count)]
    gain_local = None
    weight_local = None
    for run_inputs in (middle_states, start_states):
        weights_now = current()
        next_grads = []
        for item in range(seq_count):
            recomputed, saved_parts = forward_run(
                run_inputs[item], attn_gain, ffn_gain, weights_now, cosine, sine_table, first_row
            )
            grad_input, gain_parts, weight_parts = backward_run(
                grad_states[item],
                run_inputs[item],
                saved_parts,
                attn_gain,
                ffn_gain,
                weights_now,
                cosine,
                sine_table,
            )
            next_grads.append(grad_input)
            if gain_local is None:
                gain_local = gain_parts
                weight_local = weight_parts
            else:
                gain_local = jax.tree.map(jnp.add, gain_local, gain_parts)
                weight_local = jax.tree.map(jnp.add, weight_local, weight_parts)
        grad_states = next_grads
    across = (
        lax.psum_scatter(
            weight_local[0].astype(jnp.bfloat16), "wide", scatter_dimension=1, tiled=True
        ).astype(jnp.float32),
        lax.psum_scatter(
            weight_local[1].astype(jnp.bfloat16), "wide", scatter_dimension=1, tiled=True
        ).astype(jnp.float32),
        lax.psum_scatter(
            weight_local[2].astype(jnp.bfloat16), "wide", scatter_dimension=1, tiled=True
        ).astype(jnp.float32),
        lax.psum_scatter(
            weight_local[3].astype(jnp.bfloat16), "wide", scatter_dimension=1, tiled=True
        ).astype(jnp.float32),
        lax.psum_scatter(
            weight_local[4].astype(jnp.bfloat16), "wide", scatter_dimension=1, tiled=True
        ).astype(jnp.float32),
        lax.psum_scatter(
            weight_local[5].astype(jnp.bfloat16), "wide", scatter_dimension=1, tiled=True
        ).astype(jnp.float32),
        lax.psum_scatter(
            weight_local[6].astype(jnp.bfloat16), "wide", scatter_dimension=1, tiled=True
        ).astype(jnp.float32),
    )
    reduced = (
        lax.psum_scatter(
            across[0].astype(jnp.bfloat16), "narrow", scatter_dimension=0, tiled=True
        ).astype(jnp.float32),
        lax.psum_scatter(
            across[1].astype(jnp.bfloat16), "narrow", scatter_dimension=0, tiled=True
        ).astype(jnp.float32),
        lax.psum_scatter(
            across[2].astype(jnp.bfloat16), "narrow", scatter_dimension=0, tiled=True
        ).astype(jnp.float32),
        lax.psum_scatter(
            across[3].astype(jnp.bfloat16), "narrow", scatter_dimension=0, tiled=True
        ).astype(jnp.float32),
        lax.psum_scatter(
            across[4].astype(jnp.bfloat16), "narrow", scatter_dimension=0, tiled=True
        ).astype(jnp.float32),
        lax.psum_scatter(
            across[5].astype(jnp.bfloat16), "narrow", scatter_dimension=0, tiled=True
        ).astype(jnp.float32),
        lax.psum_scatter(
            across[6].astype(jnp.bfloat16), "narrow", scatter_dimension=0, tiled=True
        ).astype(jnp.float32),
    )
    gain_totals = lax.psum((gain_local[0], gain_local[1]), ("wide", "narrow"))
    block_output = jnp.stack(final_states).astype(jnp.bfloat16)
    input_grad = jnp.stack(grad_states)
    return (
        block_output,
        input_grad,
        gain_totals[0],
        gain_totals[1],
        reduced[0],
        reduced[1],
        reduced[2],
        reduced[3],
        reduced[4],
        reduced[5],
        reduced[6],
    )


def on_device(block_input, *rest):
    pieces = sum(weight.shape[1] for weight in rest[3:7])
    fits = (
        (lax.axis_size("wide"), lax.axis_size("narrow")) == (16, 2)
        and block_input.shape[0] == 2
        and block_input.shape[2] <= WIDE
        and {pieces, rest[7].shape[1], rest[8].shape[1], rest[9].shape[1]} == {PIECE}
    )
    plan = on_device_whole if fits else on_device_parts
    return plan(block_input, *rest)


def solution(mesh):
    placed = (
        P("wide", "narrow", None),
        P("wide", "narrow", None),
        P(),
        P(),
        P("narrow", "wide"),
        P("narrow", "wide"),
        P("narrow", "wide"),
        P("narrow", "wide"),
        P("narrow", "wide"),
        P("narrow", "wide"),
        P("narrow", "wide"),
    )
    return jax.shard_map(
        on_device,
        mesh=mesh,
        in_specs=placed,
        out_specs=(
            P("wide", "narrow", None),
            P("wide", "narrow", None),
            P(),
            P(),
            P("narrow", "wide"),
            P("narrow", "wide"),
            P("narrow", "wide"),
            P("narrow", "wide"),
            P("narrow", "wide"),
            P("narrow", "wide"),
            P("narrow", "wide"),
        ),
        check_vma=False,
    )
```

```python
import functools

import jax
import jax.numpy as jnp
import numpy as np
from jax import lax
from jax.experimental import pallas as pl
from jax.experimental.pallas import tpu as pltpu
from jax.sharding import PartitionSpec as P

H = 15
KV = 5
HD = 64
MESH = pl.DeviceIdType.MESH
F32 = jnp.float32
BF16 = jnp.bfloat16
GROUP = H // KV
PIECE = 160
CHUNKS = 5
ROWS = PIECE // CHUNKS
UNITS = 16 * ROWS
HALF = 512
WIDE = 2 * HALF
KEY_AT = H * HD
VALUE_AT = KEY_AT + KV * HD
QKV = VALUE_AT + KV * HD
VMEM_LIMIT = 62 << 20


def nt(left, right):
    return lax.dot_general(left, right, (((1,), (1,)), ((), ())), preferred_element_type=F32)


def nn(left, right):
    return jnp.dot(left, right, preferred_element_type=F32)


def tn(left, right):
    return lax.dot_general(left, right, (((0,), (0,)), ((), ())), preferred_element_type=F32)


def whole(*shape):
    return pl.BlockSpec(shape, lambda *_: (0,) * len(shape), pipeline_mode=pl.Buffered(1))


def compiler(**more):
    return pltpu.CompilerParams(vmem_limit_bytes=VMEM_LIMIT, **more)


def cost(flops, moved):
    return pl.CostEstimate(flops=int(flops), bytes_accessed=int(moved), transcendentals=0)


def span(ref, rows):
    return ref.at[..., pl.ds(rows[0], rows[1] - rows[0]), :]


class Place:
    def __init__(self):
        self.w = lax.axis_index("wide")
        self.y = lax.axis_index("narrow")
        self.z = self.w // 4
        self.x = (self.w // 2) % 2
        self.c = self.w % 2
        self.sibling = (self.w + 1 - 2 * self.c, self.y)

    def partners(self, dim):
        if dim == "x":
            return [(1 - self.x, (self.w + 2 - 4 * self.x, self.y))]
        if dim == "y":
            return [(1 - self.y, (self.w, 1 - self.y))]
        others = [(self.z + far) % 4 for far in (1, 2, 3)]
        return [(other, (self.w + 4 * (other - self.z), self.y)) for other in others]

    def origins(self, dim):
        if dim == "z":
            return [(self.z + far) % 4 for far in (3, 2, 1)]
        return [1 - getattr(self, dim)]

    def everyone(self):
        return [self.sibling] + [device for dim in "xyz" for _, device in self.partners(dim)]


def greet(devices):
    barrier = pltpu.get_barrier_semaphore()
    for device in devices:
        pl.semaphore_signal(barrier, inc=1, device_id=device, device_id_type=MESH)
    pl.semaphore_wait(barrier, len(devices))


def remote(source, target, send_sem, recv_sem, device):
    return pltpu.make_async_remote_copy(
        src_ref=source,
        dst_ref=target,
        send_sem=send_sem,
        recv_sem=recv_sem,
        device_id=device,
        device_id_type=MESH,
    )


STEPS = 3


class Gather:
    def __init__(self, me, flows, own, full, keep_sem, send, recv, cross_send, cross_recv):
        self.me, self.flows, self.own, self.full = me, flows, own, full
        self.keep_sem, self.send, self.recv = keep_sem, send, recv
        self.cross_send, self.cross_recv = cross_send, cross_recv

    def keep(self, t):
        me = self.me
        return pltpu.make_async_copy(
            self.own[t], self.full[t].at[me.y, me.z, me.x, me.c], self.keep_sem.at[t]
        )

    def blocks(self, t, flow, step, place):
        me = self.me
        rows, order = self.flows[t][flow]
        at = {"y": me.y, "z": me.z, "x": me.x}
        for name in order[:step]:
            at[name] = slice(None)
        at[order[step]] = place
        return span(self.full[t].at[at["y"], at["z"], at["x"], me.c], rows)

    def copies(self, t, flow, step):
        me = self.me
        rows, order = self.flows[t][flow]
        dim = order[step]
        target = self.blocks(t, flow, step, getattr(me, dim))
        source = span(self.own[t], rows) if step == 0 else target
        return [
            remote(
                source, target, self.send.at[t, flow, step, i], self.recv.at[t, flow, step, i], device
            )
            for i, (_, device) in enumerate(me.partners(dim))
        ]

    def landing(self, t, flow, step):
        me = self.me
        dim = self.flows[t][flow][1][step]
        devices = me.partners(dim)
        blocks = [self.blocks(t, flow, step, place) for place in me.origins(dim)]
        return [
            remote(
                block, block, self.send.at[t, flow, step, i], self.recv.at[t, flow, step, i],
                devices[i][1],
            )
            for i, block in enumerate(blocks)
        ]

    def cross(self, t, flow):
        blocks = span(self.full[t].at[:, :, :, self.me.c], self.flows[t][flow][0])
        return remote(
            blocks, blocks, self.cross_send.at[t, flow], self.cross_recv.at[t, flow],
            self.me.sibling,
        )

    def stage(self, t, step):
        count = len(self.flows[t])
        if step == 0:
            self.keep(t).start()
        if step == 1:
            self.keep(t).wait()
        for flow in range(count):
            if 0 < step <= STEPS:
                for copy in self.landing(t, flow, step - 1):
                    copy.wait_recv()
            if step < STEPS:
                for copy in self.copies(t, flow, step):
                    copy.start()
            if step == STEPS:
                self.cross(t, flow).start()
            if step == STEPS + 1:
                self.cross(t, flow).wait()
                for before in range(STEPS):
                    for copy in self.copies(t, flow, before):
                        copy.wait_send()

    @staticmethod
    def semaphores(types, flows):
        dma = pltpu.SemaphoreType.DMA
        return [
            dma((types,)), dma((types, flows, STEPS, 3)), dma((types, flows, STEPS, 3)),
            dma((types, flows)), dma((types, flows)),
        ]


class Scatter:
    def __init__(self, me, flows, terms, out, scratch):
        self.me, self.flows, self.terms, self.out = me, flows, terms, out
        (
            self.acc, self.arrived, self.load_sem, self.cross_send, self.cross_recv, self.send,
            self.recv, *self.buffers,
        ) = scratch
        self.piece = self.acc.shape[-2]

    @staticmethod
    def scratch(flows, piece):
        dma = pltpu.SemaphoreType.DMA
        types, count = len(flows), len(flows[0])
        refs = [
            pltpu.VMEM((types, 2, 4, 2, piece, HALF), BF16),
            pltpu.VMEM((types, 2, 4, 2, piece, HALF), BF16),
            dma((types,)), dma((types,)), dma((types,)),
            dma((types, count, STEPS, 3)), dma((types, count, STEPS, 3)),
        ]
        for own_flows in flows:
            for rows, order in own_flows:
                for step, dim in enumerate(order):
                    left = order[step + 1 :]
                    shape = tuple({"y": 2, "z": 4, "x": 2}[name] for name in "yzx" if name in left)
                    lines = (3 if dim == "z" else 1,)
                    refs.append(pltpu.VMEM(lines + shape + (rows[1] - rows[0], HALF), BF16))
        return refs

    def buffer(self, t, flow, step):
        return self.buffers[(t * len(self.flows[0]) + flow) * STEPS + step]

    def source(self, t, core):
        ref, first = self.terms[t]
        return span(ref.at[:, :, :, core], (first, first + self.piece))

    def cross(self, t):
        return remote(
            self.source(t, 1 - self.me.c), self.arrived.at[t], self.cross_send.at[t],
            self.cross_recv.at[t], self.me.sibling,
        )

    def load(self, t):
        return pltpu.make_async_copy(
            self.source(t, self.me.c), self.acc.at[t], self.load_sem.at[t]
        )

    def blocks(self, t, flow, step, place):
        rows, order = self.flows[t][flow]
        at = {"y": slice(None), "z": slice(None), "x": slice(None)}
        for name in order[:step]:
            at[name] = getattr(self.me, name)
        at[order[step]] = place
        return span(self.acc.at[t, at["y"], at["z"], at["x"]], rows)

    def copies(self, t, flow, step):
        buffer = self.buffer(t, flow, step)
        return [
            remote(
                self.blocks(t, flow, step, place), buffer.at[i], self.send.at[t, flow, step, i],
                self.recv.at[t, flow, step, i], device,
            )
            for i, (place, device) in enumerate(self.me.partners(self.flows[t][flow][1][step]))
        ]

    def take(self, t, flow, step):
        copies = self.copies(t, flow, step)
        for copy in copies:
            copy.wait_recv()
        target = self.blocks(t, flow, step, getattr(self.me, self.flows[t][flow][1][step]))
        buffer = self.buffer(t, flow, step)

        def add(*index):
            value = target.at[index][...] if index else target[...]
            for i in range(len(copies)):
                value = value + buffer.at[(i,) + index][...]
            if index:
                target.at[index][...] = value
            else:
                target[...] = value

        if len(target.shape) == 2:
            add()
        else:

            @pl.loop(0, target.shape[0])
            def _(index):
                add(index)

    def stage(self, t, step):
        flows = range(len(self.flows[t]))
        if step == 0:
            self.cross(t).start()
            self.load(t).start()
        if step == 1:
            self.load(t).wait()
            self.cross(t).wait()

            @pl.loop(0, 8)
            def _(index):
                half, block = index // 4, index % 4
                self.acc[t, half, block] = self.acc[t, half, block] + self.arrived[t, half, block]

        for flow in flows:
            if step > 2:
                self.take(t, flow, step - 3)
            if 2 <= step <= STEPS + 1:
                for copy in self.copies(t, flow, step - 2):
                    copy.start()
        if step == STEPS + 2:
            me = self.me
            for flow in flows:
                for before in range(STEPS):
                    for copy in self.copies(t, flow, before):
                        copy.wait_send()
            self.out[t] = self.acc[t, me.y, me.z, me.x].astype(F32)


def staggered(types, stages, gap=1):
    ticks = stages + gap * (types - 1)
    return [
        [(t, tick - gap * t) for t in range(types) if 0 <= tick - gap * t < stages]
        for tick in range(ticks)
    ]


def widen(turned, half, model):
    size = model // 2
    part = turned[half * size : (half + 1) * size, :].astype(F32)
    fill = jnp.zeros((HALF - size, part.shape[1]), F32)
    return jnp.concatenate([part, fill], axis=0).T


def narrow(value, half, model):
    return value[:, half * HALF : (half + 1) * HALF].T[: model // 2]


def turn_head(rows, cos, sin, back=False):
    first, second = rows[: HD // 2], rows[HD // 2 :]
    if back:
        return first * cos + second * sin, second * cos - first * sin
    return first * cos - second * sin, second * cos + first * sin


def qkv_kernel(model, state, gain, weight, cosine, sine, normed, scale, queries, keys, values):
    inputs = state[...]
    inv = lax.rsqrt(jnp.sum(inputs * inputs, axis=-1, keepdims=True) * (1.0 / model) + 1e-05)
    scale[...] = inv
    low = (inputs * inv * gain[...]).astype(BF16)
    normed[...] = low
    left, right = low[:, :HALF], low[:, HALF:]
    cos, sin = cosine[...], sine[...]
    count = KV * HD
    for first in range(0, QKV, count):
        rows = pl.ds(first, count)
        pre = nt(weight[0, rows, :], left) + nt(weight[1, rows, :], right)
        for index in range(KV):
            part = pre[index * HD : (index + 1) * HD]
            if first >= VALUE_AT:
                values[index] = part.astype(BF16)
                continue
            top, bottom = turn_head(part, cos, sin)
            if first < KEY_AT:
                head = first // HD + index
                queries[head, : HD // 2, :] = (top * HD ** (-0.5)).astype(BF16)
                queries[head, HD // 2 :, :] = (bottom * HD ** (-0.5)).astype(BF16)
            else:
                keys[index, : HD // 2, :] = top.astype(BF16)
                keys[index, HD // 2 :, :] = bottom.astype(BF16)


def qkv_call(model, state, gain, weight, cosine, sine, rows=512):
    tokens = state.shape[0]
    by_row = lambda width: pl.BlockSpec((rows, width), lambda i: (i, 0))
    by_lane = pl.BlockSpec((HD // 2, rows), lambda i: (0, i))
    heads = lambda count: pl.BlockSpec((count, HD, rows), lambda i: (0, 0, i))
    return pl.pallas_call(
        functools.partial(qkv_kernel, model),
        grid=(tokens // rows,),
        in_specs=[by_row(WIDE), whole(1, WIDE), whole(2, QKV, HALF), by_lane, by_lane],
        out_specs=[by_row(WIDE), by_row(1), heads(H), heads(KV), heads(KV)],
        out_shape=[
            jax.ShapeDtypeStruct((tokens, WIDE), BF16),
            jax.ShapeDtypeStruct((tokens, 1), F32),
            jax.ShapeDtypeStruct((H, HD, tokens), BF16),
            jax.ShapeDtypeStruct((KV, HD, tokens), BF16),
            jax.ShapeDtypeStruct((KV, HD, tokens), BF16),
        ],
        compiler_params=compiler(),
        cost_estimate=cost(2 * tokens * WIDE * QKV, 20e6),
        name="project_qkv",
    )(state, gain, weight, cosine, sine)


def key_mask(block):
    row = lax.broadcasted_iota(jnp.int32, (block, GROUP * block), 0)
    column = lax.broadcasted_iota(jnp.int32, (block, GROUP * block), 1)
    return row <= jnp.bitwise_and(column, block - 1)


def group_block(ref, at, block):
    return jnp.concatenate([ref[head, :, at : at + block] for head in range(GROUP)], axis=1)


def ahead_of(items, count, make):
    pending = [make(item) for item in items[:count]]
    for turn, item in enumerate(items):
        if turn + count < len(items):
            pending.append(make(items[turn + count]))
        yield item, pending.pop(0)


def attend_kernel(block, ahead, queries, keys, values, mixed, log_sum):
    tokens = keys.shape[2]
    key_rows = keys[0].T

    def scores(at):
        query = group_block(queries, at, block)
        tiles = [nn(key_rows[first : first + block], query) for first in range(0, at + block, block)]
        tiles[-1] = jnp.where(key_mask(block), tiles[-1], -jnp.inf)
        return tiles

    for at, tiles in ahead_of(list(range(0, tokens, block)), ahead, scores):
        peak = functools.reduce(
            jnp.maximum, [jnp.max(tile, axis=0, keepdims=True) for tile in tiles]
        )
        total = out = 0.0
        for index, score in enumerate(tiles):
            weight = jnp.exp(score - peak)
            total = total + jnp.sum(weight, axis=0, keepdims=True)
            value = values[0, :, index * block : (index + 1) * block]
            out = out + nn(value, weight.astype(BF16))
        out = (out * (1.0 / total)).astype(BF16)
        logs = peak + jnp.log(total)
        for head in range(GROUP):
            part = slice(head * block, (head + 1) * block)
            mixed[head, :, at : at + block] = out[:, part]
            log_sum[head, :, at : at + block] = logs[:, part]


def attend_call(queries, keys, values, block=256):
    tokens = queries.shape[2]
    heads = lambda count: pl.BlockSpec((count, HD, tokens), lambda i: (i, 0, 0))
    return pl.pallas_call(
        functools.partial(attend_kernel, block, 3),
        grid=(KV,),
        in_specs=[heads(GROUP), heads(1), heads(1)],
        out_specs=[heads(GROUP), pl.BlockSpec((GROUP, 1, tokens), lambda i: (i, 0, 0))],
        out_shape=[
            jax.ShapeDtypeStruct((H, HD, tokens), BF16),
            jax.ShapeDtypeStruct((H, 1, tokens), F32),
        ],
        compiler_params=compiler(),
        cost_estimate=cost(4 * tokens * tokens * H * 128, 20e6),
        name="attend",
    )(queries, keys, values)


def attend_back_kernel(
    block, queries, keys, values, log_sum, grad_mixed, grad_queries, grad_keys, grad_values
):
    tokens = keys.shape[2]
    key_rows, value_rows = keys[0].T, values[0].T

    def products(at):
        query, grad = group_block(queries, at, block), group_block(grad_mixed, at, block)
        return [
            (
                nn(key_rows[first : first + block], query),
                nn(value_rows[first : first + block], grad),
            )
            for first in range(0, at + block, block)
        ]

    for at, tiles in ahead_of(list(range(tokens - block, -1, -block)), 1, products):
        query, grad = group_block(queries, at, block), group_block(grad_mixed, at, block)
        logs = group_block(log_sum, at, block)
        weights = []
        delta = 0.0
        for index, (score, grad_probs) in enumerate(tiles):
            probs = jnp.exp(score - logs)
            if index * block == at:
                probs = jnp.where(key_mask(block), probs, 0.0)
            delta = delta + jnp.sum(probs * grad_probs, axis=0, keepdims=True)
            weights.append(probs)
        by_query = 0.0
        for index, (_, grad_probs) in enumerate(tiles):
            part = pl.ds(index * block, block)
            probs = weights[index]
            low = (probs * (grad_probs - delta)).astype(BF16)
            by_query = by_query + nn(keys[0, :, part], low)
            key_part = nt(query, low)
            value_part = nt(grad, probs.astype(BF16))
            if at + block == tokens:
                grad_keys[0, :, part] = key_part
                grad_values[0, :, part] = value_part
            else:
                grad_keys[0, :, part] += key_part
                grad_values[0, :, part] += value_part
        for head in range(GROUP):
            grad_queries[head, :, at : at + block] = by_query[:, head * block : (head + 1) * block]


def attend_back_call(queries, keys, values, log_sum, grad_mixed, block=256):
    tokens = queries.shape[2]
    heads = lambda count: pl.BlockSpec((count, HD, tokens), lambda i: (i, 0, 0))
    return pl.pallas_call(
        functools.partial(attend_back_kernel, block),
        grid=(KV,),
        in_specs=[
            heads(GROUP), heads(1), heads(1),
            pl.BlockSpec((GROUP, 1, tokens), lambda i: (i, 0, 0)), heads(GROUP),
        ],
        out_specs=[heads(GROUP), heads(1), heads(1)],
        out_shape=[
            jax.ShapeDtypeStruct((H, HD, tokens), F32),
            jax.ShapeDtypeStruct((KV, HD, tokens), F32),
            jax.ShapeDtypeStruct((KV, HD, tokens), F32),
        ],
        compiler_params=compiler(),
        cost_estimate=cost(10 * tokens * tokens * H * 128, 30e6),
        name="attend_back",
    )(queries, keys, values, log_sum, grad_mixed)


GATHER_FLOWS = ((((0, 80), "zyx"), ((80, 128), "zxy"), ((128, 160), "yxz")),) + (
    (((0, 48), "zyx"), ((48, 80), "zxy"), ((80, 96), "yxz")),
) * CHUNKS


def order_weights(model, sizes, sorter, raw, qkv_weight, out_weight):
    counts = [4 * size for size in sizes]
    starts = [sum(counts[:i]) for i in range(4)]
    rows = 4 * PIECE
    size = model // 2
    blank = jnp.zeros((HALF - size, HALF), F32)
    for half in range(2):
        for pair in range(2):
            outs = []
            for z in (2 * pair, 2 * pair + 1):
                block = raw[half, z * rows : (z + 1) * rows, :]
                done = nn(sorter[...], block)
                for i, first in enumerate((0, KEY_AT, VALUE_AT)):
                    at = first + z * counts[i]
                    part = done[starts[i] : starts[i] + counts[i]]
                    qkv_weight[half, at : at + counts[i], :] = part.astype(BF16)
                outs.append(done[starts[3] :])
            turned = jnp.concatenate(outs + [blank], axis=0).T
            out_weight[half * size : (half + 1) * size, pair * HALF : (pair + 1) * HALF] = turned[
                :size
            ].astype(BF16)


def sorter_matrix(sizes):
    rows = 4 * PIECE
    matrix = np.zeros((rows, rows), np.float32)
    to = 0
    first = 0
    for size in sizes:
        for device in range(4):
            for row in range(size):
                matrix[to, device * PIECE + first + row] = 1.0
                to += 1
        first += size
    return matrix


def sigmoid(value):
    return 0.5 * jnp.tanh(0.5 * value) + 0.5


def feed_block(gate_weight, up_weight, normed, rows, gate, up):
    left, right = normed[rows, :HALF], normed[rows, HALF:]
    gate_proj = nt(left, gate_weight[0]) + nt(right, gate_weight[1])
    up_proj = nt(left, up_weight[0]) + nt(right, up_weight[1])
    gate[rows, :] = gate_proj.astype(BF16)
    up[rows, :] = up_proj.astype(BF16)
    return (gate_proj * sigmoid(gate_proj) * up_proj).astype(BF16)


def out_block(model, state, mixed, out_weight, gain, hidden_state, normed, scale):
    heads = mixed[...].reshape(H * HD, mixed.shape[2])
    after = state[...] + tn(heads, out_weight[...])
    hidden_state[...] = after
    inv = lax.rsqrt(jnp.sum(after * after, axis=-1, keepdims=True) * (1.0 / model) + 1e-05)
    scale[...] = inv
    normed[...] = (after * inv * gain[...]).astype(BF16)


START_KINDS = lambda tokens, units: [
    ((2, QKV, HALF), BF16),
    ((H * HD, WIDE), BF16),
    ((tokens, WIDE), F32),
    ((tokens, WIDE), BF16),
    ((tokens, 1), F32),
    ((H, HD, tokens), BF16),
    ((KV, HD, tokens), BF16),
    ((KV, HD, tokens), BF16),
    ((H, 1, tokens), F32),
    ((tokens, WIDE), F32),
    ((H, HD, tokens), BF16),
    ((tokens, WIDE), BF16),
    ((tokens, 1), F32),
]


def feed_spec(t, first=0):
    return pl.BlockSpec(
        (None, 2, 4, 2, 2, ROWS, HALF), lambda i: (first + i, 0, 0, 0, 0, t, 0)
    )


def start_kernel(
    model, sizes, own, feed_own, seqs, gain, feed_gain, cosine, sine, sorter,
    full, feed_full, output_out, gate_out, up_out, *rest,
):
    kinds = len(START_KINDS(0, 0))
    outs_refs, rest = rest[:kinds], rest[kinds:]
    (
        qkv_weight, out_weight, state, normed, scale, queries, keys, values, log_sum, hidden_state,
        mixed, feed_normed, feed_scale,
    ), rest = rest[:kinds], rest[kinds:]
    seq, seq_sem, raw_sem, out_sem, *gather_sems = rest
    me = Place()
    y = me.y
    gather = Gather(
        me, GATHER_FLOWS, [own] + [feed_own.at[i] for i in range(CHUNKS)],
        [full] + [feed_full.at[i] for i in range(CHUNKS)], *gather_sems,
    )
    greet(me.everyone())
    swap = remote(
        seqs.at[1 - y], seq.at[y], seq_sem.at[0], seq_sem.at[1], me.partners("y")[0][1]
    )
    swap.start()
    stay = pltpu.make_async_copy(seqs.at[y], seq.at[y], seq_sem.at[2])
    stay.start()
    ticks = staggered(1 + CHUNKS, STEPS + 2)

    def tick(*counts):
        for count in counts:
            for t, stage in ticks[count]:
                gather.stage(t, stage)

    tick(0, 1, 2)
    rows = seq.shape[2]
    tokens = 2 * rows
    outs = []

    def give(index, source):
        copy = pltpu.make_async_copy(source, outs_refs[index], out_sem.at[index])
        copy.start()
        outs.append(copy)

    stay.wait()
    swap.wait()
    for part in range(2):
        for half in range(2):
            state[part * rows : (part + 1) * rows, half * HALF : (half + 1) * HALF] = widen(
                seq.at[part], half, model
            )
    give(2, state)
    tick(3, 4)

    def put_in_order(raw):
        fetch = pltpu.make_async_copy(full, raw, raw_sem.at[0])
        fetch.start()
        fetch.wait()
        order_weights(
            model, sizes, sorter, raw.reshape(2, 16 * PIECE, HALF), qkv_weight, out_weight
        )

    pl.run_scoped(put_in_order, pltpu.VMEM((2, 4, 2, 2, PIECE, HALF), BF16))
    give(0, qkv_weight)
    give(1, out_weight)
    for at in range(0, tokens, rows):
        part = pl.ds(at, rows)
        qkv_kernel(
            model, state.at[part], gain, qkv_weight, cosine.at[:, part], sine.at[:, part],
            normed.at[part], scale.at[part], queries.at[:, :, part], keys.at[:, :, part],
            values.at[:, :, part],
        )
    give(3, normed)
    give(4, scale)
    give(5, queries)
    give(6, keys)
    give(7, values)
    tick(5)

    @pl.loop(0, KV)
    def _(group):
        some = pl.ds(group * GROUP, GROUP)
        one = pl.ds(group, 1)
        attend_kernel(
            tokens // 4, 1, queries.at[some], keys.at[one], values.at[one], mixed.at[some],
            log_sum.at[some],
        )
        pl.when(group == 1)(lambda: tick(6))
        pl.when(group == 4)(lambda: tick(7))

    give(8, log_sum)
    give(10, mixed)
    out_block(model, state, mixed, out_weight, feed_gain, hidden_state, feed_normed, feed_scale)
    give(9, hidden_state)
    give(11, feed_normed)
    give(12, feed_scale)

    outs[0].wait()
    state[...] = hidden_state[...]

    def feed_body(gate_weight, up_weight, down_weight, gate, up):
        gates, ups, downs = (
            ref.reshape(2, UNITS, HALF) for ref in (gate_weight, up_weight, down_weight)
        )
        for at in range(0, tokens, rows):
            part = pl.ds(at, rows)
            low = feed_block(gates, ups, feed_normed, part, gate, up)
            state[part, :HALF] += nn(low, downs[0])
            state[part, HALF:] += nn(low, downs[1])

    def feed_chunks(first, count):
        by_unit = pl.BlockSpec((tokens, UNITS), lambda i: (0, first + i))
        pltpu.emit_pipeline(
            feed_body,
            grid=(count,),
            in_specs=[feed_spec(t, first) for t in range(3)],
            out_specs=[by_unit, by_unit],
        )(feed_full, feed_full, feed_full, gate_out, up_out)

    tick(8)
    feed_chunks(0, 3)
    tick(9)
    feed_chunks(3, 2)
    last = pltpu.make_async_copy(state, output_out, raw_sem.at[0])
    last.start()
    for copy in outs[1:]:
        copy.wait()
    last.wait()


def start_call(model, sizes, own, feed_own, seqs, gain, feed_gain, cosine, sine, sorter):
    types = 1 + CHUNKS
    tokens = 2 * seqs.shape[2]
    units = 16 * PIECE
    kinds = START_KINDS(tokens, units)
    dma = pltpu.SemaphoreType.DMA
    anywhere = pl.BlockSpec(memory_space=pl.ANY)
    inside = pl.BlockSpec(memory_space=pltpu.VMEM)
    outs = [
        ((2, 4, 2, 2, PIECE, HALF), BF16),
        ((CHUNKS, 2, 4, 2, 2, 3 * ROWS, HALF), BF16),
        ((tokens, WIDE), F32),
        ((tokens, units), BF16),
        ((tokens, units), BF16),
    ] + kinds
    return pl.pallas_call(
        functools.partial(start_kernel, model, sizes),
        out_shape=[jax.ShapeDtypeStruct(*kind) for kind in outs],
        in_specs=[anywhere] * 3 + [inside] * 5,
        out_specs=[anywhere] * len(outs),
        scratch_shapes=[pltpu.VMEM(*kind) for kind in kinds]
        + [
            pltpu.VMEM(seqs.shape, BF16),
            dma((3,)), dma((1,)), dma((len(kinds),)),
        ]
        + Gather.semaphores(types, len(GATHER_FLOWS[0])),
        compiler_params=compiler(collective_id=0, has_side_effects=True),
        name="start",
    )(own, feed_own, seqs, gain, feed_gain, cosine, sine, sorter)


def feed_kernel(
    model, block, state, heads, out_weight, gain, gate_weight, up_weight, down_weight,
    final, hidden_state, normed, scale, gate, up, output,
):
    tokens = state.shape[0]

    @pl.when(pl.program_id(0) == 0)
    def _():
        out_block(model, state, heads, out_weight, gain, hidden_state, normed, scale)
        output[...] = hidden_state[...]

    gate_weight, up_weight, down_weight = (
        ref.reshape(2, UNITS, HALF) for ref in (gate_weight, up_weight, down_weight)
    )
    for at in range(0, tokens, block):
        rows = pl.ds(at, block)
        hidden = feed_block(gate_weight, up_weight, normed, rows, gate, up)
        output[rows, :HALF] += nn(hidden, down_weight[0])
        output[rows, HALF:] += nn(hidden, down_weight[1])

    @pl.when(pl.program_id(0) == pl.num_programs(0) - 1)
    def _():
        size = model // 2
        for part in range(2):
            value = output[part * tokens // 2 : (part + 1) * tokens // 2, :]
            for half in range(2):
                final[part, half * size : (half + 1) * size, :] = narrow(value, half, model).astype(
                    BF16
                )


def feed_call(model, state, heads, out_weight, gain, weights, block=512):
    tokens = state.shape[0]
    units = CHUNKS * UNITS
    by_unit = pl.BlockSpec((tokens, UNITS), lambda i: (0, i))
    return pl.pallas_call(
        functools.partial(feed_kernel, model, block),
        grid=(CHUNKS,),
        in_specs=[
            whole(tokens, WIDE), whole(H, HD, tokens), whole(H * HD, WIDE), whole(1, WIDE),
            feed_spec(0), feed_spec(1), feed_spec(2),
        ],
        out_specs=[
            whole(2, model, tokens // 2), whole(tokens, WIDE), whole(tokens, WIDE),
            whole(tokens, 1), by_unit, by_unit,
        ],
        out_shape=[
            jax.ShapeDtypeStruct((2, model, tokens // 2), BF16),
            jax.ShapeDtypeStruct((tokens, WIDE), F32),
            jax.ShapeDtypeStruct((tokens, WIDE), BF16),
            jax.ShapeDtypeStruct((tokens, 1), F32),
            jax.ShapeDtypeStruct((tokens, units), BF16),
            jax.ShapeDtypeStruct((tokens, units), BF16),
        ],
        scratch_shapes=[pltpu.VMEM((tokens, WIDE), F32)],
        compiler_params=compiler(),
        cost_estimate=cost(2 * tokens * WIDE * (3 * units + H * HD), 50e6),
        name="feed",
    )(state, heads, out_weight, gain, weights, weights, weights)


def feed_back_kernel(
    model, block, pair, *refs,
):
    step = pl.program_id(0)
    if pair:
        mine, other, *refs = refs
        *refs, grad_out = refs
    else:
        grad_out, *refs = refs
    (
        hidden_state, gain, scale, gate, up, gate_weight, up_weight, down_weight,
        grad_state, gain_term, grad_low, grad_gate, grad_up, hidden,
    ) = refs
    tokens = grad_out.shape[0]

    @pl.when(step == 0)
    def _():
        if pair:
            count = tokens // 2
            y = lax.axis_index("narrow")
            for place, turned in ((y, mine), (1 - y, other)):
                rows = pl.ds(pl.multiple_of(place * count, count), count)
                for half in range(2):
                    columns = pl.ds(half * HALF, HALF)
                    grad_out[rows, columns] = widen(turned, half, model)
        grad_low[...] = grad_out[...].astype(BF16)
        grad_state[...] = jnp.zeros_like(grad_state)

    gate_weight, up_weight, down_weight = (
        ref.reshape(2, UNITS, HALF) for ref in (gate_weight, up_weight, down_weight)
    )

    for at in range(0, tokens, block):
        rows = pl.ds(at, block)
        grad_hidden = nt(grad_low[rows, :HALF], down_weight[0]) + nt(
            grad_low[rows, HALF:], down_weight[1]
        )
        gate_proj = gate[rows, :].astype(F32)
        up_proj = up[rows, :].astype(F32)
        sig = sigmoid(gate_proj)
        passed = gate_proj * sig
        hidden[rows, :] = (passed * up_proj).astype(BF16)
        by_gate = (grad_hidden * up_proj * (sig + passed * (1.0 - sig))).astype(BF16)
        by_up = (grad_hidden * passed).astype(BF16)
        grad_gate[rows, :] = by_gate
        grad_up[rows, :] = by_up
        grad_state[rows, :HALF] += nn(by_gate, gate_weight[0]) + nn(by_up, up_weight[0])
        grad_state[rows, HALF:] += nn(by_gate, gate_weight[1]) + nn(by_up, up_weight[1])

    @pl.when(step == pl.num_programs(0) - 1)
    def _():
        total = jnp.zeros(gain.shape, F32)
        for at in range(0, tokens, block):
            rows = pl.ds(at, block)
            grad, after, inv = grad_state[rows, :], hidden_state[rows, :], scale[rows, :]
            total = total + jnp.sum(grad * after * inv, axis=0, keepdims=True)
            upstream = grad * gain[...]
            inner = jnp.sum(upstream * after, axis=-1, keepdims=True) * (1.0 / model)
            grad_state[rows, :] = (
                grad_out[rows, :] + inv * upstream - after * (inv * inv * inv) * inner
            )
        gain_term[...] = total


def feed_back_call(
    model, grads, hidden_state, gain, scale, gate, up, weights, block=512
):
    tokens = hidden_state.shape[0]
    pair = len(grads) == 2
    units = CHUNKS * UNITS
    by_unit = pl.BlockSpec((tokens, UNITS), lambda i: (0, i))
    return pl.pallas_call(
        functools.partial(feed_back_kernel, model, block, pair),
        grid=(CHUNKS,),
        in_specs=[
            whole(*grad.shape) for grad in grads
        ]
        + [
            whole(tokens, WIDE), whole(1, WIDE), whole(tokens, 1),
            by_unit, by_unit, feed_spec(0), feed_spec(1), feed_spec(2),
        ],
        out_specs=[whole(tokens, WIDE), whole(1, WIDE), whole(tokens, WIDE)] + [by_unit] * 3,
        out_shape=[
            jax.ShapeDtypeStruct((tokens, WIDE), F32),
            jax.ShapeDtypeStruct((1, WIDE), F32),
            jax.ShapeDtypeStruct((tokens, WIDE), BF16),
        ]
        + [jax.ShapeDtypeStruct((tokens, units), BF16)] * 3,
        scratch_shapes=[pltpu.VMEM((tokens, WIDE), F32)] if pair else [],
        compiler_params=compiler(),
        cost_estimate=cost(6 * tokens * WIDE * units, 60e6),
        name="feed_back",
    )(*grads, hidden_state, gain, scale, gate, up, weights, weights, weights)


def out_back_rows(low, out_weight, grad_mixed):
    grads = nt(out_weight[...], low).astype(BF16)
    grad_mixed[...] = grads.reshape(grad_mixed.shape)


def out_back_kernel(grad_state, out_weight, grad_mixed):
    out_back_rows(grad_state[...].astype(BF16), out_weight, grad_mixed)


def out_back_call(grad_state, out_weight, rows=512):
    tokens = grad_state.shape[0]
    return pl.pallas_call(
        out_back_kernel,
        grid=(tokens // rows,),
        in_specs=[pl.BlockSpec((rows, WIDE), lambda i: (i, 0)), whole(H * HD, WIDE)],
        out_specs=pl.BlockSpec((H, HD, rows), lambda i: (0, 0, i)),
        out_shape=jax.ShapeDtypeStruct((H, HD, tokens), BF16),
        compiler_params=compiler(),
        cost_estimate=cost(2 * tokens * WIDE * H * HD, 10e6),
        name="out_back",
    )(grad_state, out_weight)


def qkv_back_rows(
    model, grad_queries, grad_keys, grad_values, state, scale, grad_state, gain, weight, cosine, sine,
    back,
):
    cos, sin = cosine[...], sine[...]
    for first, heads, factor in ((0, grad_queries, HD ** (-0.5)), (KEY_AT, grad_keys, 1.0)):
        for head in range(heads.shape[0]):
            at = first + head * HD
            top, bottom = turn_head(heads[head], cos, sin, back=True)
            back[at : at + HD // 2, :] = (top * factor).astype(BF16)
            back[at + HD // 2 : at + HD, :] = (bottom * factor).astype(BF16)
    back[VALUE_AT:, :] = grad_values[...].astype(BF16).reshape(KV * HD, back.shape[1])
    low = back[...]
    grad = jnp.concatenate([tn(low, weight[0]), tn(low, weight[1])], axis=1)
    inputs, inv = state[...], scale[...]
    gain_part = jnp.sum(grad * inputs * inv, axis=0, keepdims=True)
    upstream = grad * gain[...]
    inner = jnp.sum(upstream * inputs, axis=-1, keepdims=True) * (1.0 / model)
    return gain_part, grad_state[...] + inv * upstream - inputs * (inv * inv * inv) * inner


def qkv_back_kernel(
    model, grad_queries, grad_keys, grad_values, state, scale, grad_state, gain, weight, cosine, sine,
    grad_input, gain_term, back,
):
    gain_part, grad = qkv_back_rows(
        model, grad_queries, grad_keys, grad_values, state, scale, grad_state, gain, weight, cosine,
        sine, back,
    )
    grad_input[...] = grad

    @pl.when(pl.program_id(0) == 0)
    def _():
        gain_term[...] = jnp.zeros(gain_term.shape, F32)

    gain_term[...] += gain_part


def qkv_back_call(
    model, grad_queries, grad_keys, grad_values, state, scale, grad_state, gain, weight, cosine,
    sine, rows=256,
):
    tokens = state.shape[0]
    by_row = lambda width: pl.BlockSpec((rows, width), lambda i: (i, 0))
    heads = lambda count: pl.BlockSpec((count, HD, rows), lambda i: (0, 0, i))
    by_lane = lambda count: pl.BlockSpec((count, rows), lambda i: (0, i))
    return pl.pallas_call(
        functools.partial(qkv_back_kernel, model),
        grid=(tokens // rows,),
        in_specs=[
            heads(H), heads(KV), heads(KV), by_row(WIDE), by_row(1), by_row(WIDE), whole(1, WIDE),
            whole(2, QKV, HALF), by_lane(HD // 2), by_lane(HD // 2),
        ],
        out_specs=[by_row(WIDE), whole(1, WIDE), by_lane(QKV)],
        out_shape=[
            jax.ShapeDtypeStruct((tokens, WIDE), F32),
            jax.ShapeDtypeStruct((1, WIDE), F32),
            jax.ShapeDtypeStruct((QKV, tokens), BF16),
        ],
        compiler_params=compiler(),
        cost_estimate=cost(2 * tokens * WIDE * QKV, 30e6),
        name="qkv_back",
    )(
        grad_queries, grad_keys, grad_values, state, scale, grad_state, gain, weight, cosine, sine
    )


def spread_rows(model, sizes, sorter, rows, z):
    counts = [4 * size for size in sizes]
    gap = HALF - model // 2
    firsts = [
        z * counts[0], KEY_AT + z * counts[1], VALUE_AT + z * counts[2],
        QKV + z * counts[3] + (gap if z >= 2 else 0),
    ]
    part = jnp.concatenate([rows[firsts[i] : firsts[i] + counts[i], :] for i in range(4)], axis=0)
    return tn(sorter[...], part)


def term_rows_of(model, back, normed, low, mixed, rows):
    rows[:QKV, :] = nn(back, normed).astype(BF16)
    size = model // 2
    product = nn(mixed, low)
    blank = jnp.zeros((HALF - size, HALF), F32)
    for pair in range(2):
        part = product[:, pair * HALF : (pair + 1) * HALF]
        turned = jnp.concatenate([part, blank], axis=0).T
        rows[QKV + pair * HALF : QKV + (pair + 1) * HALF, :] = turned.astype(BF16)


def attn_terms_kernel(model, sizes, back, normed, grad_state, mixed, sorter, term, rows):
    low = grad_state[...].astype(BF16)
    size = model // 2
    heads = mixed[...].reshape(H * HD, low.shape[0])
    for half in range(2):
        term_rows_of(
            model, back[...], normed[:, half * HALF : (half + 1) * HALF], low,
            heads[half * size : (half + 1) * size], rows,
        )
        for z in range(4):
            value = spread_rows(model, sizes, sorter, rows, z)
            term[half, z] = value.astype(BF16).reshape(2, 2, PIECE, HALF)


def attn_terms_call(model, sizes, back, normed, grad_state, mixed, sorter):
    tokens = normed.shape[0]
    return pl.pallas_call(
        functools.partial(attn_terms_kernel, model, sizes),
        out_shape=jax.ShapeDtypeStruct((2, 4, 2, 2, PIECE, HALF), BF16),
        scratch_shapes=[pltpu.VMEM((QKV + WIDE, HALF), BF16)],
        compiler_params=compiler(),
        cost_estimate=cost(2 * tokens * WIDE * (QKV + WIDE), 30e6),
        name="attn_terms",
    )(back, normed, grad_state, mixed, sorter)


MAIN_FLOWS = tuple(
    (((0, 48), first), ((48, 80), second), ((80, 96), third))
    for first, second, third in (("yxz", "xyz", "zxy"), ("xyz", "yxz", "zyx")) * 3
)[:CHUNKS]
LAST_ROWS = 80
LAST_FLOWS = ((((0, 32), "xyz"), ((32, 64), "yxz"), ((64, 80), "zxy")),) * 2

FEED_STAGES = {
    0: ((0, 0),),
    1: ((0, 1), (0, 2), (1, 0)),
    2: ((1, 1), (2, 0)),
    3: ((0, 3), (1, 2), (2, 1), (3, 0)),
    4: ((3, 1), (4, 0)),
}
OUT_STAGES = {1: ((0, 4), (1, 3), (2, 2), (4, 1))}
ATTEND_STAGES = {
    1: ((0, 5), (1, 4), (2, 3), (3, 2)),
    3: ((1, 5), (2, 4), (3, 3), (4, 2)),
}
QKV_STAGES = {0: ((2, 5), (3, 4), (4, 3)), 2: ((3, 5), (4, 4))}
TERM_STAGES = {3: ((4, 5),)}


def finish_kernel(
    model, sizes, low_one, low_two, normed_one, normed_two, down_one, down_two, gate_one, gate_two,
    up_one, up_two, grad_state, out_weight, queries, keys, values, log_sum, state, scale, gain, qkv_weight,
    cosine, sine, sorter, normed, mixed, before,
    sums, mine, got, gain_term, term_out, back, low_out, grad_queries, grad_keys, grad_values,
    grad_mixed, packed, term_rows, made, swap_sem, *scratch,
):
    me = Place()
    swap = remote(packed, got, swap_sem.at[0], swap_sem.at[1], me.partners("y")[0][1])
    scatter = Scatter(
        me, MAIN_FLOWS, [(made.at[i % 2], 0) for i in range(CHUNKS)], sums, scratch
    )
    tokens = grad_state.shape[0]
    rows = tokens // 4
    greet(me.everyone())

    def run_stages(points, step):
        for at, stages in points.items():

            def act(stages=stages):
                for t, stage in stages:
                    scatter.stage(t, stage)

            pl.when(step == at)(act)

    def feed_terms(lows, normeds, load_sem):
        loads = [
            pltpu.make_async_copy(source, target, load_sem.at[i])
            for i, (source, target) in enumerate(
                (
                    (low_one, lows.at[0]), (low_two, lows.at[1]),
                    (normed_one, normeds.at[0]), (normed_two, normeds.at[1]),
                )
            )
        ]
        for load in loads:
            load.start()
        for load in loads:
            load.wait()

        def term_body(by_gate, by_gate_two, by_up, by_up_two, by_hidden, by_hidden_two):
            slot = made.at[lax.rem(pl.program_id(0), 2)]
            for t, (one, two, right) in enumerate(
                (
                    (by_gate, by_gate_two, normeds),
                    (by_up, by_up_two, normeds),
                    (by_hidden, by_hidden_two, lows),
                )
            ):
                for half in range(2):
                    lanes = pl.ds(half * HALF, HALF)
                    value = tn(one[...], right[0, :, lanes]) + tn(two[...], right[1, :, lanes])
                    slot.at[half, :, :, :, pl.ds(t * ROWS, ROWS), :][...] = value.astype(
                        BF16
                    ).reshape(4, 2, 2, ROWS, HALF)
            run_stages(FEED_STAGES, pl.program_id(0))

        by_unit = pl.BlockSpec((tokens, UNITS), lambda i: (0, i))
        pltpu.emit_pipeline(term_body, grid=(CHUNKS,), in_specs=[by_unit] * 6, out_specs=[])(
            gate_one, gate_two, up_one, up_two, down_one, down_two
        )

    pl.run_scoped(
        feed_terms,
        pltpu.VMEM((2, tokens, WIDE), BF16),
        pltpu.VMEM((2, tokens, WIDE), BF16),
        pltpu.SemaphoreType.DMA((4,)),
    )

    def out_body(grad, target, low):
        low[...] = grad[...].astype(BF16)
        out_back_rows(low[...], out_weight, target)
        run_stages(OUT_STAGES, pl.program_id(0))

    pltpu.emit_pipeline(
        out_body,
        grid=(2,),
        in_specs=[pl.BlockSpec((2 * rows, WIDE), lambda i: (i, 0))],
        out_specs=[
            pl.BlockSpec((H, HD, 2 * rows), lambda i: (0, 0, i)),
            pl.BlockSpec((2 * rows, WIDE), lambda i: (i, 0)),
        ],
    )(grad_state, grad_mixed, low_out)

    def attend_body(query, key, value, logs, grad, by_query, by_key, by_value):
        attend_back_kernel(rows, query, key, value, logs, grad, by_query, by_key, by_value)
        run_stages(ATTEND_STAGES, pl.program_id(0))

    heads = lambda count: pl.BlockSpec((count, HD, tokens), lambda i: (i, 0, 0))
    pltpu.emit_pipeline(
        attend_body,
        grid=(KV,),
        in_specs=[
            heads(GROUP), heads(1), heads(1),
            pl.BlockSpec((GROUP, 1, tokens), lambda i: (i, 0, 0)), heads(GROUP),
        ],
        out_specs=[heads(GROUP), heads(1), heads(1)],
    )(queries, keys, values, log_sum, grad_mixed, grad_queries, grad_keys, grad_values)

    gain_term[...] = jnp.zeros(gain_term.shape, F32)

    size = model // 2

    def qkv_body(by_query, by_key, by_value, inputs, inv, grad, cos, sin, by_input, low):
        gain_part, value = qkv_back_rows(
            model, by_query, by_key, by_value, inputs, inv, grad, gain, qkv_weight, cos, sin, low
        )
        gain_term[...] += gain_part
        step = pl.program_id(0)
        for count in range(2):

            @pl.when(step == count)
            def _(count=count):
                for half in range(2):
                    packed[
                        half * size : (half + 1) * size, count * rows : (count + 1) * rows
                    ] = narrow(value, half, model).astype(BF16)

        @pl.when(step == 1)
        def _():
            swap.start()

        @pl.when(step >= 2)
        def _():
            for half in range(2):
                by_input[half * size : (half + 1) * size, :] = narrow(value, half, model)

        run_stages(QKV_STAGES, step)

    order = lambda i: lax.rem(i + 2 * (1 - me.y), 4)
    by_row = lambda width: pl.BlockSpec((rows, width), lambda i: (order(i), 0))
    some = lambda count: pl.BlockSpec((count, HD, rows), lambda i: (0, 0, order(i)))
    by_lane = lambda count: pl.BlockSpec((count, rows), lambda i: (0, order(i)))
    pltpu.emit_pipeline(
        qkv_body,
        grid=(4,),
        in_specs=[
            some(H), some(KV), some(KV), by_row(WIDE), by_row(1), by_row(WIDE),
            by_lane(HD // 2), by_lane(HD // 2),
        ],
        out_specs=[
            pl.BlockSpec((model, rows), lambda i: (0, jnp.maximum(i - 2, 0))), by_lane(QKV),
        ],
    )(grad_queries, grad_keys, grad_values, state, scale, grad_state, cosine, sine, mine, back)

    def term_body(low, by_normed, grad, by_mixed, earlier, term):
        z = pl.program_id(1)

        @pl.when(z == 0)
        def _():
            heads_half = by_mixed[...]
            term_rows_of(model, low[...], by_normed[...], grad[...], heads_half, term_rows)

        for at in range(4):

            @pl.when(z == at)
            def _(at=at):
                value = spread_rows(model, sizes, sorter, term_rows, at)
                value = value + earlier[0, 0].reshape(4 * PIECE, HALF).astype(F32)
                term[0, 0] = value.astype(BF16).reshape(2, 2, PIECE, HALF)

        run_stages(TERM_STAGES, 4 * pl.program_id(0) + z)

    fixed = lambda width: pl.BlockSpec((tokens, width), lambda i, z: (0, 0))
    by_half = pl.BlockSpec((tokens, HALF), lambda i, z: (0, i))
    piece = pl.BlockSpec((1, 1, 2, 2, PIECE, HALF), lambda i, z: (i, z, 0, 0, 0, 0))
    pltpu.emit_pipeline(
        term_body,
        grid=(2, 4),
        in_specs=[
            pl.BlockSpec((QKV, tokens), lambda i, z: (0, 0)), by_half, fixed(WIDE),
            pl.BlockSpec((size, tokens), lambda i, z: (i, 0)), piece,
        ],
        out_specs=[piece],
    )(back, normed, low_out, mixed, before, term_out)
    swap.wait()


def finish_call(
    model, sizes, operands, grad_state, out_weight, queries, keys, values, log_sum, state, scale, gain,
    qkv_weight, cosine, sine, sorter, normed, mixed, before,
):
    tokens = grad_state.shape[0]
    anywhere = pl.BlockSpec(memory_space=pl.ANY)
    inside = pl.BlockSpec(memory_space=pltpu.VMEM)
    outs = [
        ((CHUNKS, 3 * ROWS, HALF), F32, inside),
        ((model, tokens // 2), F32, anywhere),
        ((model, tokens // 2), BF16, anywhere),
        ((1, WIDE), F32, inside),
        ((2, 4, 2, 2, PIECE, HALF), BF16, anywhere),
        ((QKV, tokens), BF16, anywhere),
        ((tokens, WIDE), BF16, anywhere),
        ((H, HD, tokens), F32, anywhere),
        ((KV, HD, tokens), F32, anywhere),
        ((KV, HD, tokens), F32, anywhere),
        ((H, HD, tokens), BF16, anywhere),
    ]
    return pl.pallas_call(
        functools.partial(finish_kernel, model, sizes),
        out_shape=[jax.ShapeDtypeStruct(shape, kind) for shape, kind, _ in outs],
        in_specs=[anywhere] * 11 + [inside] + [anywhere] * 6 + [inside] * 2 + [anywhere] * 2
        + [inside] + [anywhere] * 3,
        out_specs=[where for *_, where in outs],
        scratch_shapes=[
            pltpu.VMEM((model, tokens // 2), BF16),
            pltpu.VMEM((QKV + WIDE, HALF), BF16),
            pltpu.VMEM((2, 2, 4, 2, 2, 3 * ROWS, HALF), BF16),
            pltpu.SemaphoreType.DMA((2,)),
        ]
        + Scatter.scratch(MAIN_FLOWS, 3 * ROWS),
        compiler_params=compiler(collective_id=1, has_side_effects=True),
        name="finish",
    )(
        *operands, grad_state, out_weight, queries, keys, values, log_sum, state, scale, gain,
        qkv_weight, cosine, sine, sorter, normed, mixed, before,
    )[:5]


def last_kernel(term, gains, sums, gains_out, gain_own, gain_get, gain_send, gain_recv, *scratch):
    me = Place()
    y, z = me.y, me.z
    z_one = (me.w + 4 - 8 * (z % 2), y)
    z_two = (me.w + 8 - 16 * (z // 2), y)
    types = len(LAST_FLOWS)
    scatter = Scatter(me, LAST_FLOWS, [(term, t * LAST_ROWS) for t in range(types)], sums, scratch)
    ticks = staggered(types, STEPS + 3)
    gain_own[0] = gains[...]
    greet(me.everyone())

    def tick(count):
        for t, stage in ticks[count]:
            scatter.stage(t, stage)

    tick(0)
    partners = (me.sibling, me.partners("y")[0][1], me.partners("x")[0][1], z_one, z_two)

    def gain_copy(step):
        return remote(
            gain_own.at[step], gain_get.at[step], gain_send.at[step], gain_recv.at[step],
            partners[step],
        )

    gain_copy(0).start()
    for step in range(5):
        tick(1 + step)
        gain_copy(step).wait()
        if step < 4:
            gain_own[step + 1] = gain_own[step] + gain_get[step]
            gain_copy(step + 1).start()
        else:
            gains_out[...] = gain_own[step] + gain_get[step]
    for count in range(6, len(ticks)):
        tick(count)


def last_call(term, gains):
    dma = pltpu.SemaphoreType.DMA
    inside = pl.BlockSpec(memory_space=pltpu.VMEM)
    return pl.pallas_call(
        last_kernel,
        out_shape=[
            jax.ShapeDtypeStruct((len(LAST_FLOWS), LAST_ROWS, HALF), F32),
            jax.ShapeDtypeStruct(gains.shape, F32),
        ],
        in_specs=[pl.BlockSpec(memory_space=pl.ANY), inside],
        out_specs=[inside, inside],
        scratch_shapes=[
            pltpu.VMEM((5,) + gains.shape, F32),
            pltpu.VMEM((5,) + gains.shape, F32),
            dma((5,)),
            dma((5,)),
        ]
        + Scatter.scratch(LAST_FLOWS, LAST_ROWS),
        compiler_params=compiler(collective_id=2, has_side_effects=True),
        name="last",
    )(term, gains)


def halves(array, model):
    pad = [(0, 0)] * (array.ndim - 1)
    left, right = array[..., : model // 2], array[..., model // 2 :]
    pad = pad + [(0, HALF - model // 2)]
    return jnp.concatenate([jnp.pad(left, pad), jnp.pad(right, pad)], axis=-1)


def joined(array, model):
    return jnp.concatenate([array[..., : model // 2], array[..., HALF : HALF + model // 2]], axis=-1)


def rotary(count):
    positions = np.arange(count, dtype=np.float32)
    exponent = np.arange(HD // 2, dtype=np.float32) * np.float32(2.0 / HD)
    frequency = np.power(np.float32(10000.0), -exponent).astype(np.float32)
    angles = positions[:, None] * frequency[None, :]
    cosine, sine = np.cos(angles), np.sin(angles)
    return jnp.asarray(cosine.T, F32), jnp.asarray(sine.T, F32)


def on_device_whole(
    block_input, cotangent, attn_gain, ffn_gain,
    query_weight, key_weight, value_weight, out_weight, gate_weight, up_weight, down_weight,
):
    _, half_rows, model = block_input.shape
    tokens = 2 * half_rows
    y = lax.axis_index("narrow")
    flip = [(0, 1), (1, 0)]
    pieces = (query_weight, key_weight, value_weight, out_weight)
    sizes = tuple(piece.shape[1] for piece in pieces)
    starts = [sum(sizes[:i]) for i in range(5)]
    fill = lambda array: jnp.pad(
        array, [(0, 0)] * (array.ndim - 1) + [(0, HALF - array.shape[-1])]
    )
    own = fill(jnp.concatenate([piece.T for piece in pieces], axis=0))
    feed_own = fill(
        jnp.stack(
            [piece.T.reshape(CHUNKS, ROWS, -1) for piece in (gate_weight, up_weight, down_weight)],
            axis=1,
        ).reshape(CHUNKS, 3 * ROWS, -1)
    )
    gain_a = halves(attn_gain[None, :], model)
    gain_f = halves(ffn_gain[None, :], model)
    cosine, sine = rotary(tokens)
    sorter = jnp.asarray(sorter_matrix(sizes), BF16)
    (
        _, weights, output, gate, up, qkv_weight, full_out, state, normed_a, scale_a, queries, keys,
        values, log_sum, hidden_state, mixed, normed_f, scale_f,
    ) = start_call(
        model, sizes, own, feed_own, block_input.swapaxes(1, 2), gain_a, gain_f, cosine, sine, sorter
    )
    first_kept = (
        state, normed_a, scale_a, queries, keys, values, log_sum, hidden_state, mixed,
        normed_f, scale_f, gate, up,
    )

    def pick(array, index):
        return lax.dynamic_index_in_dim(array, index, 0, keepdims=False)

    state, cotangent = lax.optimization_barrier((output, cotangent))
    cotangent = cotangent.swapaxes(1, 2)
    grad_other = lax.ppermute(pick(cotangent, 1 - y), "narrow", flip)
    normed_a, scale_a, queries, keys, values = qkv_call(
        model, state, gain_a, qkv_weight, cosine, sine
    )
    mixed, log_sum = attend_call(queries, keys, values)
    final, hidden_state, normed_f, scale_f, gate, up = feed_call(
        model, state, mixed, full_out, gain_f, weights
    )
    final_got = lax.ppermute(pick(final, 1 - y), "narrow", flip)

    grad_state, gain_f_two, *feed_two = feed_back_call(
        model, (pick(cotangent, y), grad_other), hidden_state, gain_f, scale_f, gate, up, weights
    )
    feed_two = (feed_two[0], normed_f, feed_two[3], feed_two[1], feed_two[2])
    grad_mixed = out_back_call(grad_state, full_out)
    grad_queries, grad_keys, grad_values = attend_back_call(
        queries, keys, values, log_sum, grad_mixed
    )
    grad, gain_a_two, back = qkv_back_call(
        model, grad_queries, grad_keys, grad_values, state, scale_a, grad_state, gain_a, qkv_weight,
        cosine, sine,
    )
    attn_term = attn_terms_call(model, sizes, back, normed_a, grad_state, mixed, sorter)

    (
        state, normed_a, scale_a, queries, keys, values, log_sum, hidden_state, mixed,
        normed_f, scale_f, gate, up,
    ) = first_kept
    grad_state, gain_f_one, *feed_one = feed_back_call(
        model, (grad,), hidden_state, gain_f, scale_f, gate, up, weights
    )
    feed_one = (feed_one[0], normed_f, feed_one[3], feed_one[1], feed_one[2])
    operands = [array for pair in zip(feed_one, feed_two) for array in pair]
    feed_sums, grad_mine, grad_got, gain_a_one, attn_term = finish_call(
        model, sizes, operands, grad_state, full_out, queries, keys, values, log_sum, state, scale_a,
        gain_a, qkv_weight, cosine, sine, sorter, normed_a, mixed.reshape(H * HD, tokens), attn_term,
    )
    gains = jnp.concatenate([gain_a_one + gain_a_two, gain_f_one + gain_f_two], axis=0)
    attn_sums, gains = last_call(attn_term, gains)

    def placed(mine, theirs):
        theirs = theirs.astype(mine.dtype)
        return jnp.where(y == 0, jnp.stack([mine, theirs]), jnp.stack([theirs, mine])).swapaxes(1, 2)

    block_output = placed(pick(final, y), final_got)
    input_grad = placed(grad_mine, grad_got)
    gains = joined(gains, model)
    feed_sums = feed_sums[:, :, : model // 2].reshape(CHUNKS, 3, ROWS, -1)
    feed_sums = [feed_sums[:, t].reshape(PIECE, -1).T for t in range(3)]
    attn_sums = attn_sums.reshape(PIECE, HALF)
    attn_sums = [attn_sums[starts[i] : starts[i + 1], : model // 2].T for i in range(4)]
    return (
        block_output, input_grad, gains[0], gains[1], *attn_sums,
        *feed_sums,
    )


def rms_scale(values):
    return lax.rsqrt(jnp.mean(values * values, axis=-1, keepdims=True) + 1e-05)


def rotary_tables(count, first_row):
    positions = (first_row + jnp.arange(count, dtype=jnp.int32)).astype(jnp.float32)
    exponent = jnp.arange(HD // 2, dtype=jnp.int32).astype(jnp.float32) * (2.0 / HD)
    frequency = 10000.0 ** (-exponent)
    angles = positions[:, None] * frequency[None, :]
    return (jnp.cos(angles), jnp.sin(angles))


def rotate(values, cosine, sine_table):
    half_size = values.shape[-1] // 2
    first_half = values[..., :half_size]
    second_half = values[..., half_size:]
    return jnp.concatenate(
        [
            first_half * cosine - second_half * sine_table,
            second_half * cosine + first_half * sine_table,
        ],
        axis=-1,
    )


def rotate_back(values, cosine, sine_table):
    half_size = values.shape[-1] // 2
    first_half = values[..., :half_size]
    second_half = values[..., half_size:]
    return jnp.concatenate(
        [
            first_half * cosine + second_half * sine_table,
            second_half * cosine - first_half * sine_table,
        ],
        axis=-1,
    )


def contract_last(left, right):
    return lax.dot_general(
        left, right, (((1,), (1,)), ((), ())), preferred_element_type=jnp.float32
    )


def norm_back(upstream, values, inv_rms, norm_gain):
    gain_grad = jnp.sum(upstream * values * inv_rms, axis=0)
    scaled_up = upstream * norm_gain
    inner_mean = jnp.mean(scaled_up * values, axis=-1, keepdims=True)
    return (gain_grad, inv_rms * scaled_up - values * (inv_rms * inv_rms * inv_rms) * inner_mean)


def fetch_weights(
    query_weight, key_weight, value_weight, out_weight, gate_weight, up_weight, down_weight
):
    columns = (
        lax.all_gather(query_weight, "wide", axis=1, tiled=True),
        lax.all_gather(key_weight, "wide", axis=1, tiled=True),
        lax.all_gather(value_weight, "wide", axis=1, tiled=True),
        lax.all_gather(out_weight, "wide", axis=1, tiled=True),
        lax.all_gather(gate_weight, "wide", axis=1, tiled=True),
        lax.all_gather(up_weight, "wide", axis=1, tiled=True),
        lax.all_gather(down_weight, "wide", axis=1, tiled=True),
    )
    return (
        lax.all_gather(columns[0], "narrow", axis=0, tiled=True),
        lax.all_gather(columns[1], "narrow", axis=0, tiled=True),
        lax.all_gather(columns[2], "narrow", axis=0, tiled=True),
        lax.all_gather(columns[3], "narrow", axis=0, tiled=True),
        lax.all_gather(columns[4], "narrow", axis=0, tiled=True),
        lax.all_gather(columns[5], "narrow", axis=0, tiled=True),
        lax.all_gather(columns[6], "narrow", axis=0, tiled=True),
    )


def forward_run(run_input, attn_gain, ffn_gain, weights, cosine, sine_table, first_row):
    query_weight, key_weight, value_weight, out_weight, gate_weight, up_weight, down_weight = (
        weights
    )
    row_count = run_input.shape[0]
    groups = H // KV
    attn_scale = rms_scale(run_input)
    normed_attn = (run_input * attn_scale * attn_gain).astype(jnp.bfloat16)
    query_pre = jnp.dot(normed_attn, query_weight, preferred_element_type=jnp.float32).reshape(
        row_count, KV, groups, HD
    )
    queries = rotate(query_pre, cosine[:, None, None, :], sine_table[:, None, None, :]).astype(
        jnp.bfloat16
    )
    key_pre = jnp.dot(normed_attn, key_weight, preferred_element_type=jnp.float32).reshape(
        row_count, KV, HD
    )
    keys_local = (
        rotate(key_pre, cosine[:, None, :], sine_table[:, None, :])
        .astype(jnp.bfloat16)
        .reshape(row_count, KV * HD)
    )
    values_local = jnp.dot(normed_attn, value_weight, preferred_element_type=jnp.float32).astype(
        jnp.bfloat16
    )
    keys_all, values_all = (
        lax.all_gather(keys_local, "narrow", axis=0, tiled=True),
        lax.all_gather(values_local, "narrow", axis=0, tiled=True),
    )
    length = keys_all.shape[0]
    keys_all = keys_all.reshape(length, KV, HD)
    values_all = values_all.reshape(length, KV, HD)
    attn_score = jnp.einsum(
        "rgjd,pgd->gjrp", queries, keys_all, preferred_element_type=jnp.float32
    ) * HD ** (-0.5)
    visible = (first_row + jnp.arange(row_count, dtype=jnp.int32))[:, None] >= jnp.arange(
        length, dtype=jnp.int32
    )[None, :]
    attn_score = jnp.where(visible, attn_score, -jnp.inf)
    row_peak = jnp.max(attn_score, axis=-1, keepdims=True)
    weight_exp = jnp.exp(attn_score - row_peak)
    attn_probs = weight_exp / jnp.sum(weight_exp, axis=-1, keepdims=True)
    probs_low = attn_probs.astype(jnp.bfloat16)
    mixed_heads = jnp.einsum(
        "gjrp,pgd->rgjd", probs_low, values_all, preferred_element_type=jnp.float32
    ).reshape(row_count, H * HD)
    mixed_low = mixed_heads.astype(jnp.bfloat16)
    hidden_state = run_input + jnp.dot(mixed_low, out_weight, preferred_element_type=jnp.float32)
    ffn_scale = rms_scale(hidden_state)
    normed_ffn = (hidden_state * ffn_scale * ffn_gain).astype(jnp.bfloat16)
    gate_proj = jnp.dot(normed_ffn, gate_weight, preferred_element_type=jnp.float32)
    up_proj = jnp.dot(normed_ffn, up_weight, preferred_element_type=jnp.float32)
    hidden = (gate_proj / (1.0 + jnp.exp(-gate_proj)) * up_proj).astype(jnp.bfloat16)
    run_output = hidden_state + contract_last(hidden, down_weight)
    saved_parts = (
        attn_scale,
        normed_attn,
        queries,
        keys_all,
        values_all,
        attn_probs,
        probs_low,
        mixed_low,
        hidden_state,
        ffn_scale,
        normed_ffn,
        gate_proj,
        up_proj,
        hidden,
    )
    return (run_output, saved_parts)


def backward_run(
    grad_out, run_input, saved_parts, attn_gain, ffn_gain, weights, cosine, sine_table
):
    query_weight, key_weight, value_weight, out_weight, gate_weight, up_weight, down_weight = (
        weights
    )
    (
        attn_scale,
        normed_attn,
        queries,
        keys_all,
        values_all,
        attn_probs,
        probs_low,
        mixed_low,
        hidden_state,
        ffn_scale,
        normed_ffn,
        gate_proj,
        up_proj,
        hidden,
    ) = saved_parts
    row_count = run_input.shape[0]
    length = keys_all.shape[0]
    groups = H // KV
    grad_low = grad_out.astype(jnp.bfloat16)
    down_term = jnp.einsum("td,tf->df", grad_low, hidden, preferred_element_type=jnp.float32)
    grad_hidden = jnp.dot(grad_low, down_weight, preferred_element_type=jnp.float32)
    sigmoid_gate = 1.0 / (1.0 + jnp.exp(-gate_proj))
    grad_gate = (
        grad_hidden * up_proj * sigmoid_gate * (1.0 + gate_proj * (1.0 - sigmoid_gate))
    ).astype(jnp.bfloat16)
    grad_up = (grad_hidden * gate_proj * sigmoid_gate).astype(jnp.bfloat16)
    gate_term = jnp.einsum("td,tf->df", normed_ffn, grad_gate, preferred_element_type=jnp.float32)
    up_term = jnp.einsum("td,tf->df", normed_ffn, grad_up, preferred_element_type=jnp.float32)
    grad_normed_ffn = contract_last(grad_gate, gate_weight) + contract_last(grad_up, up_weight)
    ffn_gain_term, grad_through = norm_back(grad_normed_ffn, hidden_state, ffn_scale, ffn_gain)
    grad_state = grad_out + grad_through
    branch_low = grad_state.astype(jnp.bfloat16)
    out_term = jnp.einsum("tc,td->cd", mixed_low, branch_low, preferred_element_type=jnp.float32)
    grad_mixed = (
        contract_last(branch_low, out_weight)
        .astype(jnp.bfloat16)
        .reshape(row_count, KV, groups, HD)
    )
    grad_probs = jnp.einsum(
        "rgjd,pgd->gjrp", grad_mixed, values_all, preferred_element_type=jnp.float32
    )
    row_delta = jnp.sum(attn_probs * grad_probs, axis=-1, keepdims=True)
    grad_score = (attn_probs * (grad_probs - row_delta)).astype(jnp.bfloat16)
    grad_queries = jnp.einsum(
        "gjrp,pgd->rgjd", grad_score, keys_all, preferred_element_type=jnp.float32
    ) * HD ** (-0.5)
    grad_keys = jnp.einsum(
        "gjrp,rgjd->pgd", grad_score, queries, preferred_element_type=jnp.float32
    ) * HD ** (-0.5)
    grad_values = jnp.einsum(
        "gjrp,rgjd->pgd", probs_low, grad_mixed, preferred_element_type=jnp.float32
    )
    key_grads, value_grads = (
        lax.psum_scatter(
            grad_keys.reshape(length, KV * HD).astype(jnp.bfloat16),
            "narrow",
            scatter_dimension=0,
            tiled=True,
        ).astype(jnp.float32),
        lax.psum_scatter(
            grad_values.reshape(length, KV * HD).astype(jnp.bfloat16),
            "narrow",
            scatter_dimension=0,
            tiled=True,
        ).astype(jnp.float32),
    )
    query_back = (
        rotate_back(grad_queries, cosine[:, None, None, :], sine_table[:, None, None, :])
        .reshape(row_count, H * HD)
        .astype(jnp.bfloat16)
    )
    key_back = (
        rotate_back(
            key_grads.reshape(row_count, KV, HD), cosine[:, None, :], sine_table[:, None, :]
        )
        .reshape(row_count, KV * HD)
        .astype(jnp.bfloat16)
    )
    value_back = value_grads.astype(jnp.bfloat16)
    query_term = jnp.einsum(
        "td,tc->dc", normed_attn, query_back, preferred_element_type=jnp.float32
    )
    key_term = jnp.einsum("td,tc->dc", normed_attn, key_back, preferred_element_type=jnp.float32)
    value_term = jnp.einsum(
        "td,tc->dc", normed_attn, value_back, preferred_element_type=jnp.float32
    )
    grad_normed_attn = (
        contract_last(query_back, query_weight)
        + contract_last(key_back, key_weight)
        + contract_last(value_back, value_weight)
    )
    attn_gain_term, grad_norm_input = norm_back(grad_normed_attn, run_input, attn_scale, attn_gain)
    grad_input = grad_state + grad_norm_input
    return (
        grad_input,
        (attn_gain_term, ffn_gain_term),
        (query_term, key_term, value_term, out_term, gate_term, up_term, down_term),
    )


def on_device_parts(
    block_input,
    cotangent,
    attn_gain,
    ffn_gain,
    query_weight,
    key_weight,
    value_weight,
    out_weight,
    gate_weight,
    up_weight,
    down_weight,
):
    seq_count = block_input.shape[0]
    row_count = block_input.shape[1]
    first_row = lax.axis_index("narrow") * row_count
    cosine, sine_table = rotary_tables(row_count, first_row)

    def current():
        return fetch_weights(
            query_weight, key_weight, value_weight, out_weight, gate_weight, up_weight, down_weight
        )

    start_states = [block_input[item].astype(jnp.float32) for item in range(seq_count)]
    weights_now = current()
    middle_states = [
        forward_run(state, attn_gain, ffn_gain, weights_now, cosine, sine_table, first_row)[0]
        for state in start_states
    ]
    weights_now = current()
    final_states = [
        forward_run(state, attn_gain, ffn_gain, weights_now, cosine, sine_table, first_row)[0]
        for state in middle_states
    ]
    grad_states = [cotangent[item].astype(jnp.float32) for item in range(seq_count)]
    gain_local = None
    weight_local = None
    for run_inputs in (middle_states, start_states):
        weights_now = current()
        next_grads = []
        for item in range(seq_count):
            recomputed, saved_parts = forward_run(
                run_inputs[item], attn_gain, ffn_gain, weights_now, cosine, sine_table, first_row
            )
            grad_input, gain_parts, weight_parts = backward_run(
                grad_states[item],
                run_inputs[item],
                saved_parts,
                attn_gain,
                ffn_gain,
                weights_now,
                cosine,
                sine_table,
            )
            next_grads.append(grad_input)
            if gain_local is None:
                gain_local = gain_parts
                weight_local = weight_parts
            else:
                gain_local = jax.tree.map(jnp.add, gain_local, gain_parts)
                weight_local = jax.tree.map(jnp.add, weight_local, weight_parts)
        grad_states = next_grads
    across = (
        lax.psum_scatter(
            weight_local[0].astype(jnp.bfloat16), "wide", scatter_dimension=1, tiled=True
        ).astype(jnp.float32),
        lax.psum_scatter(
            weight_local[1].astype(jnp.bfloat16), "wide", scatter_dimension=1, tiled=True
        ).astype(jnp.float32),
        lax.psum_scatter(
            weight_local[2].astype(jnp.bfloat16), "wide", scatter_dimension=1, tiled=True
        ).astype(jnp.float32),
        lax.psum_scatter(
            weight_local[3].astype(jnp.bfloat16), "wide", scatter_dimension=1, tiled=True
        ).astype(jnp.float32),
        lax.psum_scatter(
            weight_local[4].astype(jnp.bfloat16), "wide", scatter_dimension=1, tiled=True
        ).astype(jnp.float32),
        lax.psum_scatter(
            weight_local[5].astype(jnp.bfloat16), "wide", scatter_dimension=1, tiled=True
        ).astype(jnp.float32),
        lax.psum_scatter(
            weight_local[6].astype(jnp.bfloat16), "wide", scatter_dimension=1, tiled=True
        ).astype(jnp.float32),
    )
    reduced = (
        lax.psum_scatter(
            across[0].astype(jnp.bfloat16), "narrow", scatter_dimension=0, tiled=True
        ).astype(jnp.float32),
        lax.psum_scatter(
            across[1].astype(jnp.bfloat16), "narrow", scatter_dimension=0, tiled=True
        ).astype(jnp.float32),
        lax.psum_scatter(
            across[2].astype(jnp.bfloat16), "narrow", scatter_dimension=0, tiled=True
        ).astype(jnp.float32),
        lax.psum_scatter(
            across[3].astype(jnp.bfloat16), "narrow", scatter_dimension=0, tiled=True
        ).astype(jnp.float32),
        lax.psum_scatter(
            across[4].astype(jnp.bfloat16), "narrow", scatter_dimension=0, tiled=True
        ).astype(jnp.float32),
        lax.psum_scatter(
            across[5].astype(jnp.bfloat16), "narrow", scatter_dimension=0, tiled=True
        ).astype(jnp.float32),
        lax.psum_scatter(
            across[6].astype(jnp.bfloat16), "narrow", scatter_dimension=0, tiled=True
        ).astype(jnp.float32),
    )
    gain_totals = lax.psum((gain_local[0], gain_local[1]), ("wide", "narrow"))
    block_output = jnp.stack(final_states).astype(jnp.bfloat16)
    input_grad = jnp.stack(grad_states)
    return (
        block_output,
        input_grad,
        gain_totals[0],
        gain_totals[1],
        reduced[0],
        reduced[1],
        reduced[2],
        reduced[3],
        reduced[4],
        reduced[5],
        reduced[6],
    )


def on_device(block_input, *rest):
    pieces = sum(weight.shape[1] for weight in rest[3:7])
    fits = (
        (lax.axis_size("wide"), lax.axis_size("narrow")) == (16, 2)
        and block_input.shape[0] == 2
        and block_input.shape[2] <= WIDE
        and {pieces, rest[7].shape[1], rest[8].shape[1], rest[9].shape[1]} == {PIECE}
    )
    plan = on_device_whole if fits else on_device_parts
    return plan(block_input, *rest)


def solution(mesh):
    placed = (
        P("wide", "narrow", None),
        P("wide", "narrow", None),
        P(),
        P(),
        P("narrow", "wide"),
        P("narrow", "wide"),
        P("narrow", "wide"),
        P("narrow", "wide"),
        P("narrow", "wide"),
        P("narrow", "wide"),
        P("narrow", "wide"),
    )
    return jax.shard_map(
        on_device,
        mesh=mesh,
        in_specs=placed,
        out_specs=(
            P("wide", "narrow", None),
            P("wide", "narrow", None),
            P(),
            P(),
            P("narrow", "wide"),
            P("narrow", "wide"),
            P("narrow", "wide"),
            P("narrow", "wide"),
            P("narrow", "wide"),
            P("narrow", "wide"),
            P("narrow", "wide"),
        ),
        check_vma=False,
    )
```

```python
import functools

import jax
import jax.numpy as jnp
import numpy as np
from jax import lax
from jax.experimental import pallas as pl
from jax.experimental.pallas import tpu as pltpu
from jax.sharding import PartitionSpec as P

H = 15
KV = 5
HD = 64
MESH = pl.DeviceIdType.MESH
F32 = jnp.float32
BF16 = jnp.bfloat16
GROUP = H // KV
PIECE = 160
CHUNKS = 5
ROWS = PIECE // CHUNKS
UNITS = 16 * ROWS
HALF = 512
WIDE = 2 * HALF
KEY_AT = H * HD
VALUE_AT = KEY_AT + KV * HD
QKV = VALUE_AT + KV * HD
VMEM_LIMIT = 62 << 20


def nt(left, right):
    return lax.dot_general(left, right, (((1,), (1,)), ((), ())), preferred_element_type=F32)


def nn(left, right):
    return jnp.dot(left, right, preferred_element_type=F32)


def tn(left, right):
    return lax.dot_general(left, right, (((0,), (0,)), ((), ())), preferred_element_type=F32)


def whole(*shape):
    return pl.BlockSpec(shape, lambda *_: (0,) * len(shape), pipeline_mode=pl.Buffered(1))


def compiler(**more):
    return pltpu.CompilerParams(vmem_limit_bytes=VMEM_LIMIT, **more)


def cost(flops, moved):
    return pl.CostEstimate(flops=int(flops), bytes_accessed=int(moved), transcendentals=0)


def span(ref, rows):
    return ref.at[..., pl.ds(rows[0], rows[1] - rows[0]), :]


class Place:
    def __init__(self):
        self.w = lax.axis_index("wide")
        self.y = lax.axis_index("narrow")
        self.z = self.w // 4
        self.x = (self.w // 2) % 2
        self.c = self.w % 2
        self.sibling = (self.w + 1 - 2 * self.c, self.y)

    def partners(self, dim):
        if dim == "x":
            return [(1 - self.x, (self.w + 2 - 4 * self.x, self.y))]
        if dim == "y":
            return [(1 - self.y, (self.w, 1 - self.y))]
        others = [(self.z + far) % 4 for far in (1, 2, 3)]
        return [(other, (self.w + 4 * (other - self.z), self.y)) for other in others]

    def origins(self, dim):
        if dim == "z":
            return [(self.z + far) % 4 for far in (3, 2, 1)]
        return [1 - getattr(self, dim)]

    def everyone(self):
        return [self.sibling] + [device for dim in "xyz" for _, device in self.partners(dim)]


def greet(devices):
    barrier = pltpu.get_barrier_semaphore()
    for device in devices:
        pl.semaphore_signal(barrier, inc=1, device_id=device, device_id_type=MESH)
    pl.semaphore_wait(barrier, len(devices))


def remote(source, target, send_sem, recv_sem, device):
    return pltpu.make_async_remote_copy(
        src_ref=source,
        dst_ref=target,
        send_sem=send_sem,
        recv_sem=recv_sem,
        device_id=device,
        device_id_type=MESH,
    )


STEPS = 3


class Gather:
    def __init__(self, me, flows, own, full, keep_sem, send, recv, cross_send, cross_recv):
        self.me, self.flows, self.own, self.full = me, flows, own, full
        self.keep_sem, self.send, self.recv = keep_sem, send, recv
        self.cross_send, self.cross_recv = cross_send, cross_recv

    def keep(self, t):
        me = self.me
        return pltpu.make_async_copy(
            self.own[t], self.full[t].at[me.y, me.z, me.x, me.c], self.keep_sem.at[t]
        )

    def blocks(self, t, flow, step, place):
        me = self.me
        rows, order = self.flows[t][flow]
        at = {"y": me.y, "z": me.z, "x": me.x}
        for name in order[:step]:
            at[name] = slice(None)
        at[order[step]] = place
        return span(self.full[t].at[at["y"], at["z"], at["x"], me.c], rows)

    def copies(self, t, flow, step):
        me = self.me
        rows, order = self.flows[t][flow]
        dim = order[step]
        target = self.blocks(t, flow, step, getattr(me, dim))
        source = span(self.own[t], rows) if step == 0 else target
        return [
            remote(
                source, target, self.send.at[t, flow, step, i], self.recv.at[t, flow, step, i], device
            )
            for i, (_, device) in enumerate(me.partners(dim))
        ]

    def landing(self, t, flow, step):
        me = self.me
        dim = self.flows[t][flow][1][step]
        devices = me.partners(dim)
        blocks = [self.blocks(t, flow, step, place) for place in me.origins(dim)]
        return [
            remote(
                block, block, self.send.at[t, flow, step, i], self.recv.at[t, flow, step, i],
                devices[i][1],
            )
            for i, block in enumerate(blocks)
        ]

    def cross(self, t, flow):
        blocks = span(self.full[t].at[:, :, :, self.me.c], self.flows[t][flow][0])
        return remote(
            blocks, blocks, self.cross_send.at[t, flow], self.cross_recv.at[t, flow],
            self.me.sibling,
        )

    def stage(self, t, step):
        count = len(self.flows[t])
        if step == 0:
            self.keep(t).start()
        if step == 1:
            self.keep(t).wait()
        for flow in range(count):
            if 0 < step <= STEPS:
                for copy in self.landing(t, flow, step - 1):
                    copy.wait_recv()
            if step < STEPS:
                for copy in self.copies(t, flow, step):
                    copy.start()
            if step == STEPS:
                self.cross(t, flow).start()
            if step == STEPS + 1:
                self.cross(t, flow).wait()
                for before in range(STEPS):
                    for copy in self.copies(t, flow, before):
                        copy.wait_send()

    @staticmethod
    def semaphores(types, flows):
        dma = pltpu.SemaphoreType.DMA
        return [
            dma((types,)), dma((types, flows, STEPS, 3)), dma((types, flows, STEPS, 3)),
            dma((types, flows)), dma((types, flows)),
        ]


class Scatter:
    def __init__(self, me, flows, terms, out, scratch):
        self.me, self.flows, self.terms, self.out = me, flows, terms, out
        (
            self.acc, self.arrived, self.load_sem, self.cross_send, self.cross_recv, self.send,
            self.recv, *self.buffers,
        ) = scratch
        self.piece = self.acc.shape[-2]

    @staticmethod
    def scratch(flows, piece):
        dma = pltpu.SemaphoreType.DMA
        types, count = len(flows), len(flows[0])
        refs = [
            pltpu.VMEM((types, 2, 4, 2, piece, HALF), BF16),
            pltpu.VMEM((types, 2, 4, 2, piece, HALF), BF16),
            dma((types,)), dma((types,)), dma((types,)),
            dma((types, count, STEPS, 3)), dma((types, count, STEPS, 3)),
        ]
        for own_flows in flows:
            for rows, order in own_flows:
                for step, dim in enumerate(order):
                    left = order[step + 1 :]
                    shape = tuple({"y": 2, "z": 4, "x": 2}[name] for name in "yzx" if name in left)
                    lines = (3 if dim == "z" else 1,)
                    refs.append(pltpu.VMEM(lines + shape + (rows[1] - rows[0], HALF), BF16))
        return refs

    def buffer(self, t, flow, step):
        return self.buffers[(t * len(self.flows[0]) + flow) * STEPS + step]

    def source(self, t, core):
        ref, first = self.terms[t]
        return span(ref.at[:, :, :, core], (first, first + self.piece))

    def cross(self, t):
        return remote(
            self.source(t, 1 - self.me.c), self.arrived.at[t], self.cross_send.at[t],
            self.cross_recv.at[t], self.me.sibling,
        )

    def load(self, t):
        return pltpu.make_async_copy(
            self.source(t, self.me.c), self.acc.at[t], self.load_sem.at[t]
        )

    def blocks(self, t, flow, step, place):
        rows, order = self.flows[t][flow]
        at = {"y": slice(None), "z": slice(None), "x": slice(None)}
        for name in order[:step]:
            at[name] = getattr(self.me, name)
        at[order[step]] = place
        return span(self.acc.at[t, at["y"], at["z"], at["x"]], rows)

    def copies(self, t, flow, step):
        buffer = self.buffer(t, flow, step)
        return [
            remote(
                self.blocks(t, flow, step, place), buffer.at[i], self.send.at[t, flow, step, i],
                self.recv.at[t, flow, step, i], device,
            )
            for i, (place, device) in enumerate(self.me.partners(self.flows[t][flow][1][step]))
        ]

    def take(self, t, flow, step):
        copies = self.copies(t, flow, step)
        for copy in copies:
            copy.wait_recv()
        target = self.blocks(t, flow, step, getattr(self.me, self.flows[t][flow][1][step]))
        buffer = self.buffer(t, flow, step)

        def add(*index):
            value = target.at[index][...] if index else target[...]
            for i in range(len(copies)):
                value = value + buffer.at[(i,) + index][...]
            if index:
                target.at[index][...] = value
            else:
                target[...] = value

        if len(target.shape) == 2:
            add()
        else:

            @pl.loop(0, target.shape[0])
            def _(index):
                add(index)

    def stage(self, t, step):
        flows = range(len(self.flows[t]))
        if step == 0:
            self.cross(t).start()
            self.load(t).start()
        if step == 1:
            self.load(t).wait()
            self.cross(t).wait()

            @pl.loop(0, 8)
            def _(index):
                half, block = index // 4, index % 4
                self.acc[t, half, block] = self.acc[t, half, block] + self.arrived[t, half, block]

        for flow in flows:
            if step > 2:
                self.take(t, flow, step - 3)
            if 2 <= step <= STEPS + 1:
                for copy in self.copies(t, flow, step - 2):
                    copy.start()
        if step == STEPS + 2:
            me = self.me
            for flow in flows:
                for before in range(STEPS):
                    for copy in self.copies(t, flow, before):
                        copy.wait_send()
            self.out[t] = self.acc[t, me.y, me.z, me.x].astype(F32)


def staggered(types, stages, gap=1):
    ticks = stages + gap * (types - 1)
    return [
        [(t, tick - gap * t) for t in range(types) if 0 <= tick - gap * t < stages]
        for tick in range(ticks)
    ]


def widen(turned, half, model):
    size = model // 2
    part = turned[half * size : (half + 1) * size, :].astype(F32)
    fill = jnp.zeros((HALF - size, part.shape[1]), F32)
    return jnp.concatenate([part, fill], axis=0).T


def narrow(value, half, model):
    return value[:, half * HALF : (half + 1) * HALF].T[: model // 2]


def turn_head(rows, cos, sin, back=False):
    first, second = rows[: HD // 2], rows[HD // 2 :]
    if back:
        return first * cos + second * sin, second * cos - first * sin
    return first * cos - second * sin, second * cos + first * sin


def qkv_kernel(model, state, gain, weight, cosine, sine, normed, scale, queries, keys, values):
    inputs = state[...]
    inv = lax.rsqrt(jnp.sum(inputs * inputs, axis=-1, keepdims=True) * (1.0 / model) + 1e-05)
    scale[...] = inv
    low = (inputs * inv * gain[...]).astype(BF16)
    normed[...] = low
    left, right = low[:, :HALF], low[:, HALF:]
    cos, sin = cosine[...], sine[...]
    count = KV * HD
    for first in range(0, QKV, count):
        rows = pl.ds(first, count)
        pre = nt(weight[0, rows, :], left) + nt(weight[1, rows, :], right)
        for index in range(KV):
            part = pre[index * HD : (index + 1) * HD]
            if first >= VALUE_AT:
                values[index] = part.astype(BF16)
                continue
            top, bottom = turn_head(part, cos, sin)
            if first < KEY_AT:
                head = first // HD + index
                queries[head, : HD // 2, :] = (top * HD ** (-0.5)).astype(BF16)
                queries[head, HD // 2 :, :] = (bottom * HD ** (-0.5)).astype(BF16)
            else:
                keys[index, : HD // 2, :] = top.astype(BF16)
                keys[index, HD // 2 :, :] = bottom.astype(BF16)


def qkv_call(model, state, gain, weight, cosine, sine, rows=512):
    tokens = state.shape[0]
    by_row = lambda width: pl.BlockSpec((rows, width), lambda i: (i, 0))
    by_lane = pl.BlockSpec((HD // 2, rows), lambda i: (0, i))
    heads = lambda count: pl.BlockSpec((count, HD, rows), lambda i: (0, 0, i))
    return pl.pallas_call(
        functools.partial(qkv_kernel, model),
        grid=(tokens // rows,),
        in_specs=[by_row(WIDE), whole(1, WIDE), whole(2, QKV, HALF), by_lane, by_lane],
        out_specs=[by_row(WIDE), by_row(1), heads(H), heads(KV), heads(KV)],
        out_shape=[
            jax.ShapeDtypeStruct((tokens, WIDE), BF16),
            jax.ShapeDtypeStruct((tokens, 1), F32),
            jax.ShapeDtypeStruct((H, HD, tokens), BF16),
            jax.ShapeDtypeStruct((KV, HD, tokens), BF16),
            jax.ShapeDtypeStruct((KV, HD, tokens), BF16),
        ],
        compiler_params=compiler(),
        cost_estimate=cost(2 * tokens * WIDE * QKV, 20e6),
        name="project_qkv",
    )(state, gain, weight, cosine, sine)


def key_mask(block):
    row = lax.broadcasted_iota(jnp.int32, (block, GROUP * block), 0)
    column = lax.broadcasted_iota(jnp.int32, (block, GROUP * block), 1)
    return row <= jnp.bitwise_and(column, block - 1)


def group_block(ref, at, block):
    return jnp.concatenate([ref[head, :, at : at + block] for head in range(GROUP)], axis=1)


def ahead_of(items, count, make):
    pending = [make(item) for item in items[:count]]
    for turn, item in enumerate(items):
        if turn + count < len(items):
            pending.append(make(items[turn + count]))
        yield item, pending.pop(0)


def attend_kernel(block, ahead, queries, keys, values, mixed, log_sum):
    tokens = keys.shape[2]
    key_rows = keys[0].T

    def scores(at):
        query = group_block(queries, at, block)
        tiles = [nn(key_rows[first : first + block], query) for first in range(0, at + block, block)]
        tiles[-1] = jnp.where(key_mask(block), tiles[-1], -jnp.inf)
        return tiles

    for at, tiles in ahead_of(list(range(0, tokens, block)), ahead, scores):
        peak = functools.reduce(
            jnp.maximum, [jnp.max(tile, axis=0, keepdims=True) for tile in tiles]
        )
        total = out = 0.0
        for index, score in enumerate(tiles):
            weight = jnp.exp(score - peak)
            total = total + jnp.sum(weight, axis=0, keepdims=True)
            value = values[0, :, index * block : (index + 1) * block]
            out = out + nn(value, weight.astype(BF16))
        out = (out * (1.0 / total)).astype(BF16)
        logs = peak + jnp.log(total)
        for head in range(GROUP):
            part = slice(head * block, (head + 1) * block)
            mixed[head, :, at : at + block] = out[:, part]
            log_sum[head, :, at : at + block] = logs[:, part]


def attend_call(queries, keys, values, block=256):
    tokens = queries.shape[2]
    heads = lambda count: pl.BlockSpec((count, HD, tokens), lambda i: (i, 0, 0))
    return pl.pallas_call(
        functools.partial(attend_kernel, block, 3),
        grid=(KV,),
        in_specs=[heads(GROUP), heads(1), heads(1)],
        out_specs=[heads(GROUP), pl.BlockSpec((GROUP, 1, tokens), lambda i: (i, 0, 0))],
        out_shape=[
            jax.ShapeDtypeStruct((H, HD, tokens), BF16),
            jax.ShapeDtypeStruct((H, 1, tokens), F32),
        ],
        compiler_params=compiler(),
        cost_estimate=cost(4 * tokens * tokens * H * 128, 20e6),
        name="attend",
    )(queries, keys, values)


def attend_back_kernel(
    block, queries, keys, values, log_sum, grad_mixed, grad_queries, grad_keys, grad_values
):
    tokens = keys.shape[2]
    key_rows, value_rows = keys[0].T, values[0].T

    def products(at):
        query, grad = group_block(queries, at, block), group_block(grad_mixed, at, block)
        return [
            (
                nn(key_rows[first : first + block], query),
                nn(value_rows[first : first + block], grad),
            )
            for first in range(0, at + block, block)
        ]

    for at, tiles in ahead_of(list(range(tokens - block, -1, -block)), 1, products):
        query, grad = group_block(queries, at, block), group_block(grad_mixed, at, block)
        logs = group_block(log_sum, at, block)
        weights = []
        delta = 0.0
        for index, (score, grad_probs) in enumerate(tiles):
            probs = jnp.exp(score - logs)
            if index * block == at:
                probs = jnp.where(key_mask(block), probs, 0.0)
            delta = delta + jnp.sum(probs * grad_probs, axis=0, keepdims=True)
            weights.append(probs)
        by_query = 0.0
        for index, (_, grad_probs) in enumerate(tiles):
            part = pl.ds(index * block, block)
            probs = weights[index]
            low = (probs * (grad_probs - delta)).astype(BF16)
            by_query = by_query + nn(keys[0, :, part], low)
            key_part = nt(query, low)
            value_part = nt(grad, probs.astype(BF16))
            if at + block == tokens:
                grad_keys[0, :, part] = key_part
                grad_values[0, :, part] = value_part
            else:
                grad_keys[0, :, part] += key_part
                grad_values[0, :, part] += value_part
        for head in range(GROUP):
            grad_queries[head, :, at : at + block] = by_query[:, head * block : (head + 1) * block]


def attend_back_call(queries, keys, values, log_sum, grad_mixed, block=256):
    tokens = queries.shape[2]
    heads = lambda count: pl.BlockSpec((count, HD, tokens), lambda i: (i, 0, 0))
    return pl.pallas_call(
        functools.partial(attend_back_kernel, block),
        grid=(KV,),
        in_specs=[
            heads(GROUP), heads(1), heads(1),
            pl.BlockSpec((GROUP, 1, tokens), lambda i: (i, 0, 0)), heads(GROUP),
        ],
        out_specs=[heads(GROUP), heads(1), heads(1)],
        out_shape=[
            jax.ShapeDtypeStruct((H, HD, tokens), F32),
            jax.ShapeDtypeStruct((KV, HD, tokens), F32),
            jax.ShapeDtypeStruct((KV, HD, tokens), F32),
        ],
        compiler_params=compiler(),
        cost_estimate=cost(10 * tokens * tokens * H * 128, 30e6),
        name="attend_back",
    )(queries, keys, values, log_sum, grad_mixed)


GATHER_FLOWS = ((((0, 80), "zyx"), ((80, 128), "zxy"), ((128, 160), "yxz")),) + (
    (((0, 48), "zyx"), ((48, 80), "zxy"), ((80, 96), "yxz")),
) * CHUNKS


def row_pairs(sizes):
    pairs = []
    by_weight = first = 0
    for size in sizes:
        for device in range(4):
            pairs.append((device * PIECE + first, by_weight, size))
            by_weight += size
        first += size
    return pairs


def order_weights(model, sizes, raw, by_device, by_weight, qkv_weight, out_weight):
    counts = [4 * size for size in sizes]
    starts = [sum(counts[:i]) for i in range(4)]
    rows = 4 * PIECE
    size = model // 2
    blank = jnp.zeros((HALF - size, HALF), F32)
    for half in range(2):
        for pair in range(2):
            outs = []
            for z in (2 * pair, 2 * pair + 1):
                by_device[...] = raw[half, z * rows : (z + 1) * rows, :].astype(F32)
                for source, target, count in row_pairs(sizes):
                    by_weight[target : target + count, :] = by_device[source : source + count, :]
                done = by_weight[...]
                for i, first in enumerate((0, KEY_AT, VALUE_AT)):
                    at = first + z * counts[i]
                    part = done[starts[i] : starts[i] + counts[i]]
                    qkv_weight[half, at : at + counts[i], :] = part.astype(BF16)
                outs.append(done[starts[3] :])
            turned = jnp.concatenate(outs + [blank], axis=0).T
            out_weight[half * size : (half + 1) * size, pair * HALF : (pair + 1) * HALF] = turned[
                :size
            ].astype(BF16)


def sigmoid(value):
    return 0.5 * jnp.tanh(0.5 * value) + 0.5


def feed_block(gate_weight, up_weight, normed, rows, gate, up):
    left, right = normed[rows, :HALF], normed[rows, HALF:]
    gate_proj = nt(left, gate_weight[0]) + nt(right, gate_weight[1])
    up_proj = nt(left, up_weight[0]) + nt(right, up_weight[1])
    gate[rows, :] = gate_proj.astype(BF16)
    up[rows, :] = up_proj.astype(BF16)
    return (gate_proj * sigmoid(gate_proj) * up_proj).astype(BF16)


def out_block(model, state, mixed, out_weight, gain, hidden_state, normed, scale):
    heads = mixed[...].reshape(H * HD, mixed.shape[2])
    after = state[...] + tn(heads, out_weight[...])
    hidden_state[...] = after
    inv = lax.rsqrt(jnp.sum(after * after, axis=-1, keepdims=True) * (1.0 / model) + 1e-05)
    scale[...] = inv
    normed[...] = (after * inv * gain[...]).astype(BF16)


START_KINDS = lambda tokens, units: [
    ((2, QKV, HALF), BF16),
    ((H * HD, WIDE), BF16),
    ((tokens, WIDE), F32),
    ((tokens, WIDE), BF16),
    ((tokens, 1), F32),
    ((H, HD, tokens), BF16),
    ((KV, HD, tokens), BF16),
    ((KV, HD, tokens), BF16),
    ((H, 1, tokens), F32),
    ((tokens, WIDE), F32),
    ((H, HD, tokens), BF16),
    ((tokens, WIDE), BF16),
    ((tokens, 1), F32),
]


def feed_spec(t, first=0):
    return pl.BlockSpec(
        (None, 2, 4, 2, 2, ROWS, HALF), lambda i: (first + i, 0, 0, 0, 0, t, 0)
    )


def start_kernel(
    model, sizes, own, feed_own, seqs, gain, feed_gain, cosine, sine,
    full, feed_full, output_out, gate_out, up_out, *rest,
):
    kinds = len(START_KINDS(0, 0))
    outs_refs, rest = rest[:kinds], rest[kinds:]
    (
        qkv_weight, out_weight, state, normed, scale, queries, keys, values, log_sum, hidden_state,
        mixed, feed_normed, feed_scale,
    ), rest = rest[:kinds], rest[kinds:]
    seq, by_device, by_weight, seq_sem, raw_sem, out_sem, *gather_sems = rest
    me = Place()
    y = me.y
    gather = Gather(
        me, GATHER_FLOWS, [own] + [feed_own.at[i] for i in range(CHUNKS)],
        [full] + [feed_full.at[i] for i in range(CHUNKS)], *gather_sems,
    )
    greet(me.everyone())
    swap = remote(
        seqs.at[1 - y], seq.at[y], seq_sem.at[0], seq_sem.at[1], me.partners("y")[0][1]
    )
    swap.start()
    stay = pltpu.make_async_copy(seqs.at[y], seq.at[y], seq_sem.at[2])
    stay.start()
    ticks = staggered(1 + CHUNKS, STEPS + 2)

    def tick(*counts):
        for count in counts:
            for t, stage in ticks[count]:
                gather.stage(t, stage)

    tick(0, 1, 2)
    rows = seq.shape[2]
    tokens = 2 * rows
    outs = []

    def give(index, source):
        copy = pltpu.make_async_copy(source, outs_refs[index], out_sem.at[index])
        copy.start()
        outs.append(copy)

    stay.wait()
    swap.wait()
    for part in range(2):
        for half in range(2):
            state[part * rows : (part + 1) * rows, half * HALF : (half + 1) * HALF] = widen(
                seq.at[part], half, model
            )
    give(2, state)
    tick(3, 4)

    def put_in_order(raw):
        fetch = pltpu.make_async_copy(full, raw, raw_sem.at[0])
        fetch.start()
        fetch.wait()
        order_weights(
            model, sizes, raw.reshape(2, 16 * PIECE, HALF), by_device, by_weight, qkv_weight,
            out_weight,
        )

    pl.run_scoped(put_in_order, pltpu.VMEM((2, 4, 2, 2, PIECE, HALF), BF16))
    give(0, qkv_weight)
    give(1, out_weight)
    for at in range(0, tokens, rows):
        part = pl.ds(at, rows)
        qkv_kernel(
            model, state.at[part], gain, qkv_weight, cosine.at[:, part], sine.at[:, part],
            normed.at[part], scale.at[part], queries.at[:, :, part], keys.at[:, :, part],
            values.at[:, :, part],
        )
    give(3, normed)
    give(4, scale)
    give(5, queries)
    give(6, keys)
    give(7, values)
    tick(5)

    @pl.loop(0, KV)
    def _(group):
        some = pl.ds(group * GROUP, GROUP)
        one = pl.ds(group, 1)
        attend_kernel(
            tokens // 4, 1, queries.at[some], keys.at[one], values.at[one], mixed.at[some],
            log_sum.at[some],
        )
        pl.when(group == 1)(lambda: tick(6))
        pl.when(group == 4)(lambda: tick(7))

    give(8, log_sum)
    give(10, mixed)
    out_block(model, state, mixed, out_weight, feed_gain, hidden_state, feed_normed, feed_scale)
    give(9, hidden_state)
    give(11, feed_normed)
    give(12, feed_scale)

    outs[0].wait()
    state[...] = hidden_state[...]

    def feed_body(gate_weight, up_weight, down_weight, gate, up):
        gates, ups, downs = (
            ref.reshape(2, UNITS, HALF) for ref in (gate_weight, up_weight, down_weight)
        )
        for at in range(0, tokens, rows):
            part = pl.ds(at, rows)
            low = feed_block(gates, ups, feed_normed, part, gate, up)
            state[part, :HALF] += nn(low, downs[0])
            state[part, HALF:] += nn(low, downs[1])

    def feed_chunks(first, count):
        by_unit = pl.BlockSpec((tokens, UNITS), lambda i: (0, first + i))
        pltpu.emit_pipeline(
            feed_body,
            grid=(count,),
            in_specs=[feed_spec(t, first) for t in range(3)],
            out_specs=[by_unit, by_unit],
        )(feed_full, feed_full, feed_full, gate_out, up_out)

    tick(8)
    feed_chunks(0, 3)
    tick(9)
    feed_chunks(3, 2)
    last = pltpu.make_async_copy(state, output_out, raw_sem.at[0])
    last.start()
    for copy in outs[1:]:
        copy.wait()
    last.wait()


def start_call(model, sizes, own, feed_own, seqs, gain, feed_gain, cosine, sine):
    types = 1 + CHUNKS
    tokens = 2 * seqs.shape[2]
    units = 16 * PIECE
    kinds = START_KINDS(tokens, units)
    dma = pltpu.SemaphoreType.DMA
    anywhere = pl.BlockSpec(memory_space=pl.ANY)
    inside = pl.BlockSpec(memory_space=pltpu.VMEM)
    outs = [
        ((2, 4, 2, 2, PIECE, HALF), BF16),
        ((CHUNKS, 2, 4, 2, 2, 3 * ROWS, HALF), BF16),
        ((tokens, WIDE), F32),
        ((tokens, units), BF16),
        ((tokens, units), BF16),
    ] + kinds
    return pl.pallas_call(
        functools.partial(start_kernel, model, sizes),
        out_shape=[jax.ShapeDtypeStruct(*kind) for kind in outs],
        in_specs=[anywhere] * 3 + [inside] * 4,
        out_specs=[anywhere] * len(outs),
        scratch_shapes=[pltpu.VMEM(*kind) for kind in kinds]
        + [
            pltpu.VMEM(seqs.shape, BF16),
            pltpu.VMEM((4 * PIECE, HALF), F32),
            pltpu.VMEM((4 * PIECE, HALF), F32),
            dma((3,)), dma((1,)), dma((len(kinds),)),
        ]
        + Gather.semaphores(types, len(GATHER_FLOWS[0])),
        compiler_params=compiler(collective_id=0, has_side_effects=True),
        name="start",
    )(own, feed_own, seqs, gain, feed_gain, cosine, sine)


def feed_kernel(
    model, block, state, heads, out_weight, gain, gate_weight, up_weight, down_weight,
    final, hidden_state, normed, scale, gate, up, output,
):
    tokens = state.shape[0]

    @pl.when(pl.program_id(0) == 0)
    def _():
        out_block(model, state, heads, out_weight, gain, hidden_state, normed, scale)
        output[...] = hidden_state[...]

    gate_weight, up_weight, down_weight = (
        ref.reshape(2, UNITS, HALF) for ref in (gate_weight, up_weight, down_weight)
    )
    for at in range(0, tokens, block):
        rows = pl.ds(at, block)
        hidden = feed_block(gate_weight, up_weight, normed, rows, gate, up)
        output[rows, :HALF] += nn(hidden, down_weight[0])
        output[rows, HALF:] += nn(hidden, down_weight[1])

    @pl.when(pl.program_id(0) == pl.num_programs(0) - 1)
    def _():
        size = model // 2
        for part in range(2):
            value = output[part * tokens // 2 : (part + 1) * tokens // 2, :]
            for half in range(2):
                final[part, half * size : (half + 1) * size, :] = narrow(value, half, model).astype(
                    BF16
                )


def feed_call(model, state, heads, out_weight, gain, weights, block=512):
    tokens = state.shape[0]
    units = CHUNKS * UNITS
    by_unit = pl.BlockSpec((tokens, UNITS), lambda i: (0, i))
    return pl.pallas_call(
        functools.partial(feed_kernel, model, block),
        grid=(CHUNKS,),
        in_specs=[
            whole(tokens, WIDE), whole(H, HD, tokens), whole(H * HD, WIDE), whole(1, WIDE),
            feed_spec(0), feed_spec(1), feed_spec(2),
        ],
        out_specs=[
            whole(2, model, tokens // 2), whole(tokens, WIDE), whole(tokens, WIDE),
            whole(tokens, 1), by_unit, by_unit,
        ],
        out_shape=[
            jax.ShapeDtypeStruct((2, model, tokens // 2), BF16),
            jax.ShapeDtypeStruct((tokens, WIDE), F32),
            jax.ShapeDtypeStruct((tokens, WIDE), BF16),
            jax.ShapeDtypeStruct((tokens, 1), F32),
            jax.ShapeDtypeStruct((tokens, units), BF16),
            jax.ShapeDtypeStruct((tokens, units), BF16),
        ],
        scratch_shapes=[pltpu.VMEM((tokens, WIDE), F32)],
        compiler_params=compiler(),
        cost_estimate=cost(2 * tokens * WIDE * (3 * units + H * HD), 50e6),
        name="feed",
    )(state, heads, out_weight, gain, weights, weights, weights)


def feed_back_kernel(
    model, block, pair, *refs,
):
    step = pl.program_id(0)
    if pair:
        both, other, *refs = refs
        *refs, grad_out = refs
    else:
        grad_out, *refs = refs
    (
        hidden_state, gain, scale, out_weight, gate, up, gate_weight, up_weight, down_weight,
        grad_state, gain_term, grad_low, branch_low, grad_mixed, grad_gate, grad_up, hidden,
    ) = refs
    tokens = grad_out.shape[0]

    @pl.when(step == 0)
    def _():
        if pair:
            count = tokens // 2
            y = lax.axis_index("narrow")
            for place, turned in ((y, both.at[y]), (1 - y, other)):
                rows = pl.ds(pl.multiple_of(place * count, count), count)
                for half in range(2):
                    columns = pl.ds(half * HALF, HALF)
                    grad_out[rows, columns] = widen(turned, half, model)
        grad_low[...] = grad_out[...].astype(BF16)
        grad_state[...] = jnp.zeros_like(grad_state)

    gate_weight, up_weight, down_weight = (
        ref.reshape(2, UNITS, HALF) for ref in (gate_weight, up_weight, down_weight)
    )

    for at in range(0, tokens, block):
        rows = pl.ds(at, block)
        grad_hidden = nt(grad_low[rows, :HALF], down_weight[0]) + nt(
            grad_low[rows, HALF:], down_weight[1]
        )
        gate_proj = gate[rows, :].astype(F32)
        up_proj = up[rows, :].astype(F32)
        sig = sigmoid(gate_proj)
        passed = gate_proj * sig
        hidden[rows, :] = (passed * up_proj).astype(BF16)
        by_gate = (grad_hidden * up_proj * (sig + passed * (1.0 - sig))).astype(BF16)
        by_up = (grad_hidden * passed).astype(BF16)
        grad_gate[rows, :] = by_gate
        grad_up[rows, :] = by_up
        grad_state[rows, :HALF] += nn(by_gate, gate_weight[0]) + nn(by_up, up_weight[0])
        grad_state[rows, HALF:] += nn(by_gate, gate_weight[1]) + nn(by_up, up_weight[1])

    @pl.when(step == pl.num_programs(0) - 1)
    def _():
        total = jnp.zeros(gain.shape, F32)
        for at in range(0, tokens, block):
            rows = pl.ds(at, block)
            grad, after, inv = grad_state[rows, :], hidden_state[rows, :], scale[rows, :]
            total = total + jnp.sum(grad * after * inv, axis=0, keepdims=True)
            upstream = grad * gain[...]
            inner = jnp.sum(upstream * after, axis=-1, keepdims=True) * (1.0 / model)
            result = grad_out[rows, :] + inv * upstream - after * (inv * inv * inv) * inner
            grad_state[rows, :] = result
            low = result.astype(BF16)
            branch_low[rows, :] = low
            part = nt(out_weight[...], low).astype(BF16)
            grad_mixed[:, :, rows] = part.reshape(H, HD, block)
        gain_term[...] = total


def feed_back_call(
    model, grads, hidden_state, gain, scale, out_weight, gate, up, weights, block=512
):
    tokens = hidden_state.shape[0]
    pair = len(grads) == 2
    units = CHUNKS * UNITS
    by_unit = pl.BlockSpec((tokens, UNITS), lambda i: (0, i))
    return pl.pallas_call(
        functools.partial(feed_back_kernel, model, block, pair),
        grid=(CHUNKS,),
        in_specs=[
            whole(*grad.shape) for grad in grads
        ]
        + [
            whole(tokens, WIDE), whole(1, WIDE), whole(tokens, 1), whole(H * HD, WIDE),
            by_unit, by_unit, feed_spec(0), feed_spec(1), feed_spec(2),
        ],
        out_specs=[
            whole(tokens, WIDE), whole(1, WIDE), whole(tokens, WIDE), whole(tokens, WIDE),
            whole(H, HD, tokens),
        ]
        + [by_unit] * 3,
        out_shape=[
            jax.ShapeDtypeStruct((tokens, WIDE), F32),
            jax.ShapeDtypeStruct((1, WIDE), F32),
            jax.ShapeDtypeStruct((tokens, WIDE), BF16),
            jax.ShapeDtypeStruct((tokens, WIDE), BF16),
            jax.ShapeDtypeStruct((H, HD, tokens), BF16),
        ]
        + [jax.ShapeDtypeStruct((tokens, units), BF16)] * 3,
        scratch_shapes=[pltpu.VMEM((tokens, WIDE), F32)] if pair else [],
        compiler_params=compiler(),
        cost_estimate=cost(6 * tokens * WIDE * units, 60e6),
        name="feed_back",
    )(*grads, hidden_state, gain, scale, out_weight, gate, up, weights, weights, weights)


def qkv_back_rows(
    model, grad_queries, grad_keys, grad_values, state, scale, grad_state, gain, weight, cosine, sine,
    back,
):
    cos, sin = cosine[...], sine[...]
    for first, heads, factor in ((0, grad_queries, HD ** (-0.5)), (KEY_AT, grad_keys, 1.0)):
        for head in range(heads.shape[0]):
            at = first + head * HD
            top, bottom = turn_head(heads[head], cos, sin, back=True)
            back[at : at + HD // 2, :] = (top * factor).astype(BF16)
            back[at + HD // 2 : at + HD, :] = (bottom * factor).astype(BF16)
    back[VALUE_AT:, :] = grad_values[...].astype(BF16).reshape(KV * HD, back.shape[1])
    low = back[...]
    grad = jnp.concatenate([tn(low, weight[0]), tn(low, weight[1])], axis=1)
    inputs, inv = state[...], scale[...]
    gain_part = jnp.sum(grad * inputs * inv, axis=0, keepdims=True)
    upstream = grad * gain[...]
    inner = jnp.sum(upstream * inputs, axis=-1, keepdims=True) * (1.0 / model)
    return gain_part, grad_state[...] + inv * upstream - inputs * (inv * inv * inv) * inner


def qkv_back_kernel(
    model, grad_queries, grad_keys, grad_values, state, scale, grad_state, gain, weight, cosine, sine,
    grad_input, gain_term, back,
):
    gain_part, grad = qkv_back_rows(
        model, grad_queries, grad_keys, grad_values, state, scale, grad_state, gain, weight, cosine,
        sine, back,
    )
    grad_input[...] = grad

    @pl.when(pl.program_id(0) == 0)
    def _():
        gain_term[...] = jnp.zeros(gain_term.shape, F32)

    gain_term[...] += gain_part


def qkv_back_call(
    model, grad_queries, grad_keys, grad_values, state, scale, grad_state, gain, weight, cosine,
    sine, rows=256,
):
    tokens = state.shape[0]
    by_row = lambda width: pl.BlockSpec((rows, width), lambda i: (i, 0))
    heads = lambda count: pl.BlockSpec((count, HD, rows), lambda i: (0, 0, i))
    by_lane = lambda count: pl.BlockSpec((count, rows), lambda i: (0, i))
    return pl.pallas_call(
        functools.partial(qkv_back_kernel, model),
        grid=(tokens // rows,),
        in_specs=[
            heads(H), heads(KV), heads(KV), by_row(WIDE), by_row(1), by_row(WIDE), whole(1, WIDE),
            whole(2, QKV, HALF), by_lane(HD // 2), by_lane(HD // 2),
        ],
        out_specs=[by_row(WIDE), whole(1, WIDE), by_lane(QKV)],
        out_shape=[
            jax.ShapeDtypeStruct((tokens, WIDE), F32),
            jax.ShapeDtypeStruct((1, WIDE), F32),
            jax.ShapeDtypeStruct((QKV, tokens), BF16),
        ],
        compiler_params=compiler(),
        cost_estimate=cost(2 * tokens * WIDE * QKV, 30e6),
        name="qkv_back",
    )(
        grad_queries, grad_keys, grad_values, state, scale, grad_state, gain, weight, cosine, sine
    )


def spread_rows(model, sizes, rows, by_device, z):
    gap = HALF - model // 2 if z >= 2 else 0
    firsts = (0, KEY_AT, VALUE_AT, QKV + gap)
    for target, source, count in row_pairs(sizes):
        weight = [i for i in range(4) if source >= 4 * sum(sizes[:i])][-1]
        at = firsts[weight] + 4 * z * sizes[weight] + source - 4 * sum(sizes[:weight])
        by_device[target : target + count, :] = rows[at : at + count, :]
    return by_device[...]


def term_rows_of(model, back, normed, low, mixed, rows):
    rows[:QKV, :] = nn(back, normed)
    size = model // 2
    product = nn(mixed, low)
    blank = jnp.zeros((HALF - size, HALF), F32)
    for pair in range(2):
        part = product[:, pair * HALF : (pair + 1) * HALF]
        turned = jnp.concatenate([part, blank], axis=0).T
        rows[QKV + pair * HALF : QKV + (pair + 1) * HALF, :] = turned


def attn_terms_kernel(model, sizes, back, normed, low, mixed, term, rows, by_device):
    z = pl.program_id(1)

    @pl.when(z == 0)
    def _():
        term_rows_of(model, back[...], normed[...], low[...], mixed[...], rows)

    for at in range(4):

        @pl.when(z == at)
        def _(at=at):
            value = spread_rows(model, sizes, rows, by_device, at)
            term[0, 0] = value.astype(BF16).reshape(2, 2, PIECE, HALF)


def attn_terms_call(model, sizes, back, normed, low, mixed):
    tokens = normed.shape[0]
    size = model // 2
    return pl.pallas_call(
        functools.partial(attn_terms_kernel, model, sizes),
        grid=(2, 4),
        in_specs=[
            whole(QKV, tokens),
            pl.BlockSpec((tokens, HALF), lambda i, z: (0, i)),
            whole(tokens, WIDE),
            pl.BlockSpec((size, tokens), lambda i, z: (i, 0)),
        ],
        out_specs=pl.BlockSpec((1, 1, 2, 2, PIECE, HALF), lambda i, z: (i, z, 0, 0, 0, 0)),
        out_shape=jax.ShapeDtypeStruct((2, 4, 2, 2, PIECE, HALF), BF16),
        scratch_shapes=[pltpu.VMEM((QKV + WIDE, HALF), F32), pltpu.VMEM((4 * PIECE, HALF), F32)],
        compiler_params=compiler(),
        cost_estimate=cost(2 * tokens * WIDE * (QKV + WIDE), 30e6),
        name="attn_terms",
    )(back, normed, low, mixed)


MAIN_FLOWS = tuple(
    (((0, 48), first), ((48, 80), second), ((80, 96), third))
    for first, second, third in (("yxz", "xyz", "zxy"), ("xyz", "yxz", "zyx")) * 3
)[:CHUNKS]
LAST_ROWS = 80
LAST_FLOWS = ((((0, 32), "xyz"), ((32, 64), "yxz"), ((64, 80), "zxy")),) * 2

FEED_STAGES = {
    0: ((0, 0),),
    1: ((0, 1), (0, 2), (1, 0)),
    2: ((1, 1), (2, 0)),
    3: ((0, 3), (1, 2), (2, 1), (3, 0)),
    4: ((3, 1), (4, 0)),
}
ATTEND_STAGES = {
    0: ((4, 1), (0, 4), (1, 3), (2, 2)),
    2: ((0, 5), (1, 4), (2, 3), (3, 2)),
    4: ((1, 5), (2, 4), (3, 3), (4, 2)),
}
QKV_STAGES = {2: ((2, 5), (3, 4), (4, 3))}
TERM_STAGES = {2: ((3, 5), (4, 4)), 7: ((4, 5),)}


def finish_kernel(
    model, sizes, low_one, low_two, normed_one, normed_two, down_one, down_two, gate_one, gate_two,
    up_one, up_two, grad_state, grad_mixed, low_state, queries, keys, values, log_sum, state, scale, gain, qkv_weight,
    cosine, sine, normed, mixed, before,
    sums, mine, got, gain_term, term_out, back, grad_queries, grad_keys, grad_values,
    packed, term_rows, by_device, made, swap_sem, *scratch,
):
    me = Place()
    swap = remote(packed, got, swap_sem.at[0], swap_sem.at[1], me.partners("y")[0][1])
    scatter = Scatter(
        me, MAIN_FLOWS, [(made.at[i % 2], 0) for i in range(CHUNKS)], sums, scratch
    )
    tokens = grad_state.shape[0]
    rows = tokens // 4
    greet(me.everyone())

    def run_stages(points, step):
        for at, stages in points.items():

            def act(stages=stages):
                for t, stage in stages:
                    scatter.stage(t, stage)

            pl.when(step == at)(act)

    def feed_terms(lows, normeds, load_sem):
        loads = [
            pltpu.make_async_copy(source, target, load_sem.at[i])
            for i, (source, target) in enumerate(
                (
                    (low_one, lows.at[0]), (low_two, lows.at[1]),
                    (normed_one, normeds.at[0]), (normed_two, normeds.at[1]),
                )
            )
        ]
        for load in loads:
            load.start()
        for load in loads:
            load.wait()

        def term_body(by_gate, by_gate_two, by_up, by_up_two, by_hidden, by_hidden_two):
            slot = made.at[lax.rem(pl.program_id(0), 2)]
            for t, (one, two, right) in enumerate(
                (
                    (by_gate, by_gate_two, normeds),
                    (by_up, by_up_two, normeds),
                    (by_hidden, by_hidden_two, lows),
                )
            ):
                for half in range(2):
                    lanes = pl.ds(half * HALF, HALF)
                    value = tn(one[...], right[0, :, lanes]) + tn(two[...], right[1, :, lanes])
                    slot.at[half, :, :, :, pl.ds(t * ROWS, ROWS), :][...] = value.astype(
                        BF16
                    ).reshape(4, 2, 2, ROWS, HALF)
            run_stages(FEED_STAGES, pl.program_id(0))

        by_unit = pl.BlockSpec((tokens, UNITS), lambda i: (0, i))
        pltpu.emit_pipeline(term_body, grid=(CHUNKS,), in_specs=[by_unit] * 6, out_specs=[])(
            gate_one, gate_two, up_one, up_two, down_one, down_two
        )

    pl.run_scoped(
        feed_terms,
        pltpu.VMEM((2, tokens, WIDE), BF16),
        pltpu.VMEM((2, tokens, WIDE), BF16),
        pltpu.SemaphoreType.DMA((4,)),
    )

    def attend_body(query, key, value, logs, grad, by_query, by_key, by_value):
        attend_back_kernel(rows, query, key, value, logs, grad, by_query, by_key, by_value)
        run_stages(ATTEND_STAGES, pl.program_id(0))

    heads = lambda count: pl.BlockSpec((count, HD, tokens), lambda i: (i, 0, 0))
    pltpu.emit_pipeline(
        attend_body,
        grid=(KV,),
        in_specs=[
            heads(GROUP), heads(1), heads(1),
            pl.BlockSpec((GROUP, 1, tokens), lambda i: (i, 0, 0)), heads(GROUP),
        ],
        out_specs=[heads(GROUP), heads(1), heads(1)],
    )(queries, keys, values, log_sum, grad_mixed, grad_queries, grad_keys, grad_values)

    gain_term[...] = jnp.zeros(gain_term.shape, F32)

    size = model // 2

    def qkv_body(by_query, by_key, by_value, inputs, inv, grad, cos, sin, by_input, low):
        gain_part, value = qkv_back_rows(
            model, by_query, by_key, by_value, inputs, inv, grad, gain, qkv_weight, cos, sin, low
        )
        gain_term[...] += gain_part
        step = pl.program_id(0)
        for count in range(2):

            @pl.when(step == count)
            def _(count=count):
                for half in range(2):
                    packed[
                        half * size : (half + 1) * size, count * rows : (count + 1) * rows
                    ] = narrow(value, half, model).astype(BF16)

        @pl.when(step == 1)
        def _():
            swap.start()

        @pl.when(step >= 2)
        def _():
            for half in range(2):
                by_input[half * size : (half + 1) * size, :] = narrow(value, half, model)

        run_stages(QKV_STAGES, step)

    order = lambda i: lax.rem(i + 2 * (1 - me.y), 4)
    by_row = lambda width: pl.BlockSpec((rows, width), lambda i: (order(i), 0))
    some = lambda count: pl.BlockSpec((count, HD, rows), lambda i: (0, 0, order(i)))
    by_lane = lambda count: pl.BlockSpec((count, rows), lambda i: (0, order(i)))
    pltpu.emit_pipeline(
        qkv_body,
        grid=(4,),
        in_specs=[
            some(H), some(KV), some(KV), by_row(WIDE), by_row(1), by_row(WIDE),
            by_lane(HD // 2), by_lane(HD // 2),
        ],
        out_specs=[
            pl.BlockSpec((model, rows), lambda i: (0, jnp.maximum(i - 2, 0))), by_lane(QKV),
        ],
    )(grad_queries, grad_keys, grad_values, state, scale, grad_state, cosine, sine, mine, back)

    def term_body(low, by_normed, grad, by_mixed, earlier, term):
        z = pl.program_id(1)

        @pl.when(z == 0)
        def _():
            heads_half = by_mixed[...]
            term_rows_of(model, low[...], by_normed[...], grad[...], heads_half, term_rows)

        for at in range(4):

            @pl.when(z == at)
            def _(at=at):
                value = spread_rows(model, sizes, term_rows, by_device, at)
                value = value + earlier[0, 0].reshape(4 * PIECE, HALF).astype(F32)
                term[0, 0] = value.astype(BF16).reshape(2, 2, PIECE, HALF)

        run_stages(TERM_STAGES, 4 * pl.program_id(0) + z)

    fixed = lambda width: pl.BlockSpec((tokens, width), lambda i, z: (0, 0))
    by_half = pl.BlockSpec((tokens, HALF), lambda i, z: (0, i))
    piece = pl.BlockSpec((1, 1, 2, 2, PIECE, HALF), lambda i, z: (i, z, 0, 0, 0, 0))
    pltpu.emit_pipeline(
        term_body,
        grid=(2, 4),
        in_specs=[
            pl.BlockSpec((QKV, tokens), lambda i, z: (0, 0)), by_half, fixed(WIDE),
            pl.BlockSpec((size, tokens), lambda i, z: (i, 0)), piece,
        ],
        out_specs=[piece],
    )(back, normed, low_state, mixed, before, term_out)
    swap.wait()


def finish_call(
    model, sizes, operands, grad_state, grad_mixed, low_state, queries, keys, values, log_sum, state,
    scale, gain,
    qkv_weight, cosine, sine, normed, mixed, before,
):
    tokens = grad_state.shape[0]
    anywhere = pl.BlockSpec(memory_space=pl.ANY)
    inside = pl.BlockSpec(memory_space=pltpu.VMEM)
    outs = [
        ((CHUNKS, 3 * ROWS, HALF), F32, inside),
        ((model, tokens // 2), F32, anywhere),
        ((model, tokens // 2), BF16, anywhere),
        ((1, WIDE), F32, inside),
        ((2, 4, 2, 2, PIECE, HALF), BF16, anywhere),
        ((QKV, tokens), BF16, anywhere),
        ((H, HD, tokens), F32, anywhere),
        ((KV, HD, tokens), F32, anywhere),
        ((KV, HD, tokens), F32, anywhere),
    ]
    return pl.pallas_call(
        functools.partial(finish_kernel, model, sizes),
        out_shape=[jax.ShapeDtypeStruct(shape, kind) for shape, kind, _ in outs],
        in_specs=[anywhere] * 19 + [inside] * 2 + [anywhere] * 5,
        out_specs=[where for *_, where in outs],
        scratch_shapes=[
            pltpu.VMEM((model, tokens // 2), BF16),
            pltpu.VMEM((QKV + WIDE, HALF), F32),
            pltpu.VMEM((4 * PIECE, HALF), F32),
            pltpu.VMEM((2, 2, 4, 2, 2, 3 * ROWS, HALF), BF16),
            pltpu.SemaphoreType.DMA((2,)),
        ]
        + Scatter.scratch(MAIN_FLOWS, 3 * ROWS),
        compiler_params=compiler(collective_id=1, has_side_effects=True),
        name="finish",
    )(
        *operands, grad_state, grad_mixed, low_state, queries, keys, values, log_sum, state, scale, gain,
        qkv_weight, cosine, sine, normed, mixed, before,
    )[:5]


def last_kernel(term, gains, sums, gains_out, gain_own, gain_get, gain_send, gain_recv, *scratch):
    me = Place()
    y, z = me.y, me.z
    z_one = (me.w + 4 - 8 * (z % 2), y)
    z_two = (me.w + 8 - 16 * (z // 2), y)
    types = len(LAST_FLOWS)
    scatter = Scatter(me, LAST_FLOWS, [(term, t * LAST_ROWS) for t in range(types)], sums, scratch)
    ticks = staggered(types, STEPS + 3)
    gain_own[0] = gains[...]
    greet(me.everyone())

    def tick(count):
        for t, stage in ticks[count]:
            scatter.stage(t, stage)

    tick(0)
    partners = (me.sibling, me.partners("y")[0][1], me.partners("x")[0][1], z_one, z_two)

    def gain_copy(step):
        return remote(
            gain_own.at[step], gain_get.at[step], gain_send.at[step], gain_recv.at[step],
            partners[step],
        )

    gain_copy(0).start()
    for step in range(5):
        tick(1 + step)
        gain_copy(step).wait()
        if step < 4:
            gain_own[step + 1] = gain_own[step] + gain_get[step]
            gain_copy(step + 1).start()
        else:
            gains_out[...] = gain_own[step] + gain_get[step]
    for count in range(6, len(ticks)):
        tick(count)


def last_call(term, gains):
    dma = pltpu.SemaphoreType.DMA
    inside = pl.BlockSpec(memory_space=pltpu.VMEM)
    return pl.pallas_call(
        last_kernel,
        out_shape=[
            jax.ShapeDtypeStruct((len(LAST_FLOWS), LAST_ROWS, HALF), F32),
            jax.ShapeDtypeStruct(gains.shape, F32),
        ],
        in_specs=[pl.BlockSpec(memory_space=pl.ANY), inside],
        out_specs=[inside, inside],
        scratch_shapes=[
            pltpu.VMEM((5,) + gains.shape, F32),
            pltpu.VMEM((5,) + gains.shape, F32),
            dma((5,)),
            dma((5,)),
        ]
        + Scatter.scratch(LAST_FLOWS, LAST_ROWS),
        compiler_params=compiler(collective_id=2, has_side_effects=True),
        name="last",
    )(term, gains)


def halves(array, model):
    pad = [(0, 0)] * (array.ndim - 1)
    left, right = array[..., : model // 2], array[..., model // 2 :]
    pad = pad + [(0, HALF - model // 2)]
    return jnp.concatenate([jnp.pad(left, pad), jnp.pad(right, pad)], axis=-1)


def joined(array, model):
    return jnp.concatenate([array[..., : model // 2], array[..., HALF : HALF + model // 2]], axis=-1)


def rotary(count):
    positions = np.arange(count, dtype=np.float32)
    exponent = np.arange(HD // 2, dtype=np.float32) * np.float32(2.0 / HD)
    frequency = np.power(np.float32(10000.0), -exponent).astype(np.float32)
    angles = positions[:, None] * frequency[None, :]
    cosine, sine = np.cos(angles), np.sin(angles)
    return jnp.asarray(cosine.T, F32), jnp.asarray(sine.T, F32)


def on_device_whole(
    block_input, cotangent, attn_gain, ffn_gain,
    query_weight, key_weight, value_weight, out_weight, gate_weight, up_weight, down_weight,
):
    _, half_rows, model = block_input.shape
    tokens = 2 * half_rows
    y = lax.axis_index("narrow")
    flip = [(0, 1), (1, 0)]
    pieces = (query_weight, key_weight, value_weight, out_weight)
    sizes = tuple(piece.shape[1] for piece in pieces)
    starts = [sum(sizes[:i]) for i in range(5)]
    fill = lambda array: jnp.pad(
        array, [(0, 0)] * (array.ndim - 1) + [(0, HALF - array.shape[-1])]
    )
    own = fill(jnp.concatenate([piece.T for piece in pieces], axis=0))
    feed_own = fill(
        jnp.stack(
            [piece.T.reshape(CHUNKS, ROWS, -1) for piece in (gate_weight, up_weight, down_weight)],
            axis=1,
        ).reshape(CHUNKS, 3 * ROWS, -1)
    )
    gain_a = halves(attn_gain[None, :], model)
    gain_f = halves(ffn_gain[None, :], model)
    cosine, sine = rotary(tokens)
    (
        _, weights, output, gate, up, qkv_weight, full_out, state, normed_a, scale_a, queries, keys,
        values, log_sum, hidden_state, mixed, normed_f, scale_f,
    ) = start_call(
        model, sizes, own, feed_own, block_input.swapaxes(1, 2), gain_a, gain_f, cosine, sine
    )
    first_kept = (
        state, normed_a, scale_a, queries, keys, values, log_sum, hidden_state, mixed,
        normed_f, scale_f, gate, up,
    )

    def pick(array, index):
        return lax.dynamic_index_in_dim(array, index, 0, keepdims=False)

    state, cotangent = lax.optimization_barrier((output, cotangent))
    cotangent = cotangent.swapaxes(1, 2)
    grad_other = lax.ppermute(pick(cotangent, 1 - y), "narrow", flip)
    normed_a, scale_a, queries, keys, values = qkv_call(
        model, state, gain_a, qkv_weight, cosine, sine
    )
    mixed, log_sum = attend_call(queries, keys, values)
    final, hidden_state, normed_f, scale_f, gate, up = feed_call(
        model, state, mixed, full_out, gain_f, weights
    )
    final_got = lax.ppermute(pick(final, 1 - y), "narrow", flip)

    grad_state, gain_f_two, grad_low, low_state, grad_mixed, *units = feed_back_call(
        model, (cotangent, grad_other), hidden_state, gain_f, scale_f, full_out, gate, up, weights
    )
    feed_two = (grad_low, normed_f, units[2], units[0], units[1])
    grad_queries, grad_keys, grad_values = attend_back_call(
        queries, keys, values, log_sum, grad_mixed
    )
    grad, gain_a_two, back = qkv_back_call(
        model, grad_queries, grad_keys, grad_values, state, scale_a, grad_state, gain_a, qkv_weight,
        cosine, sine,
    )
    attn_term = attn_terms_call(
        model, sizes, back, normed_a, low_state, mixed.reshape(H * HD, tokens)
    )

    (
        state, normed_a, scale_a, queries, keys, values, log_sum, hidden_state, mixed,
        normed_f, scale_f, gate, up,
    ) = first_kept
    grad_state, gain_f_one, grad_low, low_state, grad_mixed, *units = feed_back_call(
        model, (grad,), hidden_state, gain_f, scale_f, full_out, gate, up, weights
    )
    feed_one = (grad_low, normed_f, units[2], units[0], units[1])
    operands = [array for pair in zip(feed_one, feed_two) for array in pair]
    feed_sums, grad_mine, grad_got, gain_a_one, attn_term = finish_call(
        model, sizes, operands, grad_state, grad_mixed, low_state, queries, keys, values, log_sum, state,
        scale_a,
        gain_a, qkv_weight, cosine, sine, normed_a, mixed.reshape(H * HD, tokens), attn_term,
    )
    gains = jnp.concatenate([gain_a_one + gain_a_two, gain_f_one + gain_f_two], axis=0)
    attn_sums, gains = last_call(attn_term, gains)

    def placed(mine, theirs):
        theirs = theirs.astype(mine.dtype)
        return jnp.where(y == 0, jnp.stack([mine, theirs]), jnp.stack([theirs, mine])).swapaxes(1, 2)

    block_output = placed(pick(final, y), final_got)
    input_grad = placed(grad_mine, grad_got)
    gains = joined(gains, model)
    feed_sums = feed_sums[:, :, : model // 2].reshape(CHUNKS, 3, ROWS, -1)
    feed_sums = [feed_sums[:, t].reshape(PIECE, -1).T for t in range(3)]
    attn_sums = attn_sums.reshape(PIECE, HALF)
    attn_sums = [attn_sums[starts[i] : starts[i + 1], : model // 2].T for i in range(4)]
    return (
        block_output, input_grad, gains[0], gains[1], *attn_sums,
        *feed_sums,
    )


def rms_scale(values):
    return lax.rsqrt(jnp.mean(values * values, axis=-1, keepdims=True) + 1e-05)


def rotary_tables(count, first_row):
    positions = (first_row + jnp.arange(count, dtype=jnp.int32)).astype(jnp.float32)
    exponent = jnp.arange(HD // 2, dtype=jnp.int32).astype(jnp.float32) * (2.0 / HD)
    frequency = 10000.0 ** (-exponent)
    angles = positions[:, None] * frequency[None, :]
    return (jnp.cos(angles), jnp.sin(angles))


def rotate(values, cosine, sine_table):
    half_size = values.shape[-1] // 2
    first_half = values[..., :half_size]
    second_half = values[..., half_size:]
    return jnp.concatenate(
        [
            first_half * cosine - second_half * sine_table,
            second_half * cosine + first_half * sine_table,
        ],
        axis=-1,
    )


def rotate_back(values, cosine, sine_table):
    half_size = values.shape[-1] // 2
    first_half = values[..., :half_size]
    second_half = values[..., half_size:]
    return jnp.concatenate(
        [
            first_half * cosine + second_half * sine_table,
            second_half * cosine - first_half * sine_table,
        ],
        axis=-1,
    )


def contract_last(left, right):
    return lax.dot_general(
        left, right, (((1,), (1,)), ((), ())), preferred_element_type=jnp.float32
    )


def norm_back(upstream, values, inv_rms, norm_gain):
    gain_grad = jnp.sum(upstream * values * inv_rms, axis=0)
    scaled_up = upstream * norm_gain
    inner_mean = jnp.mean(scaled_up * values, axis=-1, keepdims=True)
    return (gain_grad, inv_rms * scaled_up - values * (inv_rms * inv_rms * inv_rms) * inner_mean)


def fetch_weights(
    query_weight, key_weight, value_weight, out_weight, gate_weight, up_weight, down_weight
):
    columns = (
        lax.all_gather(query_weight, "wide", axis=1, tiled=True),
        lax.all_gather(key_weight, "wide", axis=1, tiled=True),
        lax.all_gather(value_weight, "wide", axis=1, tiled=True),
        lax.all_gather(out_weight, "wide", axis=1, tiled=True),
        lax.all_gather(gate_weight, "wide", axis=1, tiled=True),
        lax.all_gather(up_weight, "wide", axis=1, tiled=True),
        lax.all_gather(down_weight, "wide", axis=1, tiled=True),
    )
    return (
        lax.all_gather(columns[0], "narrow", axis=0, tiled=True),
        lax.all_gather(columns[1], "narrow", axis=0, tiled=True),
        lax.all_gather(columns[2], "narrow", axis=0, tiled=True),
        lax.all_gather(columns[3], "narrow", axis=0, tiled=True),
        lax.all_gather(columns[4], "narrow", axis=0, tiled=True),
        lax.all_gather(columns[5], "narrow", axis=0, tiled=True),
        lax.all_gather(columns[6], "narrow", axis=0, tiled=True),
    )


def forward_run(run_input, attn_gain, ffn_gain, weights, cosine, sine_table, first_row):
    query_weight, key_weight, value_weight, out_weight, gate_weight, up_weight, down_weight = (
        weights
    )
    row_count = run_input.shape[0]
    groups = H // KV
    attn_scale = rms_scale(run_input)
    normed_attn = (run_input * attn_scale * attn_gain).astype(jnp.bfloat16)
    query_pre = jnp.dot(normed_attn, query_weight, preferred_element_type=jnp.float32).reshape(
        row_count, KV, groups, HD
    )
    queries = rotate(query_pre, cosine[:, None, None, :], sine_table[:, None, None, :]).astype(
        jnp.bfloat16
    )
    key_pre = jnp.dot(normed_attn, key_weight, preferred_element_type=jnp.float32).reshape(
        row_count, KV, HD
    )
    keys_local = (
        rotate(key_pre, cosine[:, None, :], sine_table[:, None, :])
        .astype(jnp.bfloat16)
        .reshape(row_count, KV * HD)
    )
    values_local = jnp.dot(normed_attn, value_weight, preferred_element_type=jnp.float32).astype(
        jnp.bfloat16
    )
    keys_all, values_all = (
        lax.all_gather(keys_local, "narrow", axis=0, tiled=True),
        lax.all_gather(values_local, "narrow", axis=0, tiled=True),
    )
    length = keys_all.shape[0]
    keys_all = keys_all.reshape(length, KV, HD)
    values_all = values_all.reshape(length, KV, HD)
    attn_score = jnp.einsum(
        "rgjd,pgd->gjrp", queries, keys_all, preferred_element_type=jnp.float32
    ) * HD ** (-0.5)
    visible = (first_row + jnp.arange(row_count, dtype=jnp.int32))[:, None] >= jnp.arange(
        length, dtype=jnp.int32
    )[None, :]
    attn_score = jnp.where(visible, attn_score, -jnp.inf)
    row_peak = jnp.max(attn_score, axis=-1, keepdims=True)
    weight_exp = jnp.exp(attn_score - row_peak)
    attn_probs = weight_exp / jnp.sum(weight_exp, axis=-1, keepdims=True)
    probs_low = attn_probs.astype(jnp.bfloat16)
    mixed_heads = jnp.einsum(
        "gjrp,pgd->rgjd", probs_low, values_all, preferred_element_type=jnp.float32
    ).reshape(row_count, H * HD)
    mixed_low = mixed_heads.astype(jnp.bfloat16)
    hidden_state = run_input + jnp.dot(mixed_low, out_weight, preferred_element_type=jnp.float32)
    ffn_scale = rms_scale(hidden_state)
    normed_ffn = (hidden_state * ffn_scale * ffn_gain).astype(jnp.bfloat16)
    gate_proj = jnp.dot(normed_ffn, gate_weight, preferred_element_type=jnp.float32)
    up_proj = jnp.dot(normed_ffn, up_weight, preferred_element_type=jnp.float32)
    hidden = (gate_proj / (1.0 + jnp.exp(-gate_proj)) * up_proj).astype(jnp.bfloat16)
    run_output = hidden_state + contract_last(hidden, down_weight)
    saved_parts = (
        attn_scale,
        normed_attn,
        queries,
        keys_all,
        values_all,
        attn_probs,
        probs_low,
        mixed_low,
        hidden_state,
        ffn_scale,
        normed_ffn,
        gate_proj,
        up_proj,
        hidden,
    )
    return (run_output, saved_parts)


def backward_run(
    grad_out, run_input, saved_parts, attn_gain, ffn_gain, weights, cosine, sine_table
):
    query_weight, key_weight, value_weight, out_weight, gate_weight, up_weight, down_weight = (
        weights
    )
    (
        attn_scale,
        normed_attn,
        queries,
        keys_all,
        values_all,
        attn_probs,
        probs_low,
        mixed_low,
        hidden_state,
        ffn_scale,
        normed_ffn,
        gate_proj,
        up_proj,
        hidden,
    ) = saved_parts
    row_count = run_input.shape[0]
    length = keys_all.shape[0]
    groups = H // KV
    grad_low = grad_out.astype(jnp.bfloat16)
    down_term = jnp.einsum("td,tf->df", grad_low, hidden, preferred_element_type=jnp.float32)
    grad_hidden = jnp.dot(grad_low, down_weight, preferred_element_type=jnp.float32)
    sigmoid_gate = 1.0 / (1.0 + jnp.exp(-gate_proj))
    grad_gate = (
        grad_hidden * up_proj * sigmoid_gate * (1.0 + gate_proj * (1.0 - sigmoid_gate))
    ).astype(jnp.bfloat16)
    grad_up = (grad_hidden * gate_proj * sigmoid_gate).astype(jnp.bfloat16)
    gate_term = jnp.einsum("td,tf->df", normed_ffn, grad_gate, preferred_element_type=jnp.float32)
    up_term = jnp.einsum("td,tf->df", normed_ffn, grad_up, preferred_element_type=jnp.float32)
    grad_normed_ffn = contract_last(grad_gate, gate_weight) + contract_last(grad_up, up_weight)
    ffn_gain_term, grad_through = norm_back(grad_normed_ffn, hidden_state, ffn_scale, ffn_gain)
    grad_state = grad_out + grad_through
    branch_low = grad_state.astype(jnp.bfloat16)
    out_term = jnp.einsum("tc,td->cd", mixed_low, branch_low, preferred_element_type=jnp.float32)
    grad_mixed = (
        contract_last(branch_low, out_weight)
        .astype(jnp.bfloat16)
        .reshape(row_count, KV, groups, HD)
    )
    grad_probs = jnp.einsum(
        "rgjd,pgd->gjrp", grad_mixed, values_all, preferred_element_type=jnp.float32
    )
    row_delta = jnp.sum(attn_probs * grad_probs, axis=-1, keepdims=True)
    grad_score = (attn_probs * (grad_probs - row_delta)).astype(jnp.bfloat16)
    grad_queries = jnp.einsum(
        "gjrp,pgd->rgjd", grad_score, keys_all, preferred_element_type=jnp.float32
    ) * HD ** (-0.5)
    grad_keys = jnp.einsum(
        "gjrp,rgjd->pgd", grad_score, queries, preferred_element_type=jnp.float32
    ) * HD ** (-0.5)
    grad_values = jnp.einsum(
        "gjrp,rgjd->pgd", probs_low, grad_mixed, preferred_element_type=jnp.float32
    )
    key_grads, value_grads = (
        lax.psum_scatter(
            grad_keys.reshape(length, KV * HD).astype(jnp.bfloat16),
            "narrow",
            scatter_dimension=0,
            tiled=True,
        ).astype(jnp.float32),
        lax.psum_scatter(
            grad_values.reshape(length, KV * HD).astype(jnp.bfloat16),
            "narrow",
            scatter_dimension=0,
            tiled=True,
        ).astype(jnp.float32),
    )
    query_back = (
        rotate_back(grad_queries, cosine[:, None, None, :], sine_table[:, None, None, :])
        .reshape(row_count, H * HD)
        .astype(jnp.bfloat16)
    )
    key_back = (
        rotate_back(
            key_grads.reshape(row_count, KV, HD), cosine[:, None, :], sine_table[:, None, :]
        )
        .reshape(row_count, KV * HD)
        .astype(jnp.bfloat16)
    )
    value_back = value_grads.astype(jnp.bfloat16)
    query_term = jnp.einsum(
        "td,tc->dc", normed_attn, query_back, preferred_element_type=jnp.float32
    )
    key_term = jnp.einsum("td,tc->dc", normed_attn, key_back, preferred_element_type=jnp.float32)
    value_term = jnp.einsum(
        "td,tc->dc", normed_attn, value_back, preferred_element_type=jnp.float32
    )
    grad_normed_attn = (
        contract_last(query_back, query_weight)
        + contract_last(key_back, key_weight)
        + contract_last(value_back, value_weight)
    )
    attn_gain_term, grad_norm_input = norm_back(grad_normed_attn, run_input, attn_scale, attn_gain)
    grad_input = grad_state + grad_norm_input
    return (
        grad_input,
        (attn_gain_term, ffn_gain_term),
        (query_term, key_term, value_term, out_term, gate_term, up_term, down_term),
    )


def on_device_parts(
    block_input,
    cotangent,
    attn_gain,
    ffn_gain,
    query_weight,
    key_weight,
    value_weight,
    out_weight,
    gate_weight,
    up_weight,
    down_weight,
):
    seq_count = block_input.shape[0]
    row_count = block_input.shape[1]
    first_row = lax.axis_index("narrow") * row_count
    cosine, sine_table = rotary_tables(row_count, first_row)

    def current():
        return fetch_weights(
            query_weight, key_weight, value_weight, out_weight, gate_weight, up_weight, down_weight
        )

    start_states = [block_input[item].astype(jnp.float32) for item in range(seq_count)]
    weights_now = current()
    middle_states = [
        forward_run(state, attn_gain, ffn_gain, weights_now, cosine, sine_table, first_row)[0]
        for state in start_states
    ]
    weights_now = current()
    final_states = [
        forward_run(state, attn_gain, ffn_gain, weights_now, cosine, sine_table, first_row)[0]
        for state in middle_states
    ]
    grad_states = [cotangent[item].astype(jnp.float32) for item in range(seq_count)]
    gain_local = None
    weight_local = None
    for run_inputs in (middle_states, start_states):
        weights_now = current()
        next_grads = []
        for item in range(seq_count):
            recomputed, saved_parts = forward_run(
                run_inputs[item], attn_gain, ffn_gain, weights_now, cosine, sine_table, first_row
            )
            grad_input, gain_parts, weight_parts = backward_run(
                grad_states[item],
                run_inputs[item],
                saved_parts,
                attn_gain,
                ffn_gain,
                weights_now,
                cosine,
                sine_table,
            )
            next_grads.append(grad_input)
            if gain_local is None:
                gain_local = gain_parts
                weight_local = weight_parts
            else:
                gain_local = jax.tree.map(jnp.add, gain_local, gain_parts)
                weight_local = jax.tree.map(jnp.add, weight_local, weight_parts)
        grad_states = next_grads
    across = (
        lax.psum_scatter(
            weight_local[0].astype(jnp.bfloat16), "wide", scatter_dimension=1, tiled=True
        ).astype(jnp.float32),
        lax.psum_scatter(
            weight_local[1].astype(jnp.bfloat16), "wide", scatter_dimension=1, tiled=True
        ).astype(jnp.float32),
        lax.psum_scatter(
            weight_local[2].astype(jnp.bfloat16), "wide", scatter_dimension=1, tiled=True
        ).astype(jnp.float32),
        lax.psum_scatter(
            weight_local[3].astype(jnp.bfloat16), "wide", scatter_dimension=1, tiled=True
        ).astype(jnp.float32),
        lax.psum_scatter(
            weight_local[4].astype(jnp.bfloat16), "wide", scatter_dimension=1, tiled=True
        ).astype(jnp.float32),
        lax.psum_scatter(
            weight_local[5].astype(jnp.bfloat16), "wide", scatter_dimension=1, tiled=True
        ).astype(jnp.float32),
        lax.psum_scatter(
            weight_local[6].astype(jnp.bfloat16), "wide", scatter_dimension=1, tiled=True
        ).astype(jnp.float32),
    )
    reduced = (
        lax.psum_scatter(
            across[0].astype(jnp.bfloat16), "narrow", scatter_dimension=0, tiled=True
        ).astype(jnp.float32),
        lax.psum_scatter(
            across[1].astype(jnp.bfloat16), "narrow", scatter_dimension=0, tiled=True
        ).astype(jnp.float32),
        lax.psum_scatter(
            across[2].astype(jnp.bfloat16), "narrow", scatter_dimension=0, tiled=True
        ).astype(jnp.float32),
        lax.psum_scatter(
            across[3].astype(jnp.bfloat16), "narrow", scatter_dimension=0, tiled=True
        ).astype(jnp.float32),
        lax.psum_scatter(
            across[4].astype(jnp.bfloat16), "narrow", scatter_dimension=0, tiled=True
        ).astype(jnp.float32),
        lax.psum_scatter(
            across[5].astype(jnp.bfloat16), "narrow", scatter_dimension=0, tiled=True
        ).astype(jnp.float32),
        lax.psum_scatter(
            across[6].astype(jnp.bfloat16), "narrow", scatter_dimension=0, tiled=True
        ).astype(jnp.float32),
    )
    gain_totals = lax.psum((gain_local[0], gain_local[1]), ("wide", "narrow"))
    block_output = jnp.stack(final_states).astype(jnp.bfloat16)
    input_grad = jnp.stack(grad_states)
    return (
        block_output,
        input_grad,
        gain_totals[0],
        gain_totals[1],
        reduced[0],
        reduced[1],
        reduced[2],
        reduced[3],
        reduced[4],
        reduced[5],
        reduced[6],
    )


def on_device(block_input, *rest):
    pieces = sum(weight.shape[1] for weight in rest[3:7])
    fits = (
        (lax.axis_size("wide"), lax.axis_size("narrow")) == (16, 2)
        and block_input.shape[0] == 2
        and block_input.shape[2] <= WIDE
        and {pieces, rest[7].shape[1], rest[8].shape[1], rest[9].shape[1]} == {PIECE}
    )
    plan = on_device_whole if fits else on_device_parts
    return plan(block_input, *rest)


def solution(mesh):
    placed = (
        P("wide", "narrow", None),
        P("wide", "narrow", None),
        P(),
        P(),
        P("narrow", "wide"),
        P("narrow", "wide"),
        P("narrow", "wide"),
        P("narrow", "wide"),
        P("narrow", "wide"),
        P("narrow", "wide"),
        P("narrow", "wide"),
    )
    return jax.shard_map(
        on_device,
        mesh=mesh,
        in_specs=placed,
        out_specs=(
            P("wide", "narrow", None),
            P("wide", "narrow", None),
            P(),
            P(),
            P("narrow", "wide"),
            P("narrow", "wide"),
            P("narrow", "wide"),
            P("narrow", "wide"),
            P("narrow", "wide"),
            P("narrow", "wide"),
            P("narrow", "wide"),
        ),
        check_vma=False,
    )
```

```python
import functools

import jax
import jax.numpy as jnp
import numpy as np
from jax import lax
from jax.experimental import pallas as pl
from jax.experimental.pallas import tpu as pltpu
from jax.sharding import PartitionSpec as P

H = 15
KV = 5
HD = 64
MESH = pl.DeviceIdType.MESH
F32 = jnp.float32
BF16 = jnp.bfloat16
GROUP = H // KV
PIECE = 160
CHUNKS = 5
ROWS = PIECE // CHUNKS
UNITS = 16 * ROWS
HALF = 512
WIDE = 2 * HALF
KEY_AT = H * HD
VALUE_AT = KEY_AT + KV * HD
QKV = VALUE_AT + KV * HD
VMEM_LIMIT = 62 << 20


def nt(left, right):
    return lax.dot_general(left, right, (((1,), (1,)), ((), ())), preferred_element_type=F32)


def nn(left, right):
    return jnp.dot(left, right, preferred_element_type=F32)


def tn(left, right):
    return lax.dot_general(left, right, (((0,), (0,)), ((), ())), preferred_element_type=F32)


def whole(*shape):
    return pl.BlockSpec(shape, lambda *_: (0,) * len(shape), pipeline_mode=pl.Buffered(1))


def compiler(**more):
    return pltpu.CompilerParams(vmem_limit_bytes=VMEM_LIMIT, **more)


def cost(flops, moved):
    return pl.CostEstimate(flops=int(flops), bytes_accessed=int(moved), transcendentals=0)


def span(ref, rows):
    return ref.at[..., pl.ds(rows[0], rows[1] - rows[0]), :]


class Place:
    def __init__(self):
        self.w = lax.axis_index("wide")
        self.y = lax.axis_index("narrow")
        self.z = self.w // 4
        self.x = (self.w // 2) % 2
        self.c = self.w % 2
        self.sibling = (self.w + 1 - 2 * self.c, self.y)

    def partners(self, dim):
        if dim == "x":
            return [(1 - self.x, (self.w + 2 - 4 * self.x, self.y))]
        if dim == "y":
            return [(1 - self.y, (self.w, 1 - self.y))]
        others = [(self.z + far) % 4 for far in (1, 2, 3)]
        return [(other, (self.w + 4 * (other - self.z), self.y)) for other in others]

    def origins(self, dim):
        if dim == "z":
            return [(self.z + far) % 4 for far in (3, 2, 1)]
        return [1 - getattr(self, dim)]

    def everyone(self):
        return [self.sibling] + [device for dim in "xyz" for _, device in self.partners(dim)]


def greet(devices):
    barrier = pltpu.get_barrier_semaphore()
    for device in devices:
        pl.semaphore_signal(barrier, inc=1, device_id=device, device_id_type=MESH)
    pl.semaphore_wait(barrier, len(devices))


def remote(source, target, send_sem, recv_sem, device):
    return pltpu.make_async_remote_copy(
        src_ref=source,
        dst_ref=target,
        send_sem=send_sem,
        recv_sem=recv_sem,
        device_id=device,
        device_id_type=MESH,
    )


STEPS = 3


class Gather:
    def __init__(self, me, flows, own, full, keep_sem, send, recv, cross_send, cross_recv):
        self.me, self.flows, self.own, self.full = me, flows, own, full
        self.keep_sem, self.send, self.recv = keep_sem, send, recv
        self.cross_send, self.cross_recv = cross_send, cross_recv

    def keep(self, t):
        me = self.me
        return pltpu.make_async_copy(
            self.own[t], self.full[t].at[me.y, me.z, me.x, me.c], self.keep_sem.at[t]
        )

    def blocks(self, t, flow, step, place):
        me = self.me
        rows, order = self.flows[t][flow]
        at = {"y": me.y, "z": me.z, "x": me.x}
        for name in order[:step]:
            at[name] = slice(None)
        at[order[step]] = place
        return span(self.full[t].at[at["y"], at["z"], at["x"], me.c], rows)

    def copies(self, t, flow, step):
        me = self.me
        rows, order = self.flows[t][flow]
        dim = order[step]
        target = self.blocks(t, flow, step, getattr(me, dim))
        source = span(self.own[t], rows) if step == 0 else target
        return [
            remote(
                source, target, self.send.at[t, flow, step, i], self.recv.at[t, flow, step, i], device
            )
            for i, (_, device) in enumerate(me.partners(dim))
        ]

    def landing(self, t, flow, step):
        me = self.me
        dim = self.flows[t][flow][1][step]
        devices = me.partners(dim)
        blocks = [self.blocks(t, flow, step, place) for place in me.origins(dim)]
        return [
            remote(
                block, block, self.send.at[t, flow, step, i], self.recv.at[t, flow, step, i],
                devices[i][1],
            )
            for i, block in enumerate(blocks)
        ]

    def cross(self, t, flow):
        blocks = span(self.full[t].at[:, :, :, self.me.c], self.flows[t][flow][0])
        return remote(
            blocks, blocks, self.cross_send.at[t, flow], self.cross_recv.at[t, flow],
            self.me.sibling,
        )

    def stage(self, t, step):
        count = len(self.flows[t])
        if step == 0:
            self.keep(t).start()
        if step == 1:
            self.keep(t).wait()
        for flow in range(count):
            if 0 < step <= STEPS:
                for copy in self.landing(t, flow, step - 1):
                    copy.wait_recv()
            if step < STEPS:
                for copy in self.copies(t, flow, step):
                    copy.start()
            if step == STEPS:
                self.cross(t, flow).start()
            if step == STEPS + 1:
                self.cross(t, flow).wait()
                for before in range(STEPS):
                    for copy in self.copies(t, flow, before):
                        copy.wait_send()

    @staticmethod
    def semaphores(types, flows):
        dma = pltpu.SemaphoreType.DMA
        return [
            dma((types,)), dma((types, flows, STEPS, 3)), dma((types, flows, STEPS, 3)),
            dma((types, flows)), dma((types, flows)),
        ]


class Scatter:
    def __init__(self, me, flows, terms, out, scratch):
        self.me, self.flows, self.terms, self.out = me, flows, terms, out
        (
            self.acc, self.arrived, self.load_sem, self.cross_send, self.cross_recv, self.send,
            self.recv, *self.buffers,
        ) = scratch
        self.piece = self.acc.shape[-2]

    @staticmethod
    def scratch(flows, piece):
        dma = pltpu.SemaphoreType.DMA
        types, count = len(flows), len(flows[0])
        refs = [
            pltpu.VMEM((types, 2, 4, 2, piece, HALF), BF16),
            pltpu.VMEM((types, 2, 4, 2, piece, HALF), BF16),
            dma((types,)), dma((types,)), dma((types,)),
            dma((types, count, STEPS, 3)), dma((types, count, STEPS, 3)),
        ]
        for own_flows in flows:
            for rows, order in own_flows:
                for step, dim in enumerate(order):
                    left = order[step + 1 :]
                    shape = tuple({"y": 2, "z": 4, "x": 2}[name] for name in "yzx" if name in left)
                    lines = (3 if dim == "z" else 1,)
                    refs.append(pltpu.VMEM(lines + shape + (rows[1] - rows[0], HALF), BF16))
        return refs

    def buffer(self, t, flow, step):
        return self.buffers[(t * len(self.flows[0]) + flow) * STEPS + step]

    def source(self, t, core):
        ref, first = self.terms[t]
        return span(ref.at[:, :, :, core], (first, first + self.piece))

    def cross(self, t):
        return remote(
            self.source(t, 1 - self.me.c), self.arrived.at[t], self.cross_send.at[t],
            self.cross_recv.at[t], self.me.sibling,
        )

    def load(self, t):
        return pltpu.make_async_copy(
            self.source(t, self.me.c), self.acc.at[t], self.load_sem.at[t]
        )

    def blocks(self, t, flow, step, place):
        rows, order = self.flows[t][flow]
        at = {"y": slice(None), "z": slice(None), "x": slice(None)}
        for name in order[:step]:
            at[name] = getattr(self.me, name)
        at[order[step]] = place
        return span(self.acc.at[t, at["y"], at["z"], at["x"]], rows)

    def copies(self, t, flow, step):
        buffer = self.buffer(t, flow, step)
        return [
            remote(
                self.blocks(t, flow, step, place), buffer.at[i], self.send.at[t, flow, step, i],
                self.recv.at[t, flow, step, i], device,
            )
            for i, (place, device) in enumerate(self.me.partners(self.flows[t][flow][1][step]))
        ]

    def take(self, t, flow, step):
        copies = self.copies(t, flow, step)
        for copy in copies:
            copy.wait_recv()
        target = self.blocks(t, flow, step, getattr(self.me, self.flows[t][flow][1][step]))
        buffer = self.buffer(t, flow, step)

        def add(*index):
            value = target.at[index][...] if index else target[...]
            for i in range(len(copies)):
                value = value + buffer.at[(i,) + index][...]
            if index:
                target.at[index][...] = value
            else:
                target[...] = value

        if len(target.shape) == 2:
            add()
        else:

            @pl.loop(0, target.shape[0])
            def _(index):
                add(index)

    def stage(self, t, step):
        flows = range(len(self.flows[t]))
        if step == 0:
            self.cross(t).start()
            self.load(t).start()
        if step == 1:
            self.load(t).wait()
            self.cross(t).wait()

            @pl.loop(0, 8)
            def _(index):
                half, block = index // 4, index % 4
                self.acc[t, half, block] = self.acc[t, half, block] + self.arrived[t, half, block]

        for flow in flows:
            if step > 2:
                self.take(t, flow, step - 3)
            if 2 <= step <= STEPS + 1:
                for copy in self.copies(t, flow, step - 2):
                    copy.start()
        if step == STEPS + 2:
            me = self.me
            for flow in flows:
                for before in range(STEPS):
                    for copy in self.copies(t, flow, before):
                        copy.wait_send()
            self.out[t] = self.acc[t, me.y, me.z, me.x].astype(F32)


def staggered(types, stages, gap=1):
    ticks = stages + gap * (types - 1)
    return [
        [(t, tick - gap * t) for t in range(types) if 0 <= tick - gap * t < stages]
        for tick in range(ticks)
    ]


def widen(turned, half, model):
    size = model // 2
    part = turned[half * size : (half + 1) * size, :].astype(F32)
    fill = jnp.zeros((HALF - size, part.shape[1]), F32)
    return jnp.concatenate([part, fill], axis=0).T


def narrow(value, half, model):
    return value[:, half * HALF : (half + 1) * HALF].T[: model // 2]


def turn_head(rows, cos, sin, back=False):
    first, second = rows[: HD // 2], rows[HD // 2 :]
    if back:
        return first * cos + second * sin, second * cos - first * sin
    return first * cos - second * sin, second * cos + first * sin


def qkv_kernel(model, state, gain, weight, cosine, sine, normed, scale, queries, keys, values):
    inputs = state[...]
    inv = lax.rsqrt(jnp.sum(inputs * inputs, axis=-1, keepdims=True) * (1.0 / model) + 1e-05)
    scale[...] = inv
    low = (inputs * inv * gain[...]).astype(BF16)
    normed[...] = low
    left, right = low[:, :HALF], low[:, HALF:]
    cos, sin = cosine[...], sine[...]
    count = KV * HD
    for first in range(0, QKV, count):
        rows = pl.ds(first, count)
        pre = nt(weight[0, rows, :], left) + nt(weight[1, rows, :], right)
        for index in range(KV):
            part = pre[index * HD : (index + 1) * HD]
            if first >= VALUE_AT:
                values[index] = part.astype(BF16)
                continue
            top, bottom = turn_head(part, cos, sin)
            if first < KEY_AT:
                head = first // HD + index
                queries[head, : HD // 2, :] = (top * HD ** (-0.5)).astype(BF16)
                queries[head, HD // 2 :, :] = (bottom * HD ** (-0.5)).astype(BF16)
            else:
                keys[index, : HD // 2, :] = top.astype(BF16)
                keys[index, HD // 2 :, :] = bottom.astype(BF16)


def qkv_call(model, state, gain, weight, cosine, sine, rows=512):
    tokens = state.shape[0]
    by_row = lambda width: pl.BlockSpec((rows, width), lambda i: (i, 0))
    by_lane = pl.BlockSpec((HD // 2, rows), lambda i: (0, i))
    heads = lambda count: pl.BlockSpec((count, HD, rows), lambda i: (0, 0, i))
    return pl.pallas_call(
        functools.partial(qkv_kernel, model),
        grid=(tokens // rows,),
        in_specs=[by_row(WIDE), whole(1, WIDE), whole(2, QKV, HALF), by_lane, by_lane],
        out_specs=[by_row(WIDE), by_row(1), heads(H), heads(KV), heads(KV)],
        out_shape=[
            jax.ShapeDtypeStruct((tokens, WIDE), BF16),
            jax.ShapeDtypeStruct((tokens, 1), F32),
            jax.ShapeDtypeStruct((H, HD, tokens), BF16),
            jax.ShapeDtypeStruct((KV, HD, tokens), BF16),
            jax.ShapeDtypeStruct((KV, HD, tokens), BF16),
        ],
        compiler_params=compiler(),
        cost_estimate=cost(2 * tokens * WIDE * QKV, 20e6),
        name="project_qkv",
    )(state, gain, weight, cosine, sine)


def key_mask(block):
    row = lax.broadcasted_iota(jnp.int32, (block, GROUP * block), 0)
    column = lax.broadcasted_iota(jnp.int32, (block, GROUP * block), 1)
    return row <= jnp.bitwise_and(column, block - 1)


def group_block(ref, at, block):
    return jnp.concatenate([ref[head, :, at : at + block] for head in range(GROUP)], axis=1)


def ahead_of(items, count, make):
    pending = [make(item) for item in items[:count]]
    for turn, item in enumerate(items):
        if turn + count < len(items):
            pending.append(make(items[turn + count]))
        yield item, pending.pop(0)


def attend_kernel(block, ahead, queries, keys, values, mixed, log_sum):
    tokens = keys.shape[2]
    key_rows = keys[0].T

    def scores(at):
        query = group_block(queries, at, block)
        tiles = [nn(key_rows[first : first + block], query) for first in range(0, at + block, block)]
        tiles[-1] = jnp.where(key_mask(block), tiles[-1], -jnp.inf)
        return tiles

    for at, tiles in ahead_of(list(range(0, tokens, block)), ahead, scores):
        peak = functools.reduce(
            jnp.maximum, [jnp.max(tile, axis=0, keepdims=True) for tile in tiles]
        )
        total = out = 0.0
        for index, score in enumerate(tiles):
            weight = jnp.exp(score - peak)
            total = total + jnp.sum(weight, axis=0, keepdims=True)
            value = values[0, :, index * block : (index + 1) * block]
            out = out + nn(value, weight.astype(BF16))
        out = (out * (1.0 / total)).astype(BF16)
        logs = peak + jnp.log(total)
        for head in range(GROUP):
            part = slice(head * block, (head + 1) * block)
            mixed[head, :, at : at + block] = out[:, part]
            log_sum[head, :, at : at + block] = logs[:, part]


def attend_call(queries, keys, values, block=256):
    tokens = queries.shape[2]
    heads = lambda count: pl.BlockSpec((count, HD, tokens), lambda i: (i, 0, 0))
    return pl.pallas_call(
        functools.partial(attend_kernel, block, 3),
        grid=(KV,),
        in_specs=[heads(GROUP), heads(1), heads(1)],
        out_specs=[heads(GROUP), pl.BlockSpec((GROUP, 1, tokens), lambda i: (i, 0, 0))],
        out_shape=[
            jax.ShapeDtypeStruct((H, HD, tokens), BF16),
            jax.ShapeDtypeStruct((H, 1, tokens), F32),
        ],
        compiler_params=compiler(),
        cost_estimate=cost(4 * tokens * tokens * H * 128, 20e6),
        name="attend",
    )(queries, keys, values)


def attend_back_kernel(
    block, queries, keys, values, log_sum, grad_mixed, grad_queries, grad_keys, grad_values
):
    tokens = keys.shape[2]
    key_rows, value_rows = keys[0].T, values[0].T

    def products(at):
        query, grad = group_block(queries, at, block), group_block(grad_mixed, at, block)
        return [
            (
                nn(key_rows[first : first + block], query),
                nn(value_rows[first : first + block], grad),
            )
            for first in range(0, at + block, block)
        ]

    for at, tiles in ahead_of(list(range(tokens - block, -1, -block)), 1, products):
        query, grad = group_block(queries, at, block), group_block(grad_mixed, at, block)
        logs = group_block(log_sum, at, block)
        weights = []
        delta = 0.0
        for index, (score, grad_probs) in enumerate(tiles):
            probs = jnp.exp(score - logs)
            if index * block == at:
                probs = jnp.where(key_mask(block), probs, 0.0)
            delta = delta + jnp.sum(probs * grad_probs, axis=0, keepdims=True)
            weights.append(probs)
        by_query = 0.0
        for index, (_, grad_probs) in enumerate(tiles):
            part = pl.ds(index * block, block)
            probs = weights[index]
            low = (probs * (grad_probs - delta)).astype(BF16)
            by_query = by_query + nn(keys[0, :, part], low)
            key_part = nt(query, low)
            value_part = nt(grad, probs.astype(BF16))
            if at + block == tokens:
                grad_keys[0, :, part] = key_part
                grad_values[0, :, part] = value_part
            else:
                grad_keys[0, :, part] += key_part
                grad_values[0, :, part] += value_part
        for head in range(GROUP):
            grad_queries[head, :, at : at + block] = by_query[:, head * block : (head + 1) * block]


def attend_back_call(queries, keys, values, log_sum, grad_mixed, block=256):
    tokens = queries.shape[2]
    heads = lambda count: pl.BlockSpec((count, HD, tokens), lambda i: (i, 0, 0))
    return pl.pallas_call(
        functools.partial(attend_back_kernel, block),
        grid=(KV,),
        in_specs=[
            heads(GROUP), heads(1), heads(1),
            pl.BlockSpec((GROUP, 1, tokens), lambda i: (i, 0, 0)), heads(GROUP),
        ],
        out_specs=[heads(GROUP), heads(1), heads(1)],
        out_shape=[
            jax.ShapeDtypeStruct((H, HD, tokens), F32),
            jax.ShapeDtypeStruct((KV, HD, tokens), F32),
            jax.ShapeDtypeStruct((KV, HD, tokens), F32),
        ],
        compiler_params=compiler(),
        cost_estimate=cost(10 * tokens * tokens * H * 128, 30e6),
        name="attend_back",
    )(queries, keys, values, log_sum, grad_mixed)


GATHER_FLOWS = ((((0, 80), "zyx"), ((80, 128), "zxy"), ((128, 160), "yxz")),) + (
    (((0, 48), "zyx"), ((48, 80), "zxy"), ((80, 96), "yxz")),
) * CHUNKS


def row_pairs(sizes):
    pairs = []
    by_weight = first = 0
    for size in sizes:
        for device in range(4):
            pairs.append((device * PIECE + first, by_weight, size))
            by_weight += size
        first += size
    return pairs


def order_weights(model, sizes, raw, by_device, by_weight, qkv_weight, out_weight):
    counts = [4 * size for size in sizes]
    starts = [sum(counts[:i]) for i in range(4)]
    rows = 4 * PIECE
    size = model // 2
    blank = jnp.zeros((HALF - size, HALF), F32)
    for half in range(2):
        for pair in range(2):
            outs = []
            for z in (2 * pair, 2 * pair + 1):
                by_device[...] = raw[half, z * rows : (z + 1) * rows, :].astype(F32)
                for source, target, count in row_pairs(sizes):
                    by_weight[target : target + count, :] = by_device[source : source + count, :]
                done = by_weight[...]
                for i, first in enumerate((0, KEY_AT, VALUE_AT)):
                    at = first + z * counts[i]
                    part = done[starts[i] : starts[i] + counts[i]]
                    qkv_weight[half, at : at + counts[i], :] = part.astype(BF16)
                outs.append(done[starts[3] :])
            turned = jnp.concatenate(outs + [blank], axis=0).T
            out_weight[half * size : (half + 1) * size, pair * HALF : (pair + 1) * HALF] = turned[
                :size
            ].astype(BF16)


def sigmoid(value):
    return 0.5 * jnp.tanh(0.5 * value) + 0.5


def feed_block(gate_weight, up_weight, normed, rows, gate, up):
    left, right = normed[rows, :HALF], normed[rows, HALF:]
    gate_proj = nt(left, gate_weight[0]) + nt(right, gate_weight[1])
    up_proj = nt(left, up_weight[0]) + nt(right, up_weight[1])
    gate[rows, :] = gate_proj.astype(BF16)
    up[rows, :] = up_proj.astype(BF16)
    return (gate_proj * sigmoid(gate_proj) * up_proj).astype(BF16)


def out_block(model, state, mixed, out_weight, gain, hidden_state, normed, scale):
    heads = mixed[...].reshape(H * HD, mixed.shape[2])
    after = state[...] + tn(heads, out_weight[...])
    hidden_state[...] = after
    inv = lax.rsqrt(jnp.sum(after * after, axis=-1, keepdims=True) * (1.0 / model) + 1e-05)
    scale[...] = inv
    normed[...] = (after * inv * gain[...]).astype(BF16)


START_KINDS = lambda tokens, units: [
    ((2, QKV, HALF), BF16),
    ((H * HD, WIDE), BF16),
    ((tokens, WIDE), F32),
    ((tokens, WIDE), BF16),
    ((tokens, 1), F32),
    ((H, HD, tokens), BF16),
    ((KV, HD, tokens), BF16),
    ((KV, HD, tokens), BF16),
    ((H, 1, tokens), F32),
    ((tokens, WIDE), F32),
    ((H, HD, tokens), BF16),
    ((tokens, WIDE), BF16),
    ((tokens, 1), F32),
]


def feed_spec(t, first=0):
    return pl.BlockSpec(
        (None, 2, 4, 2, 2, ROWS, HALF), lambda i: (first + i, 0, 0, 0, 0, t, 0)
    )


def start_kernel(
    model, sizes, own, feed_own, seqs, gain, feed_gain, cosine, sine,
    full, feed_full, output_out, gate_out, up_out, *rest,
):
    kinds = len(START_KINDS(0, 0))
    outs_refs, rest = rest[:kinds], rest[kinds:]
    (
        qkv_weight, out_weight, state, normed, scale, queries, keys, values, log_sum, hidden_state,
        mixed, feed_normed, feed_scale,
    ), rest = rest[:kinds], rest[kinds:]
    seq, by_device, by_weight, seq_sem, raw_sem, out_sem, *gather_sems = rest
    me = Place()
    y = me.y
    gather = Gather(
        me, GATHER_FLOWS, [own] + [feed_own.at[i] for i in range(CHUNKS)],
        [full] + [feed_full.at[i] for i in range(CHUNKS)], *gather_sems,
    )
    greet(me.everyone())
    swap = remote(
        seqs.at[1 - y], seq.at[y], seq_sem.at[0], seq_sem.at[1], me.partners("y")[0][1]
    )
    swap.start()
    stay = pltpu.make_async_copy(seqs.at[y], seq.at[y], seq_sem.at[2])
    stay.start()
    ticks = staggered(1 + CHUNKS, STEPS + 2)

    def tick(*counts):
        for count in counts:
            for t, stage in ticks[count]:
                gather.stage(t, stage)

    tick(0, 1, 2)
    rows = seq.shape[2]
    tokens = 2 * rows
    outs = []

    def give(index, source):
        copy = pltpu.make_async_copy(source, outs_refs[index], out_sem.at[index])
        copy.start()
        outs.append(copy)

    stay.wait()
    swap.wait()
    for part in range(2):
        for half in range(2):
            state[part * rows : (part + 1) * rows, half * HALF : (half + 1) * HALF] = widen(
                seq.at[part], half, model
            )
    give(2, state)
    tick(3, 4)

    def put_in_order(raw):
        fetch = pltpu.make_async_copy(full, raw, raw_sem.at[0])
        fetch.start()
        fetch.wait()
        order_weights(
            model, sizes, raw.reshape(2, 16 * PIECE, HALF), by_device, by_weight, qkv_weight,
            out_weight,
        )

    pl.run_scoped(put_in_order, pltpu.VMEM((2, 4, 2, 2, PIECE, HALF), BF16))
    give(0, qkv_weight)
    give(1, out_weight)
    for at in range(0, tokens, rows):
        part = pl.ds(at, rows)
        qkv_kernel(
            model, state.at[part], gain, qkv_weight, cosine.at[:, part], sine.at[:, part],
            normed.at[part], scale.at[part], queries.at[:, :, part], keys.at[:, :, part],
            values.at[:, :, part],
        )
    give(3, normed)
    give(4, scale)
    give(5, queries)
    give(6, keys)
    give(7, values)
    tick(5)

    @pl.loop(0, KV)
    def _(group):
        some = pl.ds(group * GROUP, GROUP)
        one = pl.ds(group, 1)
        attend_kernel(
            tokens // 4, 1, queries.at[some], keys.at[one], values.at[one], mixed.at[some],
            log_sum.at[some],
        )
        pl.when(group == 1)(lambda: tick(6))
        pl.when(group == 4)(lambda: tick(7))

    give(8, log_sum)
    give(10, mixed)
    out_block(model, state, mixed, out_weight, feed_gain, hidden_state, feed_normed, feed_scale)
    give(9, hidden_state)
    give(11, feed_normed)
    give(12, feed_scale)

    outs[0].wait()
    state[...] = hidden_state[...]

    def feed_body(gate_weight, up_weight, down_weight, gate, up):
        gates, ups, downs = (
            ref.reshape(2, UNITS, HALF) for ref in (gate_weight, up_weight, down_weight)
        )
        for at in range(0, tokens, rows):
            part = pl.ds(at, rows)
            low = feed_block(gates, ups, feed_normed, part, gate, up)
            state[part, :HALF] += nn(low, downs[0])
            state[part, HALF:] += nn(low, downs[1])

    def feed_chunks(first, count):
        by_unit = pl.BlockSpec((tokens, UNITS), lambda i: (0, first + i))
        pltpu.emit_pipeline(
            feed_body,
            grid=(count,),
            in_specs=[feed_spec(t, first) for t in range(3)],
            out_specs=[by_unit, by_unit],
        )(feed_full, feed_full, feed_full, gate_out, up_out)

    tick(8)
    feed_chunks(0, 3)
    tick(9)
    feed_chunks(3, 2)
    last = pltpu.make_async_copy(state, output_out, raw_sem.at[0])
    last.start()
    for copy in outs[1:]:
        copy.wait()
    last.wait()


def start_call(model, sizes, own, feed_own, seqs, gain, feed_gain, cosine, sine):
    types = 1 + CHUNKS
    tokens = 2 * seqs.shape[2]
    units = 16 * PIECE
    kinds = START_KINDS(tokens, units)
    dma = pltpu.SemaphoreType.DMA
    anywhere = pl.BlockSpec(memory_space=pl.ANY)
    inside = pl.BlockSpec(memory_space=pltpu.VMEM)
    outs = [
        ((2, 4, 2, 2, PIECE, HALF), BF16),
        ((CHUNKS, 2, 4, 2, 2, 3 * ROWS, HALF), BF16),
        ((tokens, WIDE), F32),
        ((tokens, units), BF16),
        ((tokens, units), BF16),
    ] + kinds
    return pl.pallas_call(
        functools.partial(start_kernel, model, sizes),
        out_shape=[jax.ShapeDtypeStruct(*kind) for kind in outs],
        in_specs=[anywhere] * 3 + [inside] * 4,
        out_specs=[anywhere] * len(outs),
        scratch_shapes=[pltpu.VMEM(*kind) for kind in kinds]
        + [
            pltpu.VMEM(seqs.shape, BF16),
            pltpu.VMEM((4 * PIECE, HALF), F32),
            pltpu.VMEM((4 * PIECE, HALF), F32),
            dma((3,)), dma((1,)), dma((len(kinds),)),
        ]
        + Gather.semaphores(types, len(GATHER_FLOWS[0])),
        compiler_params=compiler(collective_id=0, has_side_effects=True),
        name="start",
    )(own, feed_own, seqs, gain, feed_gain, cosine, sine)


def feed_kernel(
    model, block, state, heads, out_weight, gain, gate_weight, up_weight, down_weight,
    final, hidden_state, normed, scale, gate, up, output,
):
    tokens = state.shape[0]

    @pl.when(pl.program_id(0) == 0)
    def _():
        out_block(model, state, heads, out_weight, gain, hidden_state, normed, scale)
        output[...] = hidden_state[...]

    gate_weight, up_weight, down_weight = (
        ref.reshape(2, UNITS, HALF) for ref in (gate_weight, up_weight, down_weight)
    )
    for at in range(0, tokens, block):
        rows = pl.ds(at, block)
        hidden = feed_block(gate_weight, up_weight, normed, rows, gate, up)
        output[rows, :HALF] += nn(hidden, down_weight[0])
        output[rows, HALF:] += nn(hidden, down_weight[1])

    @pl.when(pl.program_id(0) == pl.num_programs(0) - 1)
    def _():
        size = model // 2
        for part in range(2):
            value = output[part * tokens // 2 : (part + 1) * tokens // 2, :]
            for half in range(2):
                final[part, half * size : (half + 1) * size, :] = narrow(value, half, model).astype(
                    BF16
                )


def feed_call(model, state, heads, out_weight, gain, weights, block=512):
    tokens = state.shape[0]
    units = CHUNKS * UNITS
    by_unit = pl.BlockSpec((tokens, UNITS), lambda i: (0, i))
    return pl.pallas_call(
        functools.partial(feed_kernel, model, block),
        grid=(CHUNKS,),
        in_specs=[
            whole(tokens, WIDE), whole(H, HD, tokens), whole(H * HD, WIDE), whole(1, WIDE),
            feed_spec(0), feed_spec(1), feed_spec(2),
        ],
        out_specs=[
            whole(2, model, tokens // 2), whole(tokens, WIDE), whole(tokens, WIDE),
            whole(tokens, 1), by_unit, by_unit,
        ],
        out_shape=[
            jax.ShapeDtypeStruct((2, model, tokens // 2), BF16),
            jax.ShapeDtypeStruct((tokens, WIDE), F32),
            jax.ShapeDtypeStruct((tokens, WIDE), BF16),
            jax.ShapeDtypeStruct((tokens, 1), F32),
            jax.ShapeDtypeStruct((tokens, units), BF16),
            jax.ShapeDtypeStruct((tokens, units), BF16),
        ],
        scratch_shapes=[pltpu.VMEM((tokens, WIDE), F32)],
        compiler_params=compiler(),
        cost_estimate=cost(2 * tokens * WIDE * (3 * units + H * HD), 50e6),
        name="feed",
    )(state, heads, out_weight, gain, weights, weights, weights)


def feed_back_kernel(
    model, block, pair, *refs,
):
    step = pl.program_id(0)
    if pair:
        both, other, *refs = refs
        *refs, grad_out = refs
    else:
        grad_out, *refs = refs
    (
        hidden_from, gain, scale, out_from, gate, up, gate_weight, up_weight, down_weight,
        grad_state, gain_term, grad_low, branch_low, grad_mixed, grad_gate, grad_up, hidden,
        hidden_state, out_weight, load_sem,
    ) = refs
    tokens = grad_out.shape[0]
    loads = [
        pltpu.make_async_copy(hidden_from, hidden_state, load_sem.at[0]),
        pltpu.make_async_copy(out_from, out_weight, load_sem.at[1]),
    ]

    @pl.when(step == 0)
    def _():
        for load in loads:
            load.start()

    @pl.when(step == 0)
    def _():
        if pair:
            count = tokens // 2
            y = lax.axis_index("narrow")
            for place, turned in ((y, both.at[y]), (1 - y, other)):
                rows = pl.ds(pl.multiple_of(place * count, count), count)
                for half in range(2):
                    columns = pl.ds(half * HALF, HALF)
                    grad_out[rows, columns] = widen(turned, half, model)
        grad_low[...] = grad_out[...].astype(BF16)
        grad_state[...] = jnp.zeros_like(grad_state)

    gate_weight, up_weight, down_weight = (
        ref.reshape(2, UNITS, HALF) for ref in (gate_weight, up_weight, down_weight)
    )

    for at in range(0, tokens, block):
        rows = pl.ds(at, block)
        grad_hidden = nt(grad_low[rows, :HALF], down_weight[0]) + nt(
            grad_low[rows, HALF:], down_weight[1]
        )
        gate_proj = gate[rows, :].astype(F32)
        up_proj = up[rows, :].astype(F32)
        sig = sigmoid(gate_proj)
        passed = gate_proj * sig
        hidden[rows, :] = (passed * up_proj).astype(BF16)
        by_gate = (grad_hidden * up_proj * (sig + passed * (1.0 - sig))).astype(BF16)
        by_up = (grad_hidden * passed).astype(BF16)
        grad_gate[rows, :] = by_gate
        grad_up[rows, :] = by_up
        grad_state[rows, :HALF] += nn(by_gate, gate_weight[0]) + nn(by_up, up_weight[0])
        grad_state[rows, HALF:] += nn(by_gate, gate_weight[1]) + nn(by_up, up_weight[1])

    @pl.when(step == pl.num_programs(0) - 1)
    def _():
        for load in loads:
            load.wait()
        total = jnp.zeros(gain.shape, F32)
        for at in range(0, tokens, block):
            rows = pl.ds(at, block)
            grad, after, inv = grad_state[rows, :], hidden_state[rows, :], scale[rows, :]
            total = total + jnp.sum(grad * after * inv, axis=0, keepdims=True)
            upstream = grad * gain[...]
            inner = jnp.sum(upstream * after, axis=-1, keepdims=True) * (1.0 / model)
            result = grad_out[rows, :] + inv * upstream - after * (inv * inv * inv) * inner
            grad_state[rows, :] = result
            low = result.astype(BF16)
            branch_low[rows, :] = low
            part = nt(out_weight[...], low).astype(BF16)
            grad_mixed[:, :, rows] = part.reshape(H, HD, block)
        gain_term[...] = total


def feed_back_call(
    model, grads, hidden_state, gain, scale, out_weight, gate, up, weights, block=512
):
    tokens = hidden_state.shape[0]
    pair = len(grads) == 2
    units = CHUNKS * UNITS
    by_unit = pl.BlockSpec((tokens, UNITS), lambda i: (0, i))
    return pl.pallas_call(
        functools.partial(feed_back_kernel, model, block, pair),
        grid=(CHUNKS,),
        in_specs=[
            whole(*grad.shape) for grad in grads
        ]
        + [
            pl.BlockSpec(memory_space=pl.ANY), whole(1, WIDE), whole(tokens, 1),
            pl.BlockSpec(memory_space=pl.ANY), by_unit, by_unit, feed_spec(0), feed_spec(1), feed_spec(2),
        ],
        out_specs=[
            whole(tokens, WIDE), whole(1, WIDE), whole(tokens, WIDE), whole(tokens, WIDE),
            whole(H, HD, tokens),
        ]
        + [by_unit] * 3,
        out_shape=[
            jax.ShapeDtypeStruct((tokens, WIDE), F32),
            jax.ShapeDtypeStruct((1, WIDE), F32),
            jax.ShapeDtypeStruct((tokens, WIDE), BF16),
            jax.ShapeDtypeStruct((tokens, WIDE), BF16),
            jax.ShapeDtypeStruct((H, HD, tokens), BF16),
        ]
        + [jax.ShapeDtypeStruct((tokens, units), BF16)] * 3,
        scratch_shapes=[
            pltpu.VMEM((tokens, WIDE), F32),
            pltpu.VMEM((H * HD, WIDE), BF16),
            pltpu.SemaphoreType.DMA((2,)),
        ]
        + ([pltpu.VMEM((tokens, WIDE), F32)] if pair else []),
        compiler_params=compiler(),
        cost_estimate=cost(6 * tokens * WIDE * units, 60e6),
        name="feed_back",
    )(*grads, hidden_state, gain, scale, out_weight, gate, up, weights, weights, weights)


def qkv_back_rows(
    model, grad_queries, grad_keys, grad_values, state, scale, grad_state, gain, weight, cosine, sine,
    back,
):
    cos, sin = cosine[...], sine[...]
    for first, heads, factor in ((0, grad_queries, HD ** (-0.5)), (KEY_AT, grad_keys, 1.0)):
        for head in range(heads.shape[0]):
            at = first + head * HD
            top, bottom = turn_head(heads[head], cos, sin, back=True)
            back[at : at + HD // 2, :] = (top * factor).astype(BF16)
            back[at + HD // 2 : at + HD, :] = (bottom * factor).astype(BF16)
    back[VALUE_AT:, :] = grad_values[...].astype(BF16).reshape(KV * HD, back.shape[1])
    low = back[...]
    grad = jnp.concatenate([tn(low, weight[0]), tn(low, weight[1])], axis=1)
    inputs, inv = state[...], scale[...]
    gain_part = jnp.sum(grad * inputs * inv, axis=0, keepdims=True)
    upstream = grad * gain[...]
    inner = jnp.sum(upstream * inputs, axis=-1, keepdims=True) * (1.0 / model)
    return gain_part, grad_state[...] + inv * upstream - inputs * (inv * inv * inv) * inner


def qkv_back_kernel(
    model, grad_queries, grad_keys, grad_values, state, scale, grad_state, gain, weight, cosine, sine,
    grad_input, gain_term, back,
):
    gain_part, grad = qkv_back_rows(
        model, grad_queries, grad_keys, grad_values, state, scale, grad_state, gain, weight, cosine,
        sine, back,
    )
    grad_input[...] = grad

    @pl.when(pl.program_id(0) == 0)
    def _():
        gain_term[...] = jnp.zeros(gain_term.shape, F32)

    gain_term[...] += gain_part


def qkv_back_call(
    model, grad_queries, grad_keys, grad_values, state, scale, grad_state, gain, weight, cosine,
    sine, rows=256,
):
    tokens = state.shape[0]
    by_row = lambda width: pl.BlockSpec((rows, width), lambda i: (i, 0))
    heads = lambda count: pl.BlockSpec((count, HD, rows), lambda i: (0, 0, i))
    by_lane = lambda count: pl.BlockSpec((count, rows), lambda i: (0, i))
    return pl.pallas_call(
        functools.partial(qkv_back_kernel, model),
        grid=(tokens // rows,),
        in_specs=[
            heads(H), heads(KV), heads(KV), by_row(WIDE), by_row(1), by_row(WIDE), whole(1, WIDE),
            whole(2, QKV, HALF), by_lane(HD // 2), by_lane(HD // 2),
        ],
        out_specs=[by_row(WIDE), whole(1, WIDE), by_lane(QKV)],
        out_shape=[
            jax.ShapeDtypeStruct((tokens, WIDE), F32),
            jax.ShapeDtypeStruct((1, WIDE), F32),
            jax.ShapeDtypeStruct((QKV, tokens), BF16),
        ],
        compiler_params=compiler(),
        cost_estimate=cost(2 * tokens * WIDE * QKV, 30e6),
        name="qkv_back",
    )(
        grad_queries, grad_keys, grad_values, state, scale, grad_state, gain, weight, cosine, sine
    )


def spread_rows(model, sizes, rows, by_device, z):
    gap = HALF - model // 2 if z >= 2 else 0
    firsts = (0, KEY_AT, VALUE_AT, QKV + gap)
    for target, source, count in row_pairs(sizes):
        weight = [i for i in range(4) if source >= 4 * sum(sizes[:i])][-1]
        at = firsts[weight] + 4 * z * sizes[weight] + source - 4 * sum(sizes[:weight])
        by_device[target : target + count, :] = rows[at : at + count, :]
    return by_device[...]


def term_rows_of(model, back, normed, low, mixed, rows):
    rows[:QKV, :] = nn(back, normed)
    size = model // 2
    product = nn(mixed, low)
    blank = jnp.zeros((HALF - size, HALF), F32)
    for pair in range(2):
        part = product[:, pair * HALF : (pair + 1) * HALF]
        turned = jnp.concatenate([part, blank], axis=0).T
        rows[QKV + pair * HALF : QKV + (pair + 1) * HALF, :] = turned


def attn_terms_kernel(model, sizes, back, normed, low, mixed, term, rows, by_device):
    z = pl.program_id(1)

    @pl.when(z == 0)
    def _():
        term_rows_of(model, back[...], normed[...], low[...], mixed[...], rows)

    for at in range(4):

        @pl.when(z == at)
        def _(at=at):
            value = spread_rows(model, sizes, rows, by_device, at)
            term[0, 0] = value.astype(BF16).reshape(2, 2, PIECE, HALF)


def attn_terms_call(model, sizes, back, normed, low, mixed):
    tokens = normed.shape[0]
    size = model // 2
    return pl.pallas_call(
        functools.partial(attn_terms_kernel, model, sizes),
        grid=(2, 4),
        in_specs=[
            whole(QKV, tokens),
            pl.BlockSpec((tokens, HALF), lambda i, z: (0, i)),
            whole(tokens, WIDE),
            pl.BlockSpec((size, tokens), lambda i, z: (i, 0)),
        ],
        out_specs=pl.BlockSpec((1, 1, 2, 2, PIECE, HALF), lambda i, z: (i, z, 0, 0, 0, 0)),
        out_shape=jax.ShapeDtypeStruct((2, 4, 2, 2, PIECE, HALF), BF16),
        scratch_shapes=[pltpu.VMEM((QKV + WIDE, HALF), F32), pltpu.VMEM((4 * PIECE, HALF), F32)],
        compiler_params=compiler(),
        cost_estimate=cost(2 * tokens * WIDE * (QKV + WIDE), 30e6),
        name="attn_terms",
    )(back, normed, low, mixed)


MAIN_FLOWS = tuple(
    (((0, 48), first), ((48, 80), second), ((80, 96), third))
    for first, second, third in (("yxz", "xyz", "zxy"), ("xyz", "yxz", "zyx")) * 3
)[:CHUNKS]
LAST_ROWS = 80
LAST_FLOWS = ((((0, 32), "xyz"), ((32, 64), "yxz"), ((64, 80), "zxy")),) * 2

FEED_STAGES = {
    0: ((0, 0),),
    1: ((0, 1), (0, 2), (1, 0)),
    2: ((1, 1), (2, 0)),
    3: ((0, 3), (1, 2), (2, 1), (3, 0)),
    4: ((3, 1), (4, 0)),
}
ATTEND_STAGES = {
    0: ((4, 1), (0, 4), (1, 3), (2, 2)),
    2: ((0, 5), (1, 4), (2, 3), (3, 2)),
    4: ((1, 5), (2, 4), (3, 3), (4, 2)),
}
QKV_STAGES = {2: ((2, 5), (3, 4), (4, 3))}
TERM_STAGES = {2: ((3, 5), (4, 4)), 7: ((4, 5),)}


def finish_kernel(
    model, sizes, low_one, low_two, normed_one, normed_two, down_one, down_two, gate_one, gate_two,
    up_one, up_two, grad_state, grad_mixed, low_state, queries, keys, values, log_sum, state, scale, gain, qkv_weight,
    cosine, sine, normed, mixed, before,
    sums, mine, got, gain_term, term_out, back, grad_queries, grad_keys, grad_values,
    packed, term_rows, by_device, made, swap_sem, *scratch,
):
    me = Place()
    swap = remote(packed, got, swap_sem.at[0], swap_sem.at[1], me.partners("y")[0][1])
    scatter = Scatter(
        me, MAIN_FLOWS, [(made.at[i % 2], 0) for i in range(CHUNKS)], sums, scratch
    )
    tokens = grad_state.shape[0]
    rows = tokens // 4
    greet(me.everyone())

    def run_stages(points, step):
        for at, stages in points.items():

            def act(stages=stages):
                for t, stage in stages:
                    scatter.stage(t, stage)

            pl.when(step == at)(act)

    def feed_terms(lows, normeds, load_sem):
        loads = [
            pltpu.make_async_copy(source, target, load_sem.at[i])
            for i, (source, target) in enumerate(
                (
                    (low_one, lows.at[0]), (low_two, lows.at[1]),
                    (normed_one, normeds.at[0]), (normed_two, normeds.at[1]),
                )
            )
        ]
        for load in loads:
            load.start()
        for load in loads:
            load.wait()

        def term_body(by_gate, by_gate_two, by_up, by_up_two, by_hidden, by_hidden_two):
            slot = made.at[lax.rem(pl.program_id(0), 2)]
            for t, (one, two, right) in enumerate(
                (
                    (by_gate, by_gate_two, normeds),
                    (by_up, by_up_two, normeds),
                    (by_hidden, by_hidden_two, lows),
                )
            ):
                for half in range(2):
                    lanes = pl.ds(half * HALF, HALF)
                    value = tn(one[...], right[0, :, lanes]) + tn(two[...], right[1, :, lanes])
                    slot.at[half, :, :, :, pl.ds(t * ROWS, ROWS), :][...] = value.astype(
                        BF16
                    ).reshape(4, 2, 2, ROWS, HALF)
            run_stages(FEED_STAGES, pl.program_id(0))

        by_unit = pl.BlockSpec((tokens, UNITS), lambda i: (0, i))
        pltpu.emit_pipeline(term_body, grid=(CHUNKS,), in_specs=[by_unit] * 6, out_specs=[])(
            gate_one, gate_two, up_one, up_two, down_one, down_two
        )

    pl.run_scoped(
        feed_terms,
        pltpu.VMEM((2, tokens, WIDE), BF16),
        pltpu.VMEM((2, tokens, WIDE), BF16),
        pltpu.SemaphoreType.DMA((4,)),
    )

    def attend_body(query, key, value, logs, grad, by_query, by_key, by_value):
        attend_back_kernel(rows, query, key, value, logs, grad, by_query, by_key, by_value)
        run_stages(ATTEND_STAGES, pl.program_id(0))

    heads = lambda count: pl.BlockSpec((count, HD, tokens), lambda i: (i, 0, 0))
    pltpu.emit_pipeline(
        attend_body,
        grid=(KV,),
        in_specs=[
            heads(GROUP), heads(1), heads(1),
            pl.BlockSpec((GROUP, 1, tokens), lambda i: (i, 0, 0)), heads(GROUP),
        ],
        out_specs=[heads(GROUP), heads(1), heads(1)],
    )(queries, keys, values, log_sum, grad_mixed, grad_queries, grad_keys, grad_values)

    gain_term[...] = jnp.zeros(gain_term.shape, F32)

    size = model // 2

    def qkv_body(by_query, by_key, by_value, inputs, inv, grad, cos, sin, by_input, low):
        gain_part, value = qkv_back_rows(
            model, by_query, by_key, by_value, inputs, inv, grad, gain, qkv_weight, cos, sin, low
        )
        gain_term[...] += gain_part
        step = pl.program_id(0)
        for count in range(2):

            @pl.when(step == count)
            def _(count=count):
                for half in range(2):
                    packed[
                        half * size : (half + 1) * size, count * rows : (count + 1) * rows
                    ] = narrow(value, half, model).astype(BF16)

        @pl.when(step == 1)
        def _():
            swap.start()

        @pl.when(step >= 2)
        def _():
            for half in range(2):
                by_input[half * size : (half + 1) * size, :] = narrow(value, half, model)

        run_stages(QKV_STAGES, step)

    order = lambda i: lax.rem(i + 2 * (1 - me.y), 4)
    by_row = lambda width: pl.BlockSpec((rows, width), lambda i: (order(i), 0))
    some = lambda count: pl.BlockSpec((count, HD, rows), lambda i: (0, 0, order(i)))
    by_lane = lambda count: pl.BlockSpec((count, rows), lambda i: (0, order(i)))
    pltpu.emit_pipeline(
        qkv_body,
        grid=(4,),
        in_specs=[
            some(H), some(KV), some(KV), by_row(WIDE), by_row(1), by_row(WIDE),
            by_lane(HD // 2), by_lane(HD // 2),
        ],
        out_specs=[
            pl.BlockSpec((model, rows), lambda i: (0, jnp.maximum(i - 2, 0))), by_lane(QKV),
        ],
    )(grad_queries, grad_keys, grad_values, state, scale, grad_state, cosine, sine, mine, back)

    def term_body(low, by_normed, grad, by_mixed, earlier, term):
        z = pl.program_id(1)

        @pl.when(z == 0)
        def _():
            heads_half = by_mixed[...]
            term_rows_of(model, low[...], by_normed[...], grad[...], heads_half, term_rows)

        for at in range(4):

            @pl.when(z == at)
            def _(at=at):
                value = spread_rows(model, sizes, term_rows, by_device, at)
                value = value + earlier[0, 0].reshape(4 * PIECE, HALF).astype(F32)
                term[0, 0] = value.astype(BF16).reshape(2, 2, PIECE, HALF)

        run_stages(TERM_STAGES, 4 * pl.program_id(0) + z)

    fixed = lambda width: pl.BlockSpec((tokens, width), lambda i, z: (0, 0))
    by_half = pl.BlockSpec((tokens, HALF), lambda i, z: (0, i))
    piece = pl.BlockSpec((1, 1, 2, 2, PIECE, HALF), lambda i, z: (i, z, 0, 0, 0, 0))
    pltpu.emit_pipeline(
        term_body,
        grid=(2, 4),
        in_specs=[
            pl.BlockSpec((QKV, tokens), lambda i, z: (0, 0)), by_half, fixed(WIDE),
            pl.BlockSpec((size, tokens), lambda i, z: (i, 0)), piece,
        ],
        out_specs=[piece],
    )(back, normed, low_state, mixed, before, term_out)
    swap.wait()


def finish_call(
    model, sizes, operands, grad_state, grad_mixed, low_state, queries, keys, values, log_sum, state,
    scale, gain,
    qkv_weight, cosine, sine, normed, mixed, before,
):
    tokens = grad_state.shape[0]
    anywhere = pl.BlockSpec(memory_space=pl.ANY)
    inside = pl.BlockSpec(memory_space=pltpu.VMEM)
    outs = [
        ((CHUNKS, 3 * ROWS, HALF), F32, inside),
        ((model, tokens // 2), F32, anywhere),
        ((model, tokens // 2), BF16, anywhere),
        ((1, WIDE), F32, inside),
        ((2, 4, 2, 2, PIECE, HALF), BF16, anywhere),
        ((QKV, tokens), BF16, anywhere),
        ((H, HD, tokens), F32, anywhere),
        ((KV, HD, tokens), F32, anywhere),
        ((KV, HD, tokens), F32, anywhere),
    ]
    return pl.pallas_call(
        functools.partial(finish_kernel, model, sizes),
        out_shape=[jax.ShapeDtypeStruct(shape, kind) for shape, kind, _ in outs],
        in_specs=[anywhere] * 19 + [inside] * 2 + [anywhere] * 5,
        out_specs=[where for *_, where in outs],
        scratch_shapes=[
            pltpu.VMEM((model, tokens // 2), BF16),
            pltpu.VMEM((QKV + WIDE, HALF), F32),
            pltpu.VMEM((4 * PIECE, HALF), F32),
            pltpu.VMEM((2, 2, 4, 2, 2, 3 * ROWS, HALF), BF16),
            pltpu.SemaphoreType.DMA((2,)),
        ]
        + Scatter.scratch(MAIN_FLOWS, 3 * ROWS),
        compiler_params=compiler(collective_id=1, has_side_effects=True),
        name="finish",
    )(
        *operands, grad_state, grad_mixed, low_state, queries, keys, values, log_sum, state, scale, gain,
        qkv_weight, cosine, sine, normed, mixed, before,
    )[:5]


def last_kernel(term, gains, sums, gains_out, gain_own, gain_get, gain_send, gain_recv, *scratch):
    me = Place()
    y, z = me.y, me.z
    z_one = (me.w + 4 - 8 * (z % 2), y)
    z_two = (me.w + 8 - 16 * (z // 2), y)
    types = len(LAST_FLOWS)
    scatter = Scatter(me, LAST_FLOWS, [(term, t * LAST_ROWS) for t in range(types)], sums, scratch)
    ticks = staggered(types, STEPS + 3)
    gain_own[0] = gains[...]
    greet(me.everyone())

    def tick(count):
        for t, stage in ticks[count]:
            scatter.stage(t, stage)

    tick(0)
    partners = (me.sibling, me.partners("y")[0][1], me.partners("x")[0][1], z_one, z_two)

    def gain_copy(step):
        return remote(
            gain_own.at[step], gain_get.at[step], gain_send.at[step], gain_recv.at[step],
            partners[step],
        )

    gain_copy(0).start()
    for step in range(5):
        tick(1 + step)
        gain_copy(step).wait()
        if step < 4:
            gain_own[step + 1] = gain_own[step] + gain_get[step]
            gain_copy(step + 1).start()
        else:
            gains_out[...] = gain_own[step] + gain_get[step]
    for count in range(6, len(ticks)):
        tick(count)


def last_call(term, gains):
    dma = pltpu.SemaphoreType.DMA
    inside = pl.BlockSpec(memory_space=pltpu.VMEM)
    return pl.pallas_call(
        last_kernel,
        out_shape=[
            jax.ShapeDtypeStruct((len(LAST_FLOWS), LAST_ROWS, HALF), F32),
            jax.ShapeDtypeStruct(gains.shape, F32),
        ],
        in_specs=[pl.BlockSpec(memory_space=pl.ANY), inside],
        out_specs=[inside, inside],
        scratch_shapes=[
            pltpu.VMEM((5,) + gains.shape, F32),
            pltpu.VMEM((5,) + gains.shape, F32),
            dma((5,)),
            dma((5,)),
        ]
        + Scatter.scratch(LAST_FLOWS, LAST_ROWS),
        compiler_params=compiler(collective_id=2, has_side_effects=True),
        name="last",
    )(term, gains)


def halves(array, model):
    pad = [(0, 0)] * (array.ndim - 1)
    left, right = array[..., : model // 2], array[..., model // 2 :]
    pad = pad + [(0, HALF - model // 2)]
    return jnp.concatenate([jnp.pad(left, pad), jnp.pad(right, pad)], axis=-1)


def joined(array, model):
    return jnp.concatenate([array[..., : model // 2], array[..., HALF : HALF + model // 2]], axis=-1)


def rotary(count):
    positions = np.arange(count, dtype=np.float32)
    exponent = np.arange(HD // 2, dtype=np.float32) * np.float32(2.0 / HD)
    frequency = np.power(np.float32(10000.0), -exponent).astype(np.float32)
    angles = positions[:, None] * frequency[None, :]
    cosine, sine = np.cos(angles), np.sin(angles)
    return jnp.asarray(cosine.T, F32), jnp.asarray(sine.T, F32)


def on_device_whole(
    block_input, cotangent, attn_gain, ffn_gain,
    query_weight, key_weight, value_weight, out_weight, gate_weight, up_weight, down_weight,
):
    _, half_rows, model = block_input.shape
    tokens = 2 * half_rows
    y = lax.axis_index("narrow")
    flip = [(0, 1), (1, 0)]
    pieces = (query_weight, key_weight, value_weight, out_weight)
    sizes = tuple(piece.shape[1] for piece in pieces)
    starts = [sum(sizes[:i]) for i in range(5)]
    fill = lambda array: jnp.pad(
        array, [(0, 0)] * (array.ndim - 1) + [(0, HALF - array.shape[-1])]
    )
    own = fill(jnp.concatenate([piece.T for piece in pieces], axis=0))
    feed_own = fill(
        jnp.stack(
            [piece.T.reshape(CHUNKS, ROWS, -1) for piece in (gate_weight, up_weight, down_weight)],
            axis=1,
        ).reshape(CHUNKS, 3 * ROWS, -1)
    )
    both = fill(jnp.stack([attn_gain, ffn_gain]).reshape(2, 2, model // 2)).reshape(2, 1, WIDE)
    gain_a, gain_f = both[0], both[1]
    cosine, sine = rotary(tokens)
    (
        _, weights, output, gate, up, qkv_weight, full_out, state, normed_a, scale_a, queries, keys,
        values, log_sum, hidden_state, mixed, normed_f, scale_f,
    ) = start_call(
        model, sizes, own, feed_own, block_input.swapaxes(1, 2), gain_a, gain_f, cosine, sine
    )
    first_kept = (
        state, normed_a, scale_a, queries, keys, values, log_sum, hidden_state, mixed,
        normed_f, scale_f, gate, up,
    )

    def pick(array, index):
        return lax.dynamic_index_in_dim(array, index, 0, keepdims=False)

    state, cotangent = lax.optimization_barrier((output, cotangent))
    cotangent = cotangent.swapaxes(1, 2)
    grad_other = lax.ppermute(pick(cotangent, 1 - y), "narrow", flip)
    normed_a, scale_a, queries, keys, values = qkv_call(
        model, state, gain_a, qkv_weight, cosine, sine
    )
    mixed, log_sum = attend_call(queries, keys, values)
    final, hidden_state, normed_f, scale_f, gate, up = feed_call(
        model, state, mixed, full_out, gain_f, weights
    )
    final_got = lax.ppermute(pick(final, 1 - y), "narrow", flip)

    grad_state, gain_f_two, grad_low, low_state, grad_mixed, *units = feed_back_call(
        model, (cotangent, grad_other), hidden_state, gain_f, scale_f, full_out, gate, up, weights
    )
    feed_two = (grad_low, normed_f, units[2], units[0], units[1])
    grad_queries, grad_keys, grad_values = attend_back_call(
        queries, keys, values, log_sum, grad_mixed
    )
    grad, gain_a_two, back = qkv_back_call(
        model, grad_queries, grad_keys, grad_values, state, scale_a, grad_state, gain_a, qkv_weight,
        cosine, sine,
    )
    attn_term = attn_terms_call(
        model, sizes, back, normed_a, low_state, mixed.reshape(H * HD, tokens)
    )

    (
        state, normed_a, scale_a, queries, keys, values, log_sum, hidden_state, mixed,
        normed_f, scale_f, gate, up,
    ) = first_kept
    grad_state, gain_f_one, grad_low, low_state, grad_mixed, *units = feed_back_call(
        model, (grad,), hidden_state, gain_f, scale_f, full_out, gate, up, weights
    )
    feed_one = (grad_low, normed_f, units[2], units[0], units[1])
    operands = [array for pair in zip(feed_one, feed_two) for array in pair]
    feed_sums, grad_mine, grad_got, gain_a_one, attn_term = finish_call(
        model, sizes, operands, grad_state, grad_mixed, low_state, queries, keys, values, log_sum, state,
        scale_a,
        gain_a, qkv_weight, cosine, sine, normed_a, mixed.reshape(H * HD, tokens), attn_term,
    )
    gains = jnp.concatenate([gain_a_one + gain_a_two, gain_f_one + gain_f_two], axis=0)
    attn_sums, gains = last_call(attn_term, gains)

    def placed(mine, theirs):
        theirs = theirs.astype(mine.dtype)
        return jnp.where(y == 0, jnp.stack([mine, theirs]), jnp.stack([theirs, mine])).swapaxes(1, 2)

    block_output = placed(pick(final, y), final_got)
    input_grad = placed(grad_mine, grad_got)
    gains = joined(gains, model)
    feed_sums = feed_sums[:, :, : model // 2].reshape(CHUNKS, 3, ROWS, -1)
    feed_sums = [feed_sums[:, t].reshape(PIECE, -1).T for t in range(3)]
    attn_sums = attn_sums.reshape(PIECE, HALF)
    attn_sums = [attn_sums[starts[i] : starts[i + 1], : model // 2].T for i in range(4)]
    return (
        block_output, input_grad, gains[0], gains[1], *attn_sums,
        *feed_sums,
    )


def rms_scale(values):
    return lax.rsqrt(jnp.mean(values * values, axis=-1, keepdims=True) + 1e-05)


def rotary_tables(count, first_row):
    positions = (first_row + jnp.arange(count, dtype=jnp.int32)).astype(jnp.float32)
    exponent = jnp.arange(HD // 2, dtype=jnp.int32).astype(jnp.float32) * (2.0 / HD)
    frequency = 10000.0 ** (-exponent)
    angles = positions[:, None] * frequency[None, :]
    return (jnp.cos(angles), jnp.sin(angles))


def rotate(values, cosine, sine_table):
    half_size = values.shape[-1] // 2
    first_half = values[..., :half_size]
    second_half = values[..., half_size:]
    return jnp.concatenate(
        [
            first_half * cosine - second_half * sine_table,
            second_half * cosine + first_half * sine_table,
        ],
        axis=-1,
    )


def rotate_back(values, cosine, sine_table):
    half_size = values.shape[-1] // 2
    first_half = values[..., :half_size]
    second_half = values[..., half_size:]
    return jnp.concatenate(
        [
            first_half * cosine + second_half * sine_table,
            second_half * cosine - first_half * sine_table,
        ],
        axis=-1,
    )


def contract_last(left, right):
    return lax.dot_general(
        left, right, (((1,), (1,)), ((), ())), preferred_element_type=jnp.float32
    )


def norm_back(upstream, values, inv_rms, norm_gain):
    gain_grad = jnp.sum(upstream * values * inv_rms, axis=0)
    scaled_up = upstream * norm_gain
    inner_mean = jnp.mean(scaled_up * values, axis=-1, keepdims=True)
    return (gain_grad, inv_rms * scaled_up - values * (inv_rms * inv_rms * inv_rms) * inner_mean)


def fetch_weights(
    query_weight, key_weight, value_weight, out_weight, gate_weight, up_weight, down_weight
):
    columns = (
        lax.all_gather(query_weight, "wide", axis=1, tiled=True),
        lax.all_gather(key_weight, "wide", axis=1, tiled=True),
        lax.all_gather(value_weight, "wide", axis=1, tiled=True),
        lax.all_gather(out_weight, "wide", axis=1, tiled=True),
        lax.all_gather(gate_weight, "wide", axis=1, tiled=True),
        lax.all_gather(up_weight, "wide", axis=1, tiled=True),
        lax.all_gather(down_weight, "wide", axis=1, tiled=True),
    )
    return (
        lax.all_gather(columns[0], "narrow", axis=0, tiled=True),
        lax.all_gather(columns[1], "narrow", axis=0, tiled=True),
        lax.all_gather(columns[2], "narrow", axis=0, tiled=True),
        lax.all_gather(columns[3], "narrow", axis=0, tiled=True),
        lax.all_gather(columns[4], "narrow", axis=0, tiled=True),
        lax.all_gather(columns[5], "narrow", axis=0, tiled=True),
        lax.all_gather(columns[6], "narrow", axis=0, tiled=True),
    )


def forward_run(run_input, attn_gain, ffn_gain, weights, cosine, sine_table, first_row):
    query_weight, key_weight, value_weight, out_weight, gate_weight, up_weight, down_weight = (
        weights
    )
    row_count = run_input.shape[0]
    groups = H // KV
    attn_scale = rms_scale(run_input)
    normed_attn = (run_input * attn_scale * attn_gain).astype(jnp.bfloat16)
    query_pre = jnp.dot(normed_attn, query_weight, preferred_element_type=jnp.float32).reshape(
        row_count, KV, groups, HD
    )
    queries = rotate(query_pre, cosine[:, None, None, :], sine_table[:, None, None, :]).astype(
        jnp.bfloat16
    )
    key_pre = jnp.dot(normed_attn, key_weight, preferred_element_type=jnp.float32).reshape(
        row_count, KV, HD
    )
    keys_local = (
        rotate(key_pre, cosine[:, None, :], sine_table[:, None, :])
        .astype(jnp.bfloat16)
        .reshape(row_count, KV * HD)
    )
    values_local = jnp.dot(normed_attn, value_weight, preferred_element_type=jnp.float32).astype(
        jnp.bfloat16
    )
    keys_all, values_all = (
        lax.all_gather(keys_local, "narrow", axis=0, tiled=True),
        lax.all_gather(values_local, "narrow", axis=0, tiled=True),
    )
    length = keys_all.shape[0]
    keys_all = keys_all.reshape(length, KV, HD)
    values_all = values_all.reshape(length, KV, HD)
    attn_score = jnp.einsum(
        "rgjd,pgd->gjrp", queries, keys_all, preferred_element_type=jnp.float32
    ) * HD ** (-0.5)
    visible = (first_row + jnp.arange(row_count, dtype=jnp.int32))[:, None] >= jnp.arange(
        length, dtype=jnp.int32
    )[None, :]
    attn_score = jnp.where(visible, attn_score, -jnp.inf)
    row_peak = jnp.max(attn_score, axis=-1, keepdims=True)
    weight_exp = jnp.exp(attn_score - row_peak)
    attn_probs = weight_exp / jnp.sum(weight_exp, axis=-1, keepdims=True)
    probs_low = attn_probs.astype(jnp.bfloat16)
    mixed_heads = jnp.einsum(
        "gjrp,pgd->rgjd", probs_low, values_all, preferred_element_type=jnp.float32
    ).reshape(row_count, H * HD)
    mixed_low = mixed_heads.astype(jnp.bfloat16)
    hidden_state = run_input + jnp.dot(mixed_low, out_weight, preferred_element_type=jnp.float32)
    ffn_scale = rms_scale(hidden_state)
    normed_ffn = (hidden_state * ffn_scale * ffn_gain).astype(jnp.bfloat16)
    gate_proj = jnp.dot(normed_ffn, gate_weight, preferred_element_type=jnp.float32)
    up_proj = jnp.dot(normed_ffn, up_weight, preferred_element_type=jnp.float32)
    hidden = (gate_proj / (1.0 + jnp.exp(-gate_proj)) * up_proj).astype(jnp.bfloat16)
    run_output = hidden_state + contract_last(hidden, down_weight)
    saved_parts = (
        attn_scale,
        normed_attn,
        queries,
        keys_all,
        values_all,
        attn_probs,
        probs_low,
        mixed_low,
        hidden_state,
        ffn_scale,
        normed_ffn,
        gate_proj,
        up_proj,
        hidden,
    )
    return (run_output, saved_parts)


def backward_run(
    grad_out, run_input, saved_parts, attn_gain, ffn_gain, weights, cosine, sine_table
):
    query_weight, key_weight, value_weight, out_weight, gate_weight, up_weight, down_weight = (
        weights
    )
    (
        attn_scale,
        normed_attn,
        queries,
        keys_all,
        values_all,
        attn_probs,
        probs_low,
        mixed_low,
        hidden_state,
        ffn_scale,
        normed_ffn,
        gate_proj,
        up_proj,
        hidden,
    ) = saved_parts
    row_count = run_input.shape[0]
    length = keys_all.shape[0]
    groups = H // KV
    grad_low = grad_out.astype(jnp.bfloat16)
    down_term = jnp.einsum("td,tf->df", grad_low, hidden, preferred_element_type=jnp.float32)
    grad_hidden = jnp.dot(grad_low, down_weight, preferred_element_type=jnp.float32)
    sigmoid_gate = 1.0 / (1.0 + jnp.exp(-gate_proj))
    grad_gate = (
        grad_hidden * up_proj * sigmoid_gate * (1.0 + gate_proj * (1.0 - sigmoid_gate))
    ).astype(jnp.bfloat16)
    grad_up = (grad_hidden * gate_proj * sigmoid_gate).astype(jnp.bfloat16)
    gate_term = jnp.einsum("td,tf->df", normed_ffn, grad_gate, preferred_element_type=jnp.float32)
    up_term = jnp.einsum("td,tf->df", normed_ffn, grad_up, preferred_element_type=jnp.float32)
    grad_normed_ffn = contract_last(grad_gate, gate_weight) + contract_last(grad_up, up_weight)
    ffn_gain_term, grad_through = norm_back(grad_normed_ffn, hidden_state, ffn_scale, ffn_gain)
    grad_state = grad_out + grad_through
    branch_low = grad_state.astype(jnp.bfloat16)
    out_term = jnp.einsum("tc,td->cd", mixed_low, branch_low, preferred_element_type=jnp.float32)
    grad_mixed = (
        contract_last(branch_low, out_weight)
        .astype(jnp.bfloat16)
        .reshape(row_count, KV, groups, HD)
    )
    grad_probs = jnp.einsum(
        "rgjd,pgd->gjrp", grad_mixed, values_all, preferred_element_type=jnp.float32
    )
    row_delta = jnp.sum(attn_probs * grad_probs, axis=-1, keepdims=True)
    grad_score = (attn_probs * (grad_probs - row_delta)).astype(jnp.bfloat16)
    grad_queries = jnp.einsum(
        "gjrp,pgd->rgjd", grad_score, keys_all, preferred_element_type=jnp.float32
    ) * HD ** (-0.5)
    grad_keys = jnp.einsum(
        "gjrp,rgjd->pgd", grad_score, queries, preferred_element_type=jnp.float32
    ) * HD ** (-0.5)
    grad_values = jnp.einsum(
        "gjrp,rgjd->pgd", probs_low, grad_mixed, preferred_element_type=jnp.float32
    )
    key_grads, value_grads = (
        lax.psum_scatter(
            grad_keys.reshape(length, KV * HD).astype(jnp.bfloat16),
            "narrow",
            scatter_dimension=0,
            tiled=True,
        ).astype(jnp.float32),
        lax.psum_scatter(
            grad_values.reshape(length, KV * HD).astype(jnp.bfloat16),
            "narrow",
            scatter_dimension=0,
            tiled=True,
        ).astype(jnp.float32),
    )
    query_back = (
        rotate_back(grad_queries, cosine[:, None, None, :], sine_table[:, None, None, :])
        .reshape(row_count, H * HD)
        .astype(jnp.bfloat16)
    )
    key_back = (
        rotate_back(
            key_grads.reshape(row_count, KV, HD), cosine[:, None, :], sine_table[:, None, :]
        )
        .reshape(row_count, KV * HD)
        .astype(jnp.bfloat16)
    )
    value_back = value_grads.astype(jnp.bfloat16)
    query_term = jnp.einsum(
        "td,tc->dc", normed_attn, query_back, preferred_element_type=jnp.float32
    )
    key_term = jnp.einsum("td,tc->dc", normed_attn, key_back, preferred_element_type=jnp.float32)
    value_term = jnp.einsum(
        "td,tc->dc", normed_attn, value_back, preferred_element_type=jnp.float32
    )
    grad_normed_attn = (
        contract_last(query_back, query_weight)
        + contract_last(key_back, key_weight)
        + contract_last(value_back, value_weight)
    )
    attn_gain_term, grad_norm_input = norm_back(grad_normed_attn, run_input, attn_scale, attn_gain)
    grad_input = grad_state + grad_norm_input
    return (
        grad_input,
        (attn_gain_term, ffn_gain_term),
        (query_term, key_term, value_term, out_term, gate_term, up_term, down_term),
    )


def on_device_parts(
    block_input,
    cotangent,
    attn_gain,
    ffn_gain,
    query_weight,
    key_weight,
    value_weight,
    out_weight,
    gate_weight,
    up_weight,
    down_weight,
):
    seq_count = block_input.shape[0]
    row_count = block_input.shape[1]
    first_row = lax.axis_index("narrow") * row_count
    cosine, sine_table = rotary_tables(row_count, first_row)

    def current():
        return fetch_weights(
            query_weight, key_weight, value_weight, out_weight, gate_weight, up_weight, down_weight
        )

    start_states = [block_input[item].astype(jnp.float32) for item in range(seq_count)]
    weights_now = current()
    middle_states = [
        forward_run(state, attn_gain, ffn_gain, weights_now, cosine, sine_table, first_row)[0]
        for state in start_states
    ]
    weights_now = current()
    final_states = [
        forward_run(state, attn_gain, ffn_gain, weights_now, cosine, sine_table, first_row)[0]
        for state in middle_states
    ]
    grad_states = [cotangent[item].astype(jnp.float32) for item in range(seq_count)]
    gain_local = None
    weight_local = None
    for run_inputs in (middle_states, start_states):
        weights_now = current()
        next_grads = []
        for item in range(seq_count):
            recomputed, saved_parts = forward_run(
                run_inputs[item], attn_gain, ffn_gain, weights_now, cosine, sine_table, first_row
            )
            grad_input, gain_parts, weight_parts = backward_run(
                grad_states[item],
                run_inputs[item],
                saved_parts,
                attn_gain,
                ffn_gain,
                weights_now,
                cosine,
                sine_table,
            )
            next_grads.append(grad_input)
            if gain_local is None:
                gain_local = gain_parts
                weight_local = weight_parts
            else:
                gain_local = jax.tree.map(jnp.add, gain_local, gain_parts)
                weight_local = jax.tree.map(jnp.add, weight_local, weight_parts)
        grad_states = next_grads
    across = (
        lax.psum_scatter(
            weight_local[0].astype(jnp.bfloat16), "wide", scatter_dimension=1, tiled=True
        ).astype(jnp.float32),
        lax.psum_scatter(
            weight_local[1].astype(jnp.bfloat16), "wide", scatter_dimension=1, tiled=True
        ).astype(jnp.float32),
        lax.psum_scatter(
            weight_local[2].astype(jnp.bfloat16), "wide", scatter_dimension=1, tiled=True
        ).astype(jnp.float32),
        lax.psum_scatter(
            weight_local[3].astype(jnp.bfloat16), "wide", scatter_dimension=1, tiled=True
        ).astype(jnp.float32),
        lax.psum_scatter(
            weight_local[4].astype(jnp.bfloat16), "wide", scatter_dimension=1, tiled=True
        ).astype(jnp.float32),
        lax.psum_scatter(
            weight_local[5].astype(jnp.bfloat16), "wide", scatter_dimension=1, tiled=True
        ).astype(jnp.float32),
        lax.psum_scatter(
            weight_local[6].astype(jnp.bfloat16), "wide", scatter_dimension=1, tiled=True
        ).astype(jnp.float32),
    )
    reduced = (
        lax.psum_scatter(
            across[0].astype(jnp.bfloat16), "narrow", scatter_dimension=0, tiled=True
        ).astype(jnp.float32),
        lax.psum_scatter(
            across[1].astype(jnp.bfloat16), "narrow", scatter_dimension=0, tiled=True
        ).astype(jnp.float32),
        lax.psum_scatter(
            across[2].astype(jnp.bfloat16), "narrow", scatter_dimension=0, tiled=True
        ).astype(jnp.float32),
        lax.psum_scatter(
            across[3].astype(jnp.bfloat16), "narrow", scatter_dimension=0, tiled=True
        ).astype(jnp.float32),
        lax.psum_scatter(
            across[4].astype(jnp.bfloat16), "narrow", scatter_dimension=0, tiled=True
        ).astype(jnp.float32),
        lax.psum_scatter(
            across[5].astype(jnp.bfloat16), "narrow", scatter_dimension=0, tiled=True
        ).astype(jnp.float32),
        lax.psum_scatter(
            across[6].astype(jnp.bfloat16), "narrow", scatter_dimension=0, tiled=True
        ).astype(jnp.float32),
    )
    gain_totals = lax.psum((gain_local[0], gain_local[1]), ("wide", "narrow"))
    block_output = jnp.stack(final_states).astype(jnp.bfloat16)
    input_grad = jnp.stack(grad_states)
    return (
        block_output,
        input_grad,
        gain_totals[0],
        gain_totals[1],
        reduced[0],
        reduced[1],
        reduced[2],
        reduced[3],
        reduced[4],
        reduced[5],
        reduced[6],
    )


def on_device(block_input, *rest):
    pieces = sum(weight.shape[1] for weight in rest[3:7])
    fits = (
        (lax.axis_size("wide"), lax.axis_size("narrow")) == (16, 2)
        and block_input.shape[0] == 2
        and block_input.shape[2] <= WIDE
        and {pieces, rest[7].shape[1], rest[8].shape[1], rest[9].shape[1]} == {PIECE}
    )
    plan = on_device_whole if fits else on_device_parts
    return plan(block_input, *rest)


def solution(mesh):
    placed = (
        P("wide", "narrow", None),
        P("wide", "narrow", None),
        P(),
        P(),
        P("narrow", "wide"),
        P("narrow", "wide"),
        P("narrow", "wide"),
        P("narrow", "wide"),
        P("narrow", "wide"),
        P("narrow", "wide"),
        P("narrow", "wide"),
    )
    return jax.shard_map(
        on_device,
        mesh=mesh,
        in_specs=placed,
        out_specs=(
            P("wide", "narrow", None),
            P("wide", "narrow", None),
            P(),
            P(),
            P("narrow", "wide"),
            P("narrow", "wide"),
            P("narrow", "wide"),
            P("narrow", "wide"),
            P("narrow", "wide"),
            P("narrow", "wide"),
            P("narrow", "wide"),
        ),
        check_vma=False,
    )
```
